32 devices in a mesh: lat: 16 (over z, x, core), chan: 2 (over y).
Axes of the slice: x: 2, y: 2, z: 4, core: 2. Of those that a mesh axis runs over, the one named last changes fastest.
Arguments:
- grid: bfloat16 [384, 720, 512], P('lat', None, 'chan'), may hold values from -6 to 6
- basis: float32 [384, 384, 384], P('lat'), may hold values from -16 to 16, as said below
- mix_weight: bfloat16 [2, 512, 512], P(None, None, 'chan'), may hold values from -0.1875 to 0.1875
- spectral_gain: float32 [384], replicated, may hold values from 0.5 to 4
- conv_weight: float32 [9, 512], P(None, 'chan'), may hold values from -2 to 2
- lat_offsets: int32 [9], replicated, may hold values from -1 to 1
- lon_offsets: int32 [9], replicated, may hold values from -3 to 3
- ln_gain: float32 [512], replicated, may hold values from 0.1 to 1.9
- up_weight: bfloat16 [512, 512], replicated, may hold values from -0.25 to 0.25
- down_weight: bfloat16 [512, 512], replicated, may hold values from -0.25 to 0.25
Outputs:
- result: bfloat16 [384, 720, 512], P('lat', None, 'chan')
The draws below stay inside these ranges and needn't reach their ends.
Inputs may be any that keep to these rules, and one draw needn't show every extreme that they name: basis[m, l, t] is the orthonormal associated Legendre function of degree l and order m at cos(theta_t) times a factor between 0.8 and 1.25; it is zero for l < m.
All inputs are finite; a program needn't handle non-finite values.
Results may differ from the reference program's by a relative error of at most 0.01.
Values may be sent and summed in bfloat16 or wider, within the bound.
No kernel may reach another device: no remote copies, remote signals or barrier semaphores. Data moves between devices by JAX's collectives and lax.ppermute only.
A program may use at most 192 MiB of HBM per device.

```python
import math
import jax
import jax.numpy as jnp
from jax import lax

NLAT = 384
NLON = 720
C = 512
HID = 512
MMAX = 384
L = 384
NB = 9


def legendre_table(nlat, orders_count, degrees):
    orders = jnp.arange(orders_count, dtype=jnp.int32)
    theta = math.pi * (jnp.arange(nlat, dtype=jnp.int32).astype(jnp.float32) + 0.5) / nlat
    cosine = jnp.cos(theta)[None, :]
    sine = jnp.sin(theta)[None, :]
    order = orders.astype(jnp.float32)[:, None]
    logdiag = 0.5 * (jnp.log(2.0 * order + 1.0) - math.log(2.0) + lax.lgamma(order + 0.5) - 0.5 * math.log(math.pi) - lax.lgamma(order + 1.0))
    diagonal = jnp.exp(logdiag + order * jnp.log(sine))
    start = jnp.zeros((orders_count, nlat), jnp.float32)

    def advance(carry, degree):
        prev_one, prev_two = carry
        level = degree.astype(jnp.float32)
        factor = jnp.sqrt(jnp.maximum(4.0 * level * level - 1.0, 1.0) / jnp.maximum(level * level - order * order, 1.0))
        below = level - 1.0
        inverse_prev = jnp.sqrt(jnp.maximum(below * below - order * order, 1.0) / jnp.maximum(4.0 * below * below - 1.0, 1.0))
        recursed = factor * (cosine * prev_one - prev_two * inverse_prev)
        fresh = jnp.where(level < order, 0.0, jnp.where(level == order, diagonal, recursed))
        return ((fresh, prev_one), fresh)
    _, table = lax.scan(advance, (start, start), jnp.arange(degrees, dtype=jnp.int32))
    return jnp.transpose(table, (1, 0, 2))


def draw_basis(key, part):
    table = legendre_table(NLAT, MMAX, L)
    factor = jax.random.uniform(jax.random.fold_in(key, 17), (MMAX, L, NLAT), jnp.float32, 0.8, 1.25)
    return (table * factor).astype(jnp.float32)


def set_ends(drawn, stream_key, low, high):
    index_at = [jax.random.randint(jax.random.fold_in(stream_key, axis), (), 0, length) for axis, length in enumerate(drawn.shape)]
    longest = drawn.shape.index(max(drawn.shape))
    beside = index_at[:longest] + [(index_at[longest] + 1) % drawn.shape[longest]] + index_at[longest + 1:]
    return drawn.at[tuple(index_at)].set(low).at[tuple(beside)].set(high)


def block_scale(stream_key, dims, shards, low, top_value):
    gain = 1.0
    for axis_at, blocks in shards:
        heights = jax.random.uniform(jax.random.fold_in(jax.random.fold_in(stream_key, 6), axis_at), (blocks,), jnp.float32, low / len(shards), top_value / len(shards))
        gain = gain * jnp.repeat(jnp.exp(heights), dims[axis_at] // blocks).reshape((-1,) + (1,) * (len(dims) - 1 - axis_at))
    return gain


def noise(own_key, extent, width, most, shards=(), kind=jnp.bfloat16):
    values = jax.random.normal(own_key, extent, jnp.float32) * width
    if len(shards) > 0:
        values = block_scale(own_key, extent, shards, -0.22, 0.18) * values
    return jnp.clip(values, min=-most, max=most).astype(kind)


def setup_inputs(seed: int = 0) -> dict:
    key_of = jax.random.split(jax.random.key(seed), 11)
    return {
        "grid": noise(key_of[0], (NLAT, NLON, C), 1.0, 6.0, ((0, 16), (2, 2))),
        "basis": draw_basis(jax.random.fold_in(key_of[10], 71), 0),
        "mix_weight": noise(key_of[2], (2, C, C), (2 * C) ** -0.5, 0.1875, ((2, 2),)),
        "spectral_gain": jnp.clip(jnp.exp(jax.random.uniform(key_of[3], (L,), jnp.float32, math.log(0.5), math.log(4.0))), 0.5, 4.0),
        "conv_weight": noise(key_of[4], (NB, C), NB ** -0.5, 2.0, ((1, 2),), jnp.float32),
        "lat_offsets": set_ends(jax.random.randint(key_of[5], (NB,), -1, 2), jax.random.fold_in(key_of[5], 1), -1, 1).astype(jnp.int32),
        "lon_offsets": set_ends(jax.random.randint(key_of[6], (NB,), -3, 4), jax.random.fold_in(key_of[6], 1), -3, 3).astype(jnp.int32),
        "ln_gain": jnp.clip(1.0 + 0.18 * jax.random.normal(key_of[7], (C,), jnp.float32), 0.1, 1.9),
        "up_weight": noise(key_of[8], (C, HID), C ** -0.5, 0.25),
        "down_weight": noise(key_of[9], (HID, C), HID ** -0.5, 0.25),
    }


def cycle_angle(rows, nlat):
    return math.pi * (rows.astype(jnp.float32) + 0.5) / nlat

def mlp_rows(summed, ln_gain, up_weight, down_weight):
    rows = summed.astype(jnp.float32)
    center = lax.optimization_barrier(jnp.mean(rows, axis=-1, keepdims=True))
    spread = lax.optimization_barrier(jnp.mean((rows - center) ** 2, axis=-1, keepdims=True))
    normed = ((rows - center) / jnp.sqrt(spread + 1e-05) * ln_gain).astype(jnp.bfloat16)
    hidden = jax.nn.gelu(jnp.dot(normed, up_weight, preferred_element_type=jnp.float32), approximate=True).astype(jnp.bfloat16)
    return (jnp.dot(hidden, down_weight, preferred_element_type=jnp.float32) + rows).astype(jnp.bfloat16)

def reference(grid, basis, mix_weight, spectral_gain, conv_weight, lat_offsets, lon_offsets, ln_gain, up_weight, down_weight):
    points = jnp.arange(NLON, dtype=jnp.int32)
    orders = jnp.arange(MMAX, dtype=jnp.int32)
    phase = points[:, None] * orders[None, :] % NLON
    angle = 2.0 * math.pi * phase.astype(jnp.float32) / NLON
    fwd_table = jnp.concatenate([jnp.cos(angle), -jnp.sin(angle)], axis=1).astype(jnp.bfloat16)
    weight_m = jnp.where(orders == 0, 1.0, 2.0).astype(jnp.float32)[None, :]
    inv_table = jnp.concatenate([weight_m * jnp.cos(angle), -weight_m * jnp.sin(angle)], axis=1).astype(jnp.bfloat16)

    def forward_row(row):
        return (jnp.dot(fwd_table.T, row, preferred_element_type=jnp.float32) * (1.0 / NLON)).astype(jnp.bfloat16)
    spec = lax.map(forward_row, grid)
    spec = jnp.transpose(spec.reshape(NLAT, 2, MMAX, C), (2, 0, 1, 3)).reshape(MMAX, NLAT, 2 * C)
    theta = cycle_angle(jnp.arange(NLAT, dtype=jnp.int32), NLAT)
    quad = math.pi / NLAT * jnp.sin(theta)
    fwd_leg = (basis * quad[None, None, :]).astype(jnp.bfloat16)
    inv_leg = basis.astype(jnp.bfloat16)

    def forward_mode(pair):
        return jnp.dot(pair[0], pair[1], preferred_element_type=jnp.float32).astype(jnp.bfloat16)
    coeff = lax.map(forward_mode, (fwd_leg, spec))
    real_part = mix_weight[0]
    imag_part = mix_weight[1]
    block = jnp.concatenate([jnp.concatenate([real_part, imag_part], axis=1), jnp.concatenate([-imag_part, real_part], axis=1)], axis=0)
    mixed = jnp.dot(coeff.reshape(MMAX * L, 2 * C), block, preferred_element_type=jnp.float32).reshape(MMAX, L, 2 * C)
    mixed = (mixed * spectral_gain[None, :, None]).astype(jnp.bfloat16)

    def inverse_mode(pair):
        return jnp.dot(pair[0].T, pair[1], preferred_element_type=jnp.float32).astype(jnp.bfloat16)
    back = lax.map(inverse_mode, (inv_leg, mixed))
    back = jnp.transpose(back.reshape(MMAX, NLAT, 2, C), (1, 2, 0, 3)).reshape(NLAT, 2 * MMAX, C)
    padded = jnp.pad(grid, ((1, 1), (0, 0), (0, 0)))

    def output_row(inputs):
        cycle, back_row, grid_row = inputs
        spectral = jnp.dot(inv_table, back_row, preferred_element_type=jnp.float32)
        local = jnp.zeros((NLON, C), jnp.float32)
        here = jnp.sin(cycle_angle(cycle, NLAT))
        for tap in range(NB):
            shift = lat_offsets[tap]
            source = lax.dynamic_slice_in_dim(padded, (cycle + 1 + shift).astype(jnp.int32), 1, 0)[0]
            source = jnp.roll(source, -lon_offsets[tap], axis=0)
            ratio = jnp.sin(cycle_angle(cycle + shift, NLAT)) / here
            local = local + conv_weight[tap][None, :] * ratio * source.astype(jnp.float32)
        summed = (spectral + local + grid_row.astype(jnp.float32)).astype(jnp.bfloat16)
        return mlp_rows(summed, ln_gain, up_weight, down_weight)
    return lax.map(output_row, (jnp.arange(NLAT, dtype=jnp.int32), back, grid))
```

```python
import functools
import math

import jax
import jax.numpy as jnp
import numpy as np
from jax import lax
from jax.experimental import pallas as pl
from jax.experimental.pallas import tpu as pltpu
from jax.sharding import PartitionSpec as P

MMAX = 384
L = 384
STEP = 4
LANES = 128
NEAR = 1
REACH = 3
BF = jnp.bfloat16
F32 = jnp.float32
SWAP = [(0, 1), (1, 0)]


def cycle_angle(rows, nlat):
    return math.pi * (rows.astype(F32) + 0.5) / nlat


def params(mib):
    return pltpu.CompilerParams(vmem_limit_bytes=mib * 1024 * 1024)


def cost(flops, nbytes):
    return pl.CostEstimate(flops=int(flops), bytes_accessed=int(nbytes), transcendentals=0)


def angle_table(nlon):
    phase = np.arange(nlon)[:, None] * np.arange(MMAX)[None, :] % nlon
    angle = (2.0 * math.pi * phase / nlon).astype(np.float32).astype(np.float64)
    return np.cos(angle), np.sin(angle)


def forward_kernel(scale, table_ref, grid_ref, out_ref, held):
    cycles = grid_ref.shape[0]
    rows = table_ref.shape[0]
    for t in range(cycles):
        value = jnp.dot(table_ref[...], grid_ref[t], preferred_element_type=F32)
        value = value * scale
        for at in range(held.shape[0]):
            held[at, pl.ds(t, rows, stride=cycles), :] = value[:, at * LANES : (at + 1) * LANES]
    for at in range(held.shape[0]):
        lanes = slice(at * LANES, (at + 1) * LANES)
        out_ref[:, :, lanes] = held[at].reshape(rows, cycles, LANES).astype(BF)


def forward_part(grid, table):
    cycles, nlon, width = grid.shape
    rows = table.shape[0]
    return pl.pallas_call(
        functools.partial(forward_kernel, 1.0 / nlon),
        out_shape=jax.ShapeDtypeStruct((rows, cycles, width), BF),
        in_specs=[pl.BlockSpec(memory_space=pltpu.VMEM)] * 2,
        out_specs=pl.BlockSpec(memory_space=pltpu.VMEM),
        scratch_shapes=[pltpu.VMEM((width // LANES, rows * cycles, LANES), F32)],
        compiler_params=params(40),
        cost_estimate=cost(2 * rows * nlon * cycles * width, grid.size * 2),
    )(table, grid)


def middle_kernel(counts, at_ref, spec_ref, basis_ref, quad_ref, mix_ref, gain_ref, *rest):
    outs, held = (rest[-len(counts) - 1 : -1], rest[-1])
    mode = pl.program_id(0)
    groups, sides, _, _, cycles, width = spec_ref.shape
    nlat = groups * cycles
    table = basis_ref[0]
    forward = (table * quad_ref[...]).astype(BF)
    pieces = []
    for side in range(sides):
        for part in range(2):
            piece = spec_ref[:, side, 0, part, :, :].astype(F32)
            pieces.append(piece.reshape(nlat, width).astype(BF))
    spec = jnp.concatenate(pieces, axis=1)
    coeff = jnp.dot(forward, spec, preferred_element_type=F32).astype(BF)
    mixed = jnp.dot(coeff, mix_ref[...], preferred_element_type=F32) * gain_ref[...]
    inverse = table.T.astype(BF)
    back = jnp.dot(inverse, mixed.astype(BF), preferred_element_type=F32)
    half = back.shape[1] // 2
    slots = 2 * STEP
    for part in range(2):
        for where in range(STEP):

            @pl.when(mode == where)
            def _():
                row = 2 * where + part
                for at in range(half // LANES):
                    low = part * half + at * LANES
                    held[at, pl.ds(row, nlat, stride=slots), :] = back[:, low : low + LANES]

    @pl.when(mode == STEP - 1)
    def _():
        for at in range(half // LANES):
            whole = held[at].reshape(groups * sides, nlat // (groups * sides), slots, LANES)
            start = 0
            for out, count in zip(outs, counts):
                part = whole[:, start : start + count].astype(BF)
                out[:, 0, :, :, at * LANES : (at + 1) * LANES] = part
                start += count


def middle_part(part, spec, basis, quad, mix, gain, offset, counts, filled):
    groups, sides, _, _, cycles, width = spec.shape
    nlat = groups * cycles
    modes = basis.shape[0]
    parts = modes // sides // STEP
    channels = sides * width
    slots = 2 * STEP
    everywhere = [
        jax.ShapeDtypeStruct((groups * sides, parts, count, slots, channels), BF)
        for count in counts
    ]
    fixed = lambda m, at: (0, 0)
    specs = [
        pl.BlockSpec((groups, sides, 1, 2, cycles, width), lambda m, at: (0, 0, m, 0, 0, 0)),
        pl.BlockSpec((1, L, nlat), lambda m, at: (at[0] + m, 0, 0)),
        pl.BlockSpec((1, nlat), fixed),
        pl.BlockSpec(mix.shape, fixed),
        pl.BlockSpec((L, 1), fixed),
    ]
    arguments = [spec, basis, quad, mix, gain]
    aliases = {}
    if filled is not None:
        for at, value in enumerate(filled):
            aliases[1 + len(arguments)] = at
            specs.append(pl.BlockSpec(memory_space=pl.ANY))
            arguments.append(value)
    return pl.pallas_call(
        functools.partial(middle_kernel, counts),
        out_shape=everywhere,
        grid_spec=pltpu.PrefetchScalarGridSpec(
            num_scalar_prefetch=1,
            grid=(STEP,),
            in_specs=specs,
            out_specs=[
                pl.BlockSpec(
                    (groups * sides, 1, count, slots, channels),
                    lambda m, at: (0, part, 0, 0, 0),
                )
                for count in counts
            ],
            scratch_shapes=[pltpu.VMEM((channels // LANES, nlat * slots, LANES), F32)],
        ),
        input_output_aliases=aliases,
        compiler_params=params(56),
        cost_estimate=cost(
            2 * STEP * (2 * L * nlat * 2 * channels + L * 4 * channels * channels),
            STEP * (L * nlat * 4 + nlat * channels * 8) + mix.size * 2,
        ),
    )(offset, *arguments)


def local_rows(ratio_ref, weight_ref, here_ref, after_ref, edge_ref, tail_ref, out_ref, held):
    t = pl.program_id(0)
    cycles = pl.num_programs(0)
    _, nlon, width = out_ref.shape
    near = weight_ref.shape[0] // 2
    reach = weight_ref.shape[1] // 2
    pad = 8
    block = max(size for size in range(8, 73, 8) if nlon % size == 0)
    wide = block + 2 * pad

    def fill(slot, row):
        held[slot, pl.ds(pad, nlon), :] = row
        held[slot, pl.ds(0, pad), :] = row[nlon - pad :]
        held[slot, pl.ds(pad + nlon, pad), :] = row[:pad]

    @pl.when(t == 0)
    def _():
        fill(2, edge_ref[0].astype(F32))
        fill(0, here_ref[0].astype(F32))

    after = lax.rem(t + 1, 3)

    @pl.when(t < cycles - 1)
    def _():
        fill(after, after_ref[0].astype(F32))

    @pl.when(t == cycles - 1)
    def _():
        fill(after, tail_ref[0].astype(F32))

    slots = [lax.rem(t + 2 + a, 3) for a in range(2 * near + 1)]
    for low in range(0, width, LANES):
        lanes = slice(low, low + LANES)
        weights = [
            [weight_ref[a, b : b + 1, lanes] * ratio_ref[t, a] for b in range(2 * reach + 1)]
            for a in range(2 * near + 1)
        ]

        def body(at, carry):
            start = pl.multiple_of(at * block, 8)
            rows = [held[slot, pl.ds(start, wide), lanes] for slot in slots]
            total = rows[near][pad : pad + block]
            for b in range(2 * reach + 1):
                value = rows[0] * weights[0][b]
                for a in range(1, 2 * near + 1):
                    value = value + rows[a] * weights[a][b]
                if b != reach:
                    value = pltpu.roll(value, (wide + reach - b) % wide, 0)
                total = total + value[pad : pad + block]
            out_ref[0, pl.ds(start, block), lanes] = total.astype(BF)
            return carry

        lax.fori_loop(0, nlon // block, body, 0)


def local_part(grid, before, after, ratio, weight):
    cycles, nlon, width = grid.shape
    row = (1, nlon, width)
    edge = lambda t, _: (0, 0, 0)
    return pl.pallas_call(
        local_rows,
        out_shape=jax.ShapeDtypeStruct(grid.shape, BF),
        grid_spec=pltpu.PrefetchScalarGridSpec(
            num_scalar_prefetch=1,
            grid=(cycles,),
            in_specs=[
                pl.BlockSpec(weight.shape, lambda t, _: (0, 0, 0)),
                pl.BlockSpec(row, lambda t, _: (t, 0, 0)),
                pl.BlockSpec(row, lambda t, _: (jnp.minimum(t + 1, cycles - 1), 0, 0)),
                pl.BlockSpec(row, edge),
                pl.BlockSpec(row, edge),
            ],
            out_specs=pl.BlockSpec(row, lambda t, _: (t, 0, 0)),
            scratch_shapes=[pltpu.VMEM((3, nlon + 16, width), F32)],
        ),
        compiler_params=params(32),
        cost_estimate=cost(grid.size * 400, grid.size * 6),
    )(ratio, weight, grid, grid, before, after)


def tail_kernel(place_ref, back_ref, own_ref, got_ref, table_ref, gain_ref, up_ref, down_ref, *rest):
    mine_ref, theirs_ref = rest[-2:]
    first = place_ref[1] == 0
    channels = up_ref.shape[0]
    width = own_ref.shape[2]
    back = back_ref[:, :, 0].astype(F32).reshape(table_ref.shape[1], channels).astype(BF)
    spectral = jnp.dot(table_ref[...], back, preferred_element_type=F32)
    own = own_ref[0].astype(F32)
    got = got_ref[0].astype(F32)
    low = jnp.where(first, own, got)
    high = jnp.where(first, got, own)
    local = jnp.concatenate([low, high], axis=1)
    rows = (spectral + local).astype(BF).astype(F32)
    center = jnp.mean(rows, axis=-1, keepdims=True)
    moved = rows - center
    spread = jnp.mean(moved * moved, axis=-1, keepdims=True)
    normed = (moved * lax.rsqrt(spread + 1e-05) * gain_ref[...]).astype(BF)
    hidden = jax.nn.gelu(jnp.dot(normed, up_ref[...], preferred_element_type=F32), approximate=True)
    output = jnp.dot(hidden.astype(BF), down_ref[...], preferred_element_type=F32) + rows
    low = output[:, :width]
    high = output[:, width:]
    mine_ref[0] = jnp.where(first, low, high).astype(BF)
    theirs_ref[0] = jnp.where(first, high, low).astype(BF)


def tail_part(back, own, got, start, table, ln_gain, up_weight, down_weight, place, result, cycles):
    devices, parts, count, slots, channels = back.shape
    _, nlon, width = own.shape
    fixed = lambda t, at: (0, 0)
    row = (1, nlon, width)
    specs = [
        pl.BlockSpec((devices, parts, 1, slots, channels), lambda t, at: (0, 0, t, 0, 0)),
        pl.BlockSpec(row, lambda t, at: (start + t, 0, 0)),
        pl.BlockSpec(row, lambda t, at: (start + t, 0, 0)),
        pl.BlockSpec(table.shape, fixed),
        pl.BlockSpec(ln_gain.shape, fixed),
        pl.BlockSpec(up_weight.shape, fixed),
        pl.BlockSpec(down_weight.shape, fixed),
    ]
    arguments = [back, own, got, table, ln_gain, up_weight, down_weight]
    aliases = {}
    if result is not None:
        aliases[1 + len(arguments)] = 0
        specs.append(pl.BlockSpec(memory_space=pl.ANY))
        arguments.append(result)
    return pl.pallas_call(
        tail_kernel,
        out_shape=[
            jax.ShapeDtypeStruct((cycles, nlon, width), BF),
            jax.ShapeDtypeStruct((count, nlon, width), BF),
        ],
        grid_spec=pltpu.PrefetchScalarGridSpec(
            num_scalar_prefetch=1,
            grid=(count,),
            in_specs=specs,
            out_specs=[
                pl.BlockSpec(row, lambda t, at: (at[0] + start + t, 0, 0)),
                pl.BlockSpec(row, lambda t, at: (t, 0, 0)),
            ],
        ),
        input_output_aliases=aliases,
        compiler_params=params(56),
        cost_estimate=cost(
            2 * count * nlon * channels * (table.shape[1] + 2 * channels),
            count * nlon * channels * 8,
        ),
    )(place, *arguments)


def fast(grid, basis, mix_weight, spectral_gain, conv_weight, lat_offsets, lon_offsets, ln_gain, up_weight, down_weight):
    cycles, nlon, width = grid.shape
    groups = lax.axis_size("lat")
    sides = lax.axis_size("chan")
    rank = lax.axis_index("lat")
    side = lax.axis_index("chan")
    nlat = cycles * groups
    modes = basis.shape[0]
    few = modes // sides
    parts = few // STEP
    span = cycles // sides
    counts = [span // 3] * 3 if span % 3 == 0 else [span]

    cosine, sine = angle_table(nlon)
    both = np.stack([cosine, -sine], axis=-1)
    fwd_table = np.ascontiguousarray(
        both.reshape(nlon, groups * sides, parts, STEP * 2).transpose(2, 1, 3, 0)
    ).reshape(parts, groups * sides * STEP * 2, nlon)
    weight_m = np.where(np.arange(MMAX) == 0, 1.0, 2.0)[None, :, None]
    inv_table = jnp.asarray((both * weight_m).reshape(nlon, 2 * MMAX), BF)

    gathered = []
    for part in range(parts):
        spec = forward_part(grid, jnp.asarray(fwd_table[part], BF))
        spec = spec.reshape(groups * sides, STEP, 2, cycles, width)
        spec = lax.all_to_all(spec, ("lat", "chan"), 0, 0, tiled=True)
        gathered.append(spec.reshape(groups, sides, STEP, 2, cycles, width))

    up = [(i, i + 1) for i in range(groups - 1)]
    down = [(j, i) for i, j in up]
    before = lax.ppermute(grid[-1:], "lat", up)
    after = lax.ppermute(grid[:1], "lat", down)
    own_cycles = rank * cycles + jnp.arange(cycles, dtype=jnp.int32)
    moved = own_cycles[:, None] + jnp.arange(-NEAR, NEAR + 1, dtype=jnp.int32)[None, :]
    ratio = jnp.sin(cycle_angle(moved, nlat)) / jnp.sin(cycle_angle(own_cycles, nlat))[:, None]
    by_lat = lat_offsets[None, :] == jnp.arange(-NEAR, NEAR + 1, dtype=jnp.int32)[:, None]
    by_lon = lon_offsets[None, :] == jnp.arange(-REACH, REACH + 1, dtype=jnp.int32)[:, None]
    hit = (by_lat[:, None, :] & by_lon[None, :, :])[..., None]
    weight = jnp.sum(jnp.where(hit, conv_weight[None, None], 0.0), axis=2)
    local = local_part(grid, before, after, ratio, weight)
    own = lax.dynamic_slice_in_dim(local, side * span, span, 0)
    got = lax.ppermute(
        lax.dynamic_slice_in_dim(local, (1 - side) * span, span, 0), "chan", SWAP
    )

    weights = lax.all_gather(mix_weight, "chan", axis=2, tiled=True)
    real_w, imag_w = (weights[0], weights[1])
    rows = []
    for at in range(sides):
        real_part = real_w[at * width : (at + 1) * width]
        imag_part = imag_w[at * width : (at + 1) * width]
        rows.append(jnp.concatenate([real_part, imag_part], axis=1))
        rows.append(jnp.concatenate([-imag_part, real_part], axis=1))
    mix = jnp.concatenate(rows, axis=0)
    theta = cycle_angle(jnp.arange(nlat, dtype=jnp.int32), nlat)
    quad = (math.pi / nlat * jnp.sin(theta))[None, :]
    gain = spectral_gain[:, None]

    filled = None
    for part in range(parts):
        offset = (side * few + part * STEP).astype(jnp.int32).reshape(1)
        filled = middle_part(
            part, gathered[part], basis, quad, mix, gain, offset, counts, filled
        )

    place = jnp.stack([side * span, side]).astype(jnp.int32)
    result = None
    start = 0
    sent = []
    for value, count in zip(filled, counts):
        back = lax.all_to_all(value, ("lat", "chan"), 0, 0, tiled=True)
        result, theirs = tail_part(
            back, own, got, start, inv_table, ln_gain[None, :], up_weight, down_weight,
            place, result, cycles,
        )
        sent.append((start, lax.ppermute(theirs, "chan", SWAP)))
        start += count
    for start, value in sent:
        result = lax.dynamic_update_slice_in_dim(result, value, (1 - side) * span + start, 0)
    return result


def padded_2(value, sides, width):
    for axis, dim in sides:
        size, length = (lax.axis_size(axis), value.shape[dim])
        up = [(i, (i + 1) % size) for i in range(size - 1)]
        down = [(j, i) for i, j in up]
        last = lax.slice_in_dim(value, length - width, length, axis=dim)
        first = lax.slice_in_dim(value, 0, width, axis=dim)
        before = lax.ppermute(last, axis, up)
        after = lax.ppermute(first, axis, down)
        value = jnp.concatenate([before, value, after], axis=dim)
    return value


def complex_mix(real_in, imag_in, real_w, imag_w):
    real_out = jnp.dot(real_in, real_w, preferred_element_type=jnp.float32) - jnp.dot(
        imag_in, imag_w, preferred_element_type=jnp.float32
    )
    imag_out = jnp.dot(real_in, imag_w, preferred_element_type=jnp.float32) + jnp.dot(
        imag_in, real_w, preferred_element_type=jnp.float32
    )
    return (real_out, imag_out)


def plain(
    grid,
    basis,
    mix_weight,
    spectral_gain,
    conv_weight,
    lat_offsets,
    lon_offsets,
    ln_gain,
    up_weight,
    down_weight,
):
    cycles, nlon, width = grid.shape
    groups = lax.axis_size("lat")
    rank = lax.axis_index("lat")
    nlat = cycles * groups
    modes = basis.shape[0]
    points = jnp.arange(nlon, dtype=jnp.int32)
    all_orders = jnp.arange(MMAX, dtype=jnp.int32)
    phase = points[:, None] * all_orders[None, :] % nlon
    angle = 2.0 * math.pi * phase.astype(jnp.float32) / nlon
    fwd_table = (
        jnp.stack([jnp.cos(angle), -jnp.sin(angle)], axis=-1)
        .reshape(nlon, 2 * MMAX)
        .astype(jnp.bfloat16)
    )
    weight_m = jnp.where(all_orders == 0, 1.0, 2.0).astype(jnp.float32)[None, :]
    inv_table = (
        jnp.stack([weight_m * jnp.cos(angle), -weight_m * jnp.sin(angle)], axis=-1)
        .reshape(nlon, 2 * MMAX)
        .T.astype(jnp.bfloat16)
    )
    spec = jnp.einsum("tpc,pk->tkc", grid, fwd_table, preferred_element_type=jnp.float32) * (
        1.0 / nlon
    )
    spec = spec.astype(jnp.bfloat16).reshape(cycles, groups, modes, 2, width)
    gathered = lax.all_to_all(spec, "lat", split_axis=1, concat_axis=0, tiled=True).reshape(
        nlat, modes, 2 * width
    )
    theta = cycle_angle(jnp.arange(nlat, dtype=jnp.int32), nlat)
    quad = math.pi / nlat * jnp.sin(theta)
    fwd_leg = (basis * quad[None, None, :]).astype(jnp.bfloat16)
    inv_leg = basis.astype(jnp.bfloat16)
    coeff = jnp.einsum(
        "jlt,tjk->jlk", fwd_leg, gathered, preferred_element_type=jnp.float32
    ).astype(jnp.bfloat16)
    coeff = coeff.reshape(modes, L, 2, width)
    piece = lax.all_gather(coeff, "chan", axis=3, tiled=True)
    count = piece.shape[3]
    real_w = mix_weight[0]
    imag_w = mix_weight[1]
    real_out, imag_out = complex_mix(
        piece[:, :, 0, :].reshape(-1, count), piece[:, :, 1, :].reshape(-1, count), real_w, imag_w
    )
    summed_modes = jnp.concatenate([real_out, imag_out], axis=1)
    mixed = (summed_modes.reshape(modes, L, 2 * width) * spectral_gain[None, :, None]).astype(
        jnp.bfloat16
    )
    back = jnp.einsum("jlt,jlk->tjk", inv_leg, mixed, preferred_element_type=jnp.float32).astype(
        jnp.bfloat16
    )
    back = lax.all_to_all(
        back.reshape(nlat, 1, modes, 2, width), "lat", split_axis=0, concat_axis=1, tiled=True
    )
    back = back.reshape(cycles, 2 * MMAX, width)
    spectral = jnp.einsum("tkc,kp->tpc", back, inv_table, preferred_element_type=jnp.float32)
    padded = padded_2(grid, (("lat", 0),), 1)
    own_cycles = rank * cycles + jnp.arange(cycles, dtype=jnp.int32)
    here = jnp.sin(cycle_angle(own_cycles, nlat))
    local = jnp.zeros((cycles, nlon, width), jnp.float32)
    for tap in range(conv_weight.shape[0]):
        shift = lat_offsets[tap]
        source = lax.dynamic_slice_in_dim(padded, 1 + shift, cycles, 0)
        source = jnp.roll(source, -lon_offsets[tap], axis=1)
        ratio = (jnp.sin(cycle_angle(own_cycles + shift, nlat)) / here)[:, None, None]
        local = local + conv_weight[tap][None, None, :] * ratio * source.astype(jnp.float32)
    summed = (spectral + local + grid.astype(jnp.float32)).astype(jnp.bfloat16)
    block = lax.all_to_all(summed, "chan", split_axis=1, concat_axis=2, tiled=True)
    count, span, channels = block.shape
    rows = block.reshape(-1, channels).astype(jnp.float32)
    center = jnp.mean(rows, axis=-1, keepdims=True)
    spread = jnp.mean((rows - center) ** 2, axis=-1, keepdims=True)
    normed = ((rows - center) / jnp.sqrt(spread + 1e-05) * ln_gain).astype(jnp.bfloat16)
    hidden = jax.nn.gelu(
        jnp.dot(normed, up_weight, preferred_element_type=jnp.float32), approximate=True
    ).astype(jnp.bfloat16)
    output = (jnp.dot(hidden, down_weight, preferred_element_type=jnp.float32) + rows).astype(
        jnp.bfloat16
    )
    return lax.all_to_all(
        output.reshape(count, span, channels), "chan", split_axis=2, concat_axis=1, tiled=True
    )


def on_device(*arguments):
    grid, basis = arguments[:2]
    cycles, nlon, width = grid.shape
    sides = lax.axis_size("chan")
    fits = (
        sides == 2
        and cycles % 8 == 0
        and cycles % sides == 0
        and basis.shape[0] % (sides * STEP) == 0
        and nlon % 8 == 0
        and width % 128 == 0
    )
    return (fast if fits else plain)(*arguments)


def solution(mesh):
    return jax.shard_map(
        on_device,
        mesh=mesh,
        in_specs=(
            P("lat", None, "chan"),
            P("lat", None, None),
            P(None, None, "chan"),
            P(),
            P(None, "chan"),
            P(),
            P(),
            P(),
            P(),
            P(),
        ),
        out_specs=P("lat", None, "chan"),
        check_vma=False,
    )
```

```python
import functools
import math

import jax
import jax.numpy as jnp
import numpy as np
from jax import lax
from jax.experimental import pallas as pl
from jax.experimental.pallas import tpu as pltpu
from jax.sharding import PartitionSpec as P

MMAX = 384
L = 384
STEP = 4
LANES = 128
NEAR = 1
REACH = 3
BF = jnp.bfloat16
F32 = jnp.float32
SWAP = [(0, 1), (1, 0)]


def cycle_angle(rows, nlat):
    return math.pi * (rows.astype(F32) + 0.5) / nlat


def params(mib):
    return pltpu.CompilerParams(vmem_limit_bytes=mib * 1024 * 1024)


def cost(flops, nbytes):
    return pl.CostEstimate(flops=int(flops), bytes_accessed=int(nbytes), transcendentals=0)


def angle_table(nlon):
    phase = np.arange(nlon)[:, None] * np.arange(MMAX)[None, :] % nlon
    angle = (2.0 * math.pi * phase / nlon).astype(np.float32).astype(np.float64)
    return np.cos(angle), np.sin(angle)


def forward_kernel(scale, table_ref, grid_ref, *rest):
    out_ref, held = rest[-2:]
    cycles = grid_ref.shape[0]
    rows = table_ref.shape[0]
    for t in range(cycles):
        value = jnp.dot(table_ref[...], grid_ref[t], preferred_element_type=F32)
        value = value * scale
        for at in range(held.shape[0]):
            held[at, pl.ds(t, rows, stride=cycles), :] = value[:, at * LANES : (at + 1) * LANES]
    for at in range(held.shape[0]):
        lanes = slice(at * LANES, (at + 1) * LANES)
        out_ref[:, :, lanes] = held[at].reshape(rows, cycles, LANES).astype(BF)


def forward_part(grid, table, first):
    cycles, nlon, width = grid.shape
    rows = table.shape[0]
    return pl.pallas_call(
        functools.partial(forward_kernel, 1.0 / nlon),
        out_shape=jax.ShapeDtypeStruct((rows, cycles, width), BF),
        in_specs=[pl.BlockSpec(memory_space=pltpu.VMEM)] * 2
        + [pl.BlockSpec(memory_space=pl.ANY)] * len(first),
        out_specs=pl.BlockSpec(memory_space=pltpu.VMEM),
        scratch_shapes=[pltpu.VMEM((width // LANES, rows * cycles, LANES), F32)],
        compiler_params=params(40),
        cost_estimate=cost(2 * rows * nlon * cycles * width, grid.size * 2),
    )(table, grid, *first)


def middle_kernel(counts, at_ref, spec_ref, basis_ref, quad_ref, own_ref, other_ref, gain_ref, *rest):
    outs, mix_ref, held = (rest[-len(counts) - 2 : -2], rest[-2], rest[-1])
    mode = pl.program_id(0)
    groups, sides, _, _, cycles, width = spec_ref.shape

    @pl.when(mode == 0)
    def _():
        first = at_ref[1] == 0
        channels = sides * width
        own = own_ref[...].astype(F32)
        other = other_ref[...].astype(F32)
        low = jnp.where(first, own, other)
        high = jnp.where(first, other, own)
        whole = jnp.concatenate([low, high], axis=2).astype(BF)
        for at in range(sides):
            block = whole[:, at * width : (at + 1) * width]
            real = pl.ds(2 * at * width, width)
            imag = pl.ds((2 * at + 1) * width, width)
            mix_ref[real, 0:channels] = block[0]
            mix_ref[real, channels : 2 * channels] = block[1]
            mix_ref[imag, 0:channels] = -block[1]
            mix_ref[imag, channels : 2 * channels] = block[0]

    nlat = groups * cycles
    table = basis_ref[0]
    forward = (table * quad_ref[...]).astype(BF)
    pieces = []
    for side in range(sides):
        for part in range(2):
            piece = spec_ref[:, side, 0, part, :, :].astype(F32)
            pieces.append(piece.reshape(nlat, width).astype(BF))
    spec = jnp.concatenate(pieces, axis=1)
    coeff = jnp.dot(forward, spec, preferred_element_type=F32).astype(BF)
    mixed = jnp.dot(coeff, mix_ref[...], preferred_element_type=F32) * gain_ref[...]
    inverse = table.T.astype(BF)
    back = jnp.dot(inverse, mixed.astype(BF), preferred_element_type=F32)
    half = back.shape[1] // 2
    slots = 2 * STEP
    for part in range(2):
        for where in range(STEP):

            @pl.when(mode == where)
            def _():
                row = 2 * where + part
                for at in range(half // LANES):
                    low = part * half + at * LANES
                    held[at, pl.ds(row, nlat, stride=slots), :] = back[:, low : low + LANES]

    @pl.when(mode == STEP - 1)
    def _():
        for at in range(half // LANES):
            whole = held[at].reshape(groups * sides, nlat // (groups * sides), slots, LANES)
            start = 0
            for out, count in zip(outs, counts):
                part = whole[:, start : start + count].astype(BF)
                out[:, 0, :, :, at * LANES : (at + 1) * LANES] = part
                start += count


def middle_part(part, spec, basis, quad, mix, other, gain, offset, counts, filled, first):
    groups, sides, _, _, cycles, width = spec.shape
    nlat = groups * cycles
    modes = basis.shape[0]
    parts = modes // sides // STEP
    channels = sides * width
    slots = 2 * STEP
    everywhere = [
        jax.ShapeDtypeStruct((groups * sides, parts, count, slots, channels), BF)
        for count in counts
    ]
    fixed = lambda m, at: (0, 0)
    specs = [
        pl.BlockSpec((groups, sides, 1, 2, cycles, width), lambda m, at: (0, 0, m, 0, 0, 0)),
        pl.BlockSpec((1, L, nlat), lambda m, at: (at[0] + m, 0, 0)),
        pl.BlockSpec((1, nlat), fixed),
        pl.BlockSpec(mix.shape, lambda m, at: (0, 0, 0)),
        pl.BlockSpec(mix.shape, lambda m, at: (0, 0, 0)),
        pl.BlockSpec((L, 1), fixed),
    ]
    arguments = [spec, basis, quad, mix, other, gain]
    aliases = {}
    if filled is not None:
        for at, value in enumerate(filled):
            aliases[1 + len(arguments)] = at
            specs.append(pl.BlockSpec(memory_space=pl.ANY))
            arguments.append(value)
    specs += [pl.BlockSpec(memory_space=pl.ANY)] * len(first)
    arguments += first
    return pl.pallas_call(
        functools.partial(middle_kernel, counts),
        out_shape=everywhere,
        grid_spec=pltpu.PrefetchScalarGridSpec(
            num_scalar_prefetch=1,
            grid=(STEP,),
            in_specs=specs,
            out_specs=[
                pl.BlockSpec(
                    (groups * sides, 1, count, slots, channels),
                    lambda m, at: (0, part, 0, 0, 0),
                )
                for count in counts
            ],
            scratch_shapes=[
                pltpu.VMEM((2 * channels, 2 * channels), BF),
                pltpu.VMEM((channels // LANES, nlat * slots, LANES), F32),
            ],
        ),
        input_output_aliases=aliases,
        compiler_params=params(56),
        cost_estimate=cost(
            2 * STEP * (2 * L * nlat * 2 * channels + L * 4 * channels * channels),
            STEP * (L * nlat * 4 + nlat * channels * 8) + mix.size * 2,
        ),
    )(offset, *arguments)


def local_rows(ratio_ref, weight_ref, here_ref, after_ref, edge_ref, tail_ref, out_ref, held):
    t = pl.program_id(0)
    cycles = pl.num_programs(0)
    _, nlon, width = out_ref.shape
    near = weight_ref.shape[0] // 2
    reach = weight_ref.shape[1] // 2
    pad = 8
    block = max(size for size in range(8, 73, 8) if nlon % size == 0)
    wide = block + 2 * pad

    def fill(slot, row):
        held[slot, pl.ds(pad, nlon), :] = row
        held[slot, pl.ds(0, pad), :] = row[nlon - pad :]
        held[slot, pl.ds(pad + nlon, pad), :] = row[:pad]

    @pl.when(t == 0)
    def _():
        fill(2, edge_ref[0].astype(F32))
        fill(0, here_ref[0].astype(F32))

    after = lax.rem(t + 1, 3)

    @pl.when(t < cycles - 1)
    def _():
        fill(after, after_ref[0].astype(F32))

    @pl.when(t == cycles - 1)
    def _():
        fill(after, tail_ref[0].astype(F32))

    slots = [lax.rem(t + 2 + a, 3) for a in range(2 * near + 1)]
    for low in range(0, width, LANES):
        lanes = slice(low, low + LANES)
        weights = [
            [weight_ref[a, b : b + 1, lanes] * ratio_ref[t, a] for b in range(2 * reach + 1)]
            for a in range(2 * near + 1)
        ]

        def body(at, carry):
            start = pl.multiple_of(at * block, 8)
            rows = [held[slot, pl.ds(start, wide), lanes] for slot in slots]
            total = rows[near][pad : pad + block]
            for b in range(2 * reach + 1):
                value = rows[0] * weights[0][b]
                for a in range(1, 2 * near + 1):
                    value = value + rows[a] * weights[a][b]
                if b != reach:
                    value = pltpu.roll(value, (wide + reach - b) % wide, 0)
                total = total + value[pad : pad + block]
            out_ref[0, pl.ds(start, block), lanes] = total.astype(BF)
            return carry

        lax.fori_loop(0, nlon // block, body, 0)


def local_part(grid, before, after, ratio, weight):
    cycles, nlon, width = grid.shape
    row = (1, nlon, width)
    edge = lambda t, _: (0, 0, 0)
    return pl.pallas_call(
        local_rows,
        out_shape=jax.ShapeDtypeStruct(grid.shape, BF),
        grid_spec=pltpu.PrefetchScalarGridSpec(
            num_scalar_prefetch=1,
            grid=(cycles,),
            in_specs=[
                pl.BlockSpec(weight.shape, lambda t, _: (0, 0, 0)),
                pl.BlockSpec(row, lambda t, _: (t, 0, 0)),
                pl.BlockSpec(row, lambda t, _: (jnp.minimum(t + 1, cycles - 1), 0, 0)),
                pl.BlockSpec(row, edge),
                pl.BlockSpec(row, edge),
            ],
            out_specs=pl.BlockSpec(row, lambda t, _: (t, 0, 0)),
            scratch_shapes=[pltpu.VMEM((3, nlon + 16, width), F32)],
        ),
        compiler_params=params(32),
        cost_estimate=cost(grid.size * 400, grid.size * 6),
    )(ratio, weight, grid, grid, before, after)


def tail_kernel(place_ref, back_ref, own_ref, got_ref, table_ref, gain_ref, up_ref, down_ref, *rest):
    mine_ref, theirs_ref = rest[-2:]
    first = place_ref[1] == 0
    channels = up_ref.shape[0]
    width = own_ref.shape[2]
    back = back_ref[:, :, 0].astype(F32).reshape(table_ref.shape[1], channels).astype(BF)
    spectral = jnp.dot(table_ref[...], back, preferred_element_type=F32)
    own = own_ref[0].astype(F32)
    got = got_ref[0].astype(F32)
    low = jnp.where(first, own, got)
    high = jnp.where(first, got, own)
    local = jnp.concatenate([low, high], axis=1)
    rows = (spectral + local).astype(BF).astype(F32)
    center = jnp.mean(rows, axis=-1, keepdims=True)
    moved = rows - center
    spread = jnp.mean(moved * moved, axis=-1, keepdims=True)
    normed = (moved * lax.rsqrt(spread + 1e-05) * gain_ref[...]).astype(BF)
    hidden = jax.nn.gelu(jnp.dot(normed, up_ref[...], preferred_element_type=F32), approximate=True)
    output = jnp.dot(hidden.astype(BF), down_ref[...], preferred_element_type=F32) + rows
    low = output[:, :width]
    high = output[:, width:]
    mine_ref[0] = jnp.where(first, low, high).astype(BF)
    theirs_ref[0] = jnp.where(first, high, low).astype(BF)


def tail_part(back, own, got, start, table, ln_gain, up_weight, down_weight, place, result, cycles):
    devices, parts, count, slots, channels = back.shape
    _, nlon, width = own.shape
    fixed = lambda t, at: (0, 0)
    row = (1, nlon, width)
    specs = [
        pl.BlockSpec((devices, parts, 1, slots, channels), lambda t, at: (0, 0, t, 0, 0)),
        pl.BlockSpec(row, lambda t, at: (start + t, 0, 0)),
        pl.BlockSpec(row, lambda t, at: (t, 0, 0)),
        pl.BlockSpec(table.shape, fixed),
        pl.BlockSpec(ln_gain.shape, fixed),
        pl.BlockSpec(up_weight.shape, fixed),
        pl.BlockSpec(down_weight.shape, fixed),
    ]
    arguments = [back, own, got, table, ln_gain, up_weight, down_weight]
    aliases = {}
    if result is not None:
        aliases[1 + len(arguments)] = 0
        specs.append(pl.BlockSpec(memory_space=pl.ANY))
        arguments.append(result)
    return pl.pallas_call(
        tail_kernel,
        out_shape=[
            jax.ShapeDtypeStruct((cycles, nlon, width), BF),
            jax.ShapeDtypeStruct((count, nlon, width), BF),
        ],
        grid_spec=pltpu.PrefetchScalarGridSpec(
            num_scalar_prefetch=1,
            grid=(count,),
            in_specs=specs,
            out_specs=[
                pl.BlockSpec(row, lambda t, at: (at[0] + start + t, 0, 0)),
                pl.BlockSpec(row, lambda t, at: (t, 0, 0)),
            ],
        ),
        input_output_aliases=aliases,
        compiler_params=params(56),
        cost_estimate=cost(
            2 * count * nlon * channels * (table.shape[1] + 2 * channels),
            count * nlon * channels * 8,
        ),
    )(place, *arguments)


def fast(grid, basis, mix_weight, spectral_gain, conv_weight, lat_offsets, lon_offsets, ln_gain, up_weight, down_weight):
    cycles, nlon, width = grid.shape
    groups = lax.axis_size("lat")
    sides = lax.axis_size("chan")
    rank = lax.axis_index("lat")
    side = lax.axis_index("chan")
    nlat = cycles * groups
    modes = basis.shape[0]
    few = modes // sides
    parts = few // STEP
    span = cycles // sides
    counts = [span // 2, span // 3, span // 6] if span % 6 == 0 else [span]

    cosine, sine = angle_table(nlon)
    both = np.stack([cosine, -sine], axis=-1)
    fwd_table = np.ascontiguousarray(
        both.reshape(nlon, groups * sides, parts, STEP * 2).transpose(2, 1, 3, 0)
    ).reshape(parts, groups * sides * STEP * 2, nlon)
    weight_m = np.where(np.arange(MMAX) == 0, 1.0, 2.0)[None, :, None]
    inv_table = jnp.asarray((both * weight_m).reshape(nlon, 2 * MMAX), BF)

    up = [(i, i + 1) for i in range(groups - 1)]
    down = [(j, i) for i, j in up]
    before = lax.ppermute(grid[-1:], "lat", up)
    after = lax.ppermute(grid[:1], "lat", down)
    own_cycles = rank * cycles + jnp.arange(cycles, dtype=jnp.int32)
    moved = own_cycles[:, None] + jnp.arange(-NEAR, NEAR + 1, dtype=jnp.int32)[None, :]
    ratio = jnp.sin(cycle_angle(moved, nlat)) / jnp.sin(cycle_angle(own_cycles, nlat))[:, None]
    by_lat = lat_offsets[None, :] == jnp.arange(-NEAR, NEAR + 1, dtype=jnp.int32)[:, None]
    by_lon = lon_offsets[None, :] == jnp.arange(-REACH, REACH + 1, dtype=jnp.int32)[:, None]
    hit = (by_lat[:, None, :] & by_lon[None, :, :])[..., None]
    weight = jnp.sum(jnp.where(hit, conv_weight[None, None], 0.0), axis=2)
    local = local_part(grid, before, after, ratio, weight)
    own = lax.dynamic_slice_in_dim(local, side * span, span, 0)
    got = []
    start = 0
    for count in counts:
        piece = lax.dynamic_slice_in_dim(local, (1 - side) * span + start, count, 0)
        got.append(lax.ppermute(piece, "chan", SWAP))
        start += count

    gathered = []
    for part in range(parts):
        first = [local] if part == min(1, parts - 1) else []
        spec = forward_part(grid, jnp.asarray(fwd_table[part], BF), first)
        spec = spec.reshape(groups * sides, STEP, 2, cycles, width)
        if part == parts - 1:
            spec, got[0] = lax.optimization_barrier((spec, got[0]))
        spec = lax.all_to_all(spec, ("lat", "chan"), 0, 0, tiled=True)
        gathered.append(spec.reshape(groups, sides, STEP, 2, cycles, width))

    other = lax.ppermute(mix_weight, "chan", SWAP)
    theta = cycle_angle(jnp.arange(nlat, dtype=jnp.int32), nlat)
    quad = (math.pi / nlat * jnp.sin(theta))[None, :]
    gain = spectral_gain[:, None]

    filled = None
    for part in range(parts):
        offset = jnp.stack([side * few + part * STEP, side]).astype(jnp.int32)
        filled = middle_part(
            part, gathered[part], basis, quad, mix_weight, other, gain, offset, counts, filled,
            got[1:] if part == parts - 1 else [],
        )

    place = jnp.stack([side * span, side]).astype(jnp.int32)
    result = None
    start = 0
    sent = []
    back = None
    for value, count in zip(filled, counts):
        if back is not None:
            value, back = lax.optimization_barrier((value, back))
        if len(sent) > 1:
            value, last = lax.optimization_barrier((value, sent[-2]))
            sent[-2] = last
        back = lax.all_to_all(value, ("lat", "chan"), 0, 0, tiled=True)
        result, theirs = tail_part(
            back, own, got[len(sent)], start, inv_table, ln_gain[None, :], up_weight, down_weight,
            place, result, cycles,
        )
        sent.append(lax.ppermute(theirs, "chan", SWAP))
        start += count
    start = 0
    for value, count in zip(sent, counts):
        result = lax.dynamic_update_slice_in_dim(result, value, (1 - side) * span + start, 0)
        start += count
    return result


def padded_2(value, sides, width):
    for axis, dim in sides:
        size, length = (lax.axis_size(axis), value.shape[dim])
        up = [(i, (i + 1) % size) for i in range(size - 1)]
        down = [(j, i) for i, j in up]
        last = lax.slice_in_dim(value, length - width, length, axis=dim)
        first = lax.slice_in_dim(value, 0, width, axis=dim)
        before = lax.ppermute(last, axis, up)
        after = lax.ppermute(first, axis, down)
        value = jnp.concatenate([before, value, after], axis=dim)
    return value


def complex_mix(real_in, imag_in, real_w, imag_w):
    real_out = jnp.dot(real_in, real_w, preferred_element_type=jnp.float32) - jnp.dot(
        imag_in, imag_w, preferred_element_type=jnp.float32
    )
    imag_out = jnp.dot(real_in, imag_w, preferred_element_type=jnp.float32) + jnp.dot(
        imag_in, real_w, preferred_element_type=jnp.float32
    )
    return (real_out, imag_out)


def plain(
    grid,
    basis,
    mix_weight,
    spectral_gain,
    conv_weight,
    lat_offsets,
    lon_offsets,
    ln_gain,
    up_weight,
    down_weight,
):
    cycles, nlon, width = grid.shape
    groups = lax.axis_size("lat")
    rank = lax.axis_index("lat")
    nlat = cycles * groups
    modes = basis.shape[0]
    points = jnp.arange(nlon, dtype=jnp.int32)
    all_orders = jnp.arange(MMAX, dtype=jnp.int32)
    phase = points[:, None] * all_orders[None, :] % nlon
    angle = 2.0 * math.pi * phase.astype(jnp.float32) / nlon
    fwd_table = (
        jnp.stack([jnp.cos(angle), -jnp.sin(angle)], axis=-1)
        .reshape(nlon, 2 * MMAX)
        .astype(jnp.bfloat16)
    )
    weight_m = jnp.where(all_orders == 0, 1.0, 2.0).astype(jnp.float32)[None, :]
    inv_table = (
        jnp.stack([weight_m * jnp.cos(angle), -weight_m * jnp.sin(angle)], axis=-1)
        .reshape(nlon, 2 * MMAX)
        .T.astype(jnp.bfloat16)
    )
    spec = jnp.einsum("tpc,pk->tkc", grid, fwd_table, preferred_element_type=jnp.float32) * (
        1.0 / nlon
    )
    spec = spec.astype(jnp.bfloat16).reshape(cycles, groups, modes, 2, width)
    gathered = lax.all_to_all(spec, "lat", split_axis=1, concat_axis=0, tiled=True).reshape(
        nlat, modes, 2 * width
    )
    theta = cycle_angle(jnp.arange(nlat, dtype=jnp.int32), nlat)
    quad = math.pi / nlat * jnp.sin(theta)
    fwd_leg = (basis * quad[None, None, :]).astype(jnp.bfloat16)
    inv_leg = basis.astype(jnp.bfloat16)
    coeff = jnp.einsum(
        "jlt,tjk->jlk", fwd_leg, gathered, preferred_element_type=jnp.float32
    ).astype(jnp.bfloat16)
    coeff = coeff.reshape(modes, L, 2, width)
    piece = lax.all_gather(coeff, "chan", axis=3, tiled=True)
    count = piece.shape[3]
    real_w = mix_weight[0]
    imag_w = mix_weight[1]
    real_out, imag_out = complex_mix(
        piece[:, :, 0, :].reshape(-1, count), piece[:, :, 1, :].reshape(-1, count), real_w, imag_w
    )
    summed_modes = jnp.concatenate([real_out, imag_out], axis=1)
    mixed = (summed_modes.reshape(modes, L, 2 * width) * spectral_gain[None, :, None]).astype(
        jnp.bfloat16
    )
    back = jnp.einsum("jlt,jlk->tjk", inv_leg, mixed, preferred_element_type=jnp.float32).astype(
        jnp.bfloat16
    )
    back = lax.all_to_all(
        back.reshape(nlat, 1, modes, 2, width), "lat", split_axis=0, concat_axis=1, tiled=True
    )
    back = back.reshape(cycles, 2 * MMAX, width)
    spectral = jnp.einsum("tkc,kp->tpc", back, inv_table, preferred_element_type=jnp.float32)
    padded = padded_2(grid, (("lat", 0),), 1)
    own_cycles = rank * cycles + jnp.arange(cycles, dtype=jnp.int32)
    here = jnp.sin(cycle_angle(own_cycles, nlat))
    local = jnp.zeros((cycles, nlon, width), jnp.float32)
    for tap in range(conv_weight.shape[0]):
        shift = lat_offsets[tap]
        source = lax.dynamic_slice_in_dim(padded, 1 + shift, cycles, 0)
        source = jnp.roll(source, -lon_offsets[tap], axis=1)
        ratio = (jnp.sin(cycle_angle(own_cycles + shift, nlat)) / here)[:, None, None]
        local = local + conv_weight[tap][None, None, :] * ratio * source.astype(jnp.float32)
    summed = (spectral + local + grid.astype(jnp.float32)).astype(jnp.bfloat16)
    block = lax.all_to_all(summed, "chan", split_axis=1, concat_axis=2, tiled=True)
    count, span, channels = block.shape
    rows = block.reshape(-1, channels).astype(jnp.float32)
    center = jnp.mean(rows, axis=-1, keepdims=True)
    spread = jnp.mean((rows - center) ** 2, axis=-1, keepdims=True)
    normed = ((rows - center) / jnp.sqrt(spread + 1e-05) * ln_gain).astype(jnp.bfloat16)
    hidden = jax.nn.gelu(
        jnp.dot(normed, up_weight, preferred_element_type=jnp.float32), approximate=True
    ).astype(jnp.bfloat16)
    output = (jnp.dot(hidden, down_weight, preferred_element_type=jnp.float32) + rows).astype(
        jnp.bfloat16
    )
    return lax.all_to_all(
        output.reshape(count, span, channels), "chan", split_axis=2, concat_axis=1, tiled=True
    )


def on_device(*arguments):
    grid, basis = arguments[:2]
    cycles, nlon, width = grid.shape
    sides = lax.axis_size("chan")
    fits = (
        sides == 2
        and cycles % 8 == 0
        and cycles % sides == 0
        and basis.shape[0] % (sides * STEP) == 0
        and nlon % 8 == 0
        and width % 128 == 0
    )
    return (fast if fits else plain)(*arguments)


def solution(mesh):
    return jax.shard_map(
        on_device,
        mesh=mesh,
        in_specs=(
            P("lat", None, "chan"),
            P("lat", None, None),
            P(None, None, "chan"),
            P(),
            P(None, "chan"),
            P(),
            P(),
            P(),
            P(),
            P(),
        ),
        out_specs=P("lat", None, "chan"),
        check_vma=False,
    )
```

```python
import functools
import math

import jax
import jax.numpy as jnp
import numpy as np
from jax import lax
from jax.experimental import pallas as pl
from jax.experimental.pallas import tpu as pltpu
from jax.sharding import PartitionSpec as P

MMAX = 384
L = 384
STEP = 4
LANES = 128
NEAR = 1
REACH = 3
BF = jnp.bfloat16
F32 = jnp.float32
SWAP = [(0, 1), (1, 0)]


def cycle_angle(rows, nlat):
    return math.pi * (rows.astype(F32) + 0.5) / nlat


def params(mib):
    return pltpu.CompilerParams(vmem_limit_bytes=mib * 1024 * 1024)


def cost(flops, nbytes):
    return pl.CostEstimate(flops=int(flops), bytes_accessed=int(nbytes), transcendentals=0)


def angle_table(nlon):
    phase = np.arange(nlon)[:, None] * np.arange(MMAX)[None, :] % nlon
    angle = (2.0 * math.pi * phase / nlon).astype(np.float32).astype(np.float64)
    return np.cos(angle), np.sin(angle)


def forward_kernel(scale, table_ref, grid_ref, *rest):
    out_ref, held = rest[-2:]
    few = grid_ref.shape[0]
    cycles = out_ref.shape[1]
    rows = table_ref.shape[0]
    step = pl.program_id(0)
    for t in range(few):
        value = jnp.dot(table_ref[...], grid_ref[t], preferred_element_type=F32)
        value = value * scale
        for at in range(held.shape[0]):
            part = value[:, at * LANES : (at + 1) * LANES]
            held[at, pl.ds(step * few + t, rows, stride=cycles), :] = part

    @pl.when(step == pl.num_programs(0) - 1)
    def _():
        for at in range(held.shape[0]):
            lanes = slice(at * LANES, (at + 1) * LANES)
            out_ref[:, :, lanes] = held[at].reshape(rows, cycles, LANES).astype(BF)


def forward_part(grid, table, first):
    cycles, nlon, width = grid.shape
    rows = table.shape[0]
    few = 4
    return pl.pallas_call(
        functools.partial(forward_kernel, 1.0 / nlon),
        out_shape=jax.ShapeDtypeStruct((rows, cycles, width), BF),
        grid=(cycles // few,),
        in_specs=[
            pl.BlockSpec(table.shape, lambda t: (0, 0)),
            pl.BlockSpec((few, nlon, width), lambda t: (t, 0, 0)),
        ]
        + [pl.BlockSpec(memory_space=pl.ANY)] * len(first),
        out_specs=pl.BlockSpec((rows, cycles, width), lambda t: (0, 0, 0)),
        scratch_shapes=[pltpu.VMEM((width // LANES, rows * cycles, LANES), F32)],
        compiler_params=params(58),
        cost_estimate=cost(2 * rows * nlon * cycles * width, grid.size * 2),
    )(table, grid, *first)


def middle_kernel(counts, at_ref, spec_ref, basis_ref, quad_ref, own_ref, other_ref, gain_ref, *rest):
    outs, mix_ref, held = (rest[-len(counts) - 2 : -2], rest[-2], rest[-1])
    mode = pl.program_id(0)
    groups, sides, _, _, cycles, width = spec_ref.shape

    @pl.when(mode == 0)
    def _():
        first = at_ref[1] == 0
        channels = sides * width
        own = own_ref[...].astype(F32)
        other = other_ref[...].astype(F32)
        low = jnp.where(first, own, other)
        high = jnp.where(first, other, own)
        whole = jnp.concatenate([low, high], axis=2).astype(BF)
        for at in range(sides):
            block = whole[:, at * width : (at + 1) * width]
            real = pl.ds(2 * at * width, width)
            imag = pl.ds((2 * at + 1) * width, width)
            mix_ref[real, 0:channels] = block[0]
            mix_ref[real, channels : 2 * channels] = block[1]
            mix_ref[imag, 0:channels] = -block[1]
            mix_ref[imag, channels : 2 * channels] = block[0]

    nlat = groups * cycles
    table = basis_ref[0]
    forward = (table * quad_ref[...]).astype(BF)
    pieces = []
    for side in range(sides):
        for part in range(2):
            piece = spec_ref[:, side, 0, part, :, :].astype(F32)
            pieces.append(piece.reshape(nlat, width).astype(BF))
    spec = jnp.concatenate(pieces, axis=1)
    coeff = jnp.dot(forward, spec, preferred_element_type=F32).astype(BF)
    mixed = jnp.dot(coeff, mix_ref[...], preferred_element_type=F32) * gain_ref[...]
    inverse = table.T.astype(BF)
    back = jnp.dot(inverse, mixed.astype(BF), preferred_element_type=F32)
    half = back.shape[1] // 2
    slots = 2 * STEP
    for part in range(2):
        for where in range(STEP):

            @pl.when(mode == where)
            def _():
                row = 2 * where + part
                for at in range(half // LANES):
                    low = part * half + at * LANES
                    held[at, pl.ds(row, nlat, stride=slots), :] = back[:, low : low + LANES]

    @pl.when(mode == STEP - 1)
    def _():
        for at in range(half // LANES):
            whole = held[at].reshape(groups * sides, nlat // (groups * sides), slots, LANES)
            start = 0
            for out, count in zip(outs, counts):
                part = whole[:, start : start + count].astype(BF)
                out[:, 0, :, :, at * LANES : (at + 1) * LANES] = part
                start += count


def middle_part(part, spec, basis, quad, mix, other, gain, offset, counts, filled, first):
    groups, sides, _, _, cycles, width = spec.shape
    nlat = groups * cycles
    modes = basis.shape[0]
    parts = modes // sides // STEP
    channels = sides * width
    slots = 2 * STEP
    everywhere = [
        jax.ShapeDtypeStruct((groups * sides, parts, count, slots, channels), BF)
        for count in counts
    ]
    fixed = lambda m, at: (0, 0)
    specs = [
        pl.BlockSpec((groups, sides, 1, 2, cycles, width), lambda m, at: (0, 0, m, 0, 0, 0)),
        pl.BlockSpec((1, L, nlat), lambda m, at: (at[0] + m, 0, 0)),
        pl.BlockSpec((1, nlat), fixed),
        pl.BlockSpec(mix.shape, lambda m, at: (0, 0, 0)),
        pl.BlockSpec(mix.shape, lambda m, at: (0, 0, 0)),
        pl.BlockSpec((L, 1), fixed),
    ]
    arguments = [spec, basis, quad, mix, other, gain]
    aliases = {}
    if filled is not None:
        for at, value in enumerate(filled):
            aliases[1 + len(arguments)] = at
            specs.append(pl.BlockSpec(memory_space=pl.ANY))
            arguments.append(value)
    specs += [pl.BlockSpec(memory_space=pl.ANY)] * len(first)
    arguments += first
    return pl.pallas_call(
        functools.partial(middle_kernel, counts),
        out_shape=everywhere,
        grid_spec=pltpu.PrefetchScalarGridSpec(
            num_scalar_prefetch=1,
            grid=(STEP,),
            in_specs=specs,
            out_specs=[
                pl.BlockSpec(
                    (groups * sides, 1, count, slots, channels),
                    lambda m, at: (0, part, 0, 0, 0),
                )
                for count in counts
            ],
            scratch_shapes=[
                pltpu.VMEM((2 * channels, 2 * channels), BF),
                pltpu.VMEM((channels // LANES, nlat * slots, LANES), F32),
            ],
        ),
        input_output_aliases=aliases,
        compiler_params=params(60),
        cost_estimate=cost(
            2 * STEP * (2 * L * nlat * 2 * channels + L * 4 * channels * channels),
            STEP * (L * nlat * 4 + nlat * channels * 8) + mix.size * 2,
        ),
    )(offset, *arguments)


def local_rows(base_ref, ratio_ref, weight_ref, prev_ref, here_ref, after_ref, edge_ref, tail_ref, out_ref, held):
    t = pl.program_id(0)
    cycle = base_ref[0] + t
    cycles = base_ref[1]
    _, nlon, width = out_ref.shape
    near = weight_ref.shape[0] // 2
    reach = weight_ref.shape[1] // 2
    pad = 8
    block = max(size for size in range(8, 73, 8) if nlon % size == 0)
    wide = block + 2 * pad

    def fill(slot, row):
        held[slot, pl.ds(pad, nlon), :] = row
        held[slot, pl.ds(0, pad), :] = row[nlon - pad :]
        held[slot, pl.ds(pad + nlon, pad), :] = row[:pad]

    @pl.when(t == 0)
    def _():
        fill(0, here_ref[0].astype(F32))

        @pl.when(cycle == 0)
        def _():
            fill(2, edge_ref[0].astype(F32))

        @pl.when(cycle > 0)
        def _():
            fill(2, prev_ref[0].astype(F32))

    after = lax.rem(t + 1, 3)

    @pl.when(cycle < cycles - 1)
    def _():
        fill(after, after_ref[0].astype(F32))

    @pl.when(cycle == cycles - 1)
    def _():
        fill(after, tail_ref[0].astype(F32))

    slots = [lax.rem(t + 2 + a, 3) for a in range(2 * near + 1)]
    for low in range(0, width, LANES):
        lanes = slice(low, low + LANES)
        weights = [
            [weight_ref[a, b : b + 1, lanes] * ratio_ref[cycle, a] for b in range(2 * reach + 1)]
            for a in range(2 * near + 1)
        ]

        def body(at, carry):
            start = pl.multiple_of(at * block, 8)
            rows = [held[slot, pl.ds(start, wide), lanes] for slot in slots]
            total = rows[near][pad : pad + block]
            for b in range(2 * reach + 1):
                value = rows[0] * weights[0][b]
                for a in range(1, 2 * near + 1):
                    value = value + rows[a] * weights[a][b]
                if b != reach:
                    value = pltpu.roll(value, (wide + reach - b) % wide, 0)
                total = total + value[pad : pad + block]
            out_ref[0, pl.ds(start, block), lanes] = total.astype(BF)
            return carry

        lax.fori_loop(0, nlon // block, body, 0)


def local_part(grid, before, after, ratio, weight, base, span):
    cycles, nlon, width = grid.shape
    row = (1, nlon, width)
    edge = lambda t, *_: (0, 0, 0)
    return pl.pallas_call(
        local_rows,
        out_shape=jax.ShapeDtypeStruct((span, nlon, width), BF),
        grid_spec=pltpu.PrefetchScalarGridSpec(
            num_scalar_prefetch=2,
            grid=(span,),
            in_specs=[
                pl.BlockSpec(weight.shape, edge),
                pl.BlockSpec(row, lambda t, at, _: (jnp.maximum(at[0] - 1, 0), 0, 0)),
                pl.BlockSpec(row, lambda t, at, _: (at[0] + t, 0, 0)),
                pl.BlockSpec(row, lambda t, at, _: (jnp.minimum(at[0] + t + 1, cycles - 1), 0, 0)),
                pl.BlockSpec(row, edge),
                pl.BlockSpec(row, edge),
            ],
            out_specs=pl.BlockSpec(row, lambda t, *_: (t, 0, 0)),
            scratch_shapes=[pltpu.VMEM((3, nlon + 16, width), F32)],
        ),
        compiler_params=params(58),
        cost_estimate=cost(span * nlon * width * 400, span * nlon * width * 6),
    )(jnp.stack([base, cycles]).astype(jnp.int32), ratio, weight, grid, grid, grid, before, after)


def exchanged(value, counts):
    got = []
    start = 0
    for count in counts:
        piece = lax.slice_in_dim(value, start, start + count, axis=0)
        got.append(lax.ppermute(piece, "chan", SWAP))
        start += count
    return got


def tail_kernel(place_ref, back_ref, own_ref, got_ref, table_ref, gain_ref, up_ref, down_ref, *rest):
    mine_ref, theirs_ref = rest[-2:]
    first = place_ref[1] == 0
    channels = up_ref.shape[0]
    width = own_ref.shape[2]
    back = back_ref[:, :, 0].astype(F32).reshape(table_ref.shape[1], channels).astype(BF)
    spectral = jnp.dot(table_ref[...], back, preferred_element_type=F32)
    own = own_ref[0].astype(F32)
    got = got_ref[0].astype(F32)
    low = jnp.where(first, own, got)
    high = jnp.where(first, got, own)
    local = jnp.concatenate([low, high], axis=1)
    rows = (spectral + local).astype(BF).astype(F32)
    center = jnp.mean(rows, axis=-1, keepdims=True)
    moved = rows - center
    spread = jnp.mean(moved * moved, axis=-1, keepdims=True)
    normed = (moved * lax.rsqrt(spread + 1e-05) * gain_ref[...]).astype(BF)
    hidden = jax.nn.gelu(jnp.dot(normed, up_ref[...], preferred_element_type=F32), approximate=True)
    output = jnp.dot(hidden.astype(BF), down_ref[...], preferred_element_type=F32) + rows
    low = output[:, :width]
    high = output[:, width:]
    mine_ref[0] = jnp.where(first, low, high).astype(BF)
    theirs_ref[0] = jnp.where(first, high, low).astype(BF)


def tail_part(back, own, got, start, table, ln_gain, up_weight, down_weight, place, result, cycles):
    devices, parts, count, slots, channels = back.shape
    _, nlon, width = own.shape
    fixed = lambda t, at: (0, 0)
    row = (1, nlon, width)
    specs = [
        pl.BlockSpec((devices, parts, 1, slots, channels), lambda t, at: (0, 0, t, 0, 0)),
        pl.BlockSpec(row, lambda t, at: (start + t, 0, 0)),
        pl.BlockSpec(row, lambda t, at: (t, 0, 0)),
        pl.BlockSpec(table.shape, fixed),
        pl.BlockSpec(ln_gain.shape, fixed),
        pl.BlockSpec(up_weight.shape, fixed),
        pl.BlockSpec(down_weight.shape, fixed),
    ]
    arguments = [back, own, got, table, ln_gain, up_weight, down_weight]
    aliases = {}
    if result is not None:
        aliases[1 + len(arguments)] = 0
        specs.append(pl.BlockSpec(memory_space=pl.ANY))
        arguments.append(result)
    return pl.pallas_call(
        tail_kernel,
        out_shape=[
            jax.ShapeDtypeStruct((cycles, nlon, width), BF),
            jax.ShapeDtypeStruct((count, nlon, width), BF),
        ],
        grid_spec=pltpu.PrefetchScalarGridSpec(
            num_scalar_prefetch=1,
            grid=(count,),
            in_specs=specs,
            out_specs=[
                pl.BlockSpec(row, lambda t, at: (at[0] + start + t, 0, 0)),
                pl.BlockSpec(row, lambda t, at: (t, 0, 0)),
            ],
        ),
        input_output_aliases=aliases,
        compiler_params=params(60),
        cost_estimate=cost(
            2 * count * nlon * channels * (table.shape[1] + 2 * channels),
            count * nlon * channels * 8,
        ),
    )(place, *arguments)


def fast(grid, basis, mix_weight, spectral_gain, conv_weight, lat_offsets, lon_offsets, ln_gain, up_weight, down_weight):
    cycles, nlon, width = grid.shape
    groups = lax.axis_size("lat")
    sides = lax.axis_size("chan")
    rank = lax.axis_index("lat")
    side = lax.axis_index("chan")
    nlat = cycles * groups
    modes = basis.shape[0]
    few = modes // sides
    parts = few // STEP
    span = cycles // sides
    counts = [span // 4] * 4

    cosine, sine = angle_table(nlon)
    both = np.stack([cosine, -sine], axis=-1)
    fwd_table = np.ascontiguousarray(
        both.reshape(nlon, groups * sides, parts, STEP * 2).transpose(2, 1, 3, 0)
    ).reshape(parts, groups * sides * STEP * 2, nlon)
    weight_m = np.where(np.arange(MMAX) == 0, 1.0, 2.0)[None, :, None]
    inv_table = jnp.asarray((both * weight_m).reshape(nlon, 2 * MMAX), BF)

    up = [(i, i + 1) for i in range(groups - 1)]
    down = [(j, i) for i, j in up]
    before = lax.ppermute(grid[-1:], "lat", up)
    after = lax.ppermute(grid[:1], "lat", down)
    own_cycles = rank * cycles + jnp.arange(cycles, dtype=jnp.int32)
    moved = own_cycles[:, None] + jnp.arange(-NEAR, NEAR + 1, dtype=jnp.int32)[None, :]
    ratio = jnp.sin(cycle_angle(moved, nlat)) / jnp.sin(cycle_angle(own_cycles, nlat))[:, None]
    by_lat = lat_offsets[None, :] == jnp.arange(-NEAR, NEAR + 1, dtype=jnp.int32)[:, None]
    by_lon = lon_offsets[None, :] == jnp.arange(-REACH, REACH + 1, dtype=jnp.int32)[:, None]
    hit = (by_lat[:, None, :] & by_lon[None, :, :])[..., None]
    weight = jnp.sum(jnp.where(hit, conv_weight[None, None], 0.0), axis=2)

    other = lax.ppermute(mix_weight, "chan", SWAP)
    gathered = []
    for part in range(parts):
        spec = forward_part(grid, jnp.asarray(fwd_table[part], BF), [])
        spec = spec.reshape(groups * sides, STEP, 2, cycles, width)
        if part == 0:
            spec, before, after = lax.optimization_barrier((spec, before, after))
            asked = local_part(grid, before, after, ratio, weight, (1 - side) * span, span)
            got = exchanged(asked, counts)
        elif part == 1:
            spec, other, got[0] = lax.optimization_barrier((spec, other, got[0]))
            own = local_part(grid, before, after, ratio, weight, side * span, span)
        elif part == 2:
            spec, got[1], own = lax.optimization_barrier((spec, got[1], own))
        spec = lax.all_to_all(spec, ("lat", "chan"), 0, 0, tiled=True)
        gathered.append(spec.reshape(groups, sides, STEP, 2, cycles, width))

    theta = cycle_angle(jnp.arange(nlat, dtype=jnp.int32), nlat)
    quad = (math.pi / nlat * jnp.sin(theta))[None, :]
    gain = spectral_gain[:, None]

    filled = None
    for part in range(parts):
        offset = jnp.stack([side * few + part * STEP, side]).astype(jnp.int32)
        filled = middle_part(
            part, gathered[part], basis, quad, mix_weight, other, gain, offset, counts, filled,
            got[2:3] if part == parts - 1 else [],
        )

    place = jnp.stack([side * span, side]).astype(jnp.int32)
    result = None
    start = 0
    sent = []
    back = None
    for at, (value, count) in enumerate(zip(filled, counts)):
        if at > 0:
            value, back = lax.optimization_barrier((value, back))
        if at == 1:
            value, got[3] = lax.optimization_barrier((value, got[3]))
        if at > 1:
            value, sent[at - 2] = lax.optimization_barrier((value, sent[at - 2]))
        back = lax.all_to_all(value, ("lat", "chan"), 0, 0, tiled=True)
        result, theirs = tail_part(
            back, own, got[at], start, inv_table, ln_gain[None, :], up_weight, down_weight,
            place, result, cycles,
        )
        sent.append(lax.ppermute(theirs, "chan", SWAP))
        start += count
    start = 0
    for value, count in zip(sent, counts):
        result = lax.dynamic_update_slice_in_dim(result, value, (1 - side) * span + start, 0)
        start += count
    return result


def padded_2(value, sides, width):
    for axis, dim in sides:
        size, length = (lax.axis_size(axis), value.shape[dim])
        up = [(i, (i + 1) % size) for i in range(size - 1)]
        down = [(j, i) for i, j in up]
        last = lax.slice_in_dim(value, length - width, length, axis=dim)
        first = lax.slice_in_dim(value, 0, width, axis=dim)
        before = lax.ppermute(last, axis, up)
        after = lax.ppermute(first, axis, down)
        value = jnp.concatenate([before, value, after], axis=dim)
    return value


def complex_mix(real_in, imag_in, real_w, imag_w):
    real_out = jnp.dot(real_in, real_w, preferred_element_type=jnp.float32) - jnp.dot(
        imag_in, imag_w, preferred_element_type=jnp.float32
    )
    imag_out = jnp.dot(real_in, imag_w, preferred_element_type=jnp.float32) + jnp.dot(
        imag_in, real_w, preferred_element_type=jnp.float32
    )
    return (real_out, imag_out)


def plain(
    grid,
    basis,
    mix_weight,
    spectral_gain,
    conv_weight,
    lat_offsets,
    lon_offsets,
    ln_gain,
    up_weight,
    down_weight,
):
    cycles, nlon, width = grid.shape
    groups = lax.axis_size("lat")
    rank = lax.axis_index("lat")
    nlat = cycles * groups
    modes = basis.shape[0]
    points = jnp.arange(nlon, dtype=jnp.int32)
    all_orders = jnp.arange(MMAX, dtype=jnp.int32)
    phase = points[:, None] * all_orders[None, :] % nlon
    angle = 2.0 * math.pi * phase.astype(jnp.float32) / nlon
    fwd_table = (
        jnp.stack([jnp.cos(angle), -jnp.sin(angle)], axis=-1)
        .reshape(nlon, 2 * MMAX)
        .astype(jnp.bfloat16)
    )
    weight_m = jnp.where(all_orders == 0, 1.0, 2.0).astype(jnp.float32)[None, :]
    inv_table = (
        jnp.stack([weight_m * jnp.cos(angle), -weight_m * jnp.sin(angle)], axis=-1)
        .reshape(nlon, 2 * MMAX)
        .T.astype(jnp.bfloat16)
    )
    spec = jnp.einsum("tpc,pk->tkc", grid, fwd_table, preferred_element_type=jnp.float32) * (
        1.0 / nlon
    )
    spec = spec.astype(jnp.bfloat16).reshape(cycles, groups, modes, 2, width)
    gathered = lax.all_to_all(spec, "lat", split_axis=1, concat_axis=0, tiled=True).reshape(
        nlat, modes, 2 * width
    )
    theta = cycle_angle(jnp.arange(nlat, dtype=jnp.int32), nlat)
    quad = math.pi / nlat * jnp.sin(theta)
    fwd_leg = (basis * quad[None, None, :]).astype(jnp.bfloat16)
    inv_leg = basis.astype(jnp.bfloat16)
    coeff = jnp.einsum(
        "jlt,tjk->jlk", fwd_leg, gathered, preferred_element_type=jnp.float32
    ).astype(jnp.bfloat16)
    coeff = coeff.reshape(modes, L, 2, width)
    piece = lax.all_gather(coeff, "chan", axis=3, tiled=True)
    count = piece.shape[3]
    real_w = mix_weight[0]
    imag_w = mix_weight[1]
    real_out, imag_out = complex_mix(
        piece[:, :, 0, :].reshape(-1, count), piece[:, :, 1, :].reshape(-1, count), real_w, imag_w
    )
    summed_modes = jnp.concatenate([real_out, imag_out], axis=1)
    mixed = (summed_modes.reshape(modes, L, 2 * width) * spectral_gain[None, :, None]).astype(
        jnp.bfloat16
    )
    back = jnp.einsum("jlt,jlk->tjk", inv_leg, mixed, preferred_element_type=jnp.float32).astype(
        jnp.bfloat16
    )
    back = lax.all_to_all(
        back.reshape(nlat, 1, modes, 2, width), "lat", split_axis=0, concat_axis=1, tiled=True
    )
    back = back.reshape(cycles, 2 * MMAX, width)
    spectral = jnp.einsum("tkc,kp->tpc", back, inv_table, preferred_element_type=jnp.float32)
    padded = padded_2(grid, (("lat", 0),), 1)
    own_cycles = rank * cycles + jnp.arange(cycles, dtype=jnp.int32)
    here = jnp.sin(cycle_angle(own_cycles, nlat))
    local = jnp.zeros((cycles, nlon, width), jnp.float32)
    for tap in range(conv_weight.shape[0]):
        shift = lat_offsets[tap]
        source = lax.dynamic_slice_in_dim(padded, 1 + shift, cycles, 0)
        source = jnp.roll(source, -lon_offsets[tap], axis=1)
        ratio = (jnp.sin(cycle_angle(own_cycles + shift, nlat)) / here)[:, None, None]
        local = local + conv_weight[tap][None, None, :] * ratio * source.astype(jnp.float32)
    summed = (spectral + local + grid.astype(jnp.float32)).astype(jnp.bfloat16)
    block = lax.all_to_all(summed, "chan", split_axis=1, concat_axis=2, tiled=True)
    count, span, channels = block.shape
    rows = block.reshape(-1, channels).astype(jnp.float32)
    center = jnp.mean(rows, axis=-1, keepdims=True)
    spread = jnp.mean((rows - center) ** 2, axis=-1, keepdims=True)
    normed = ((rows - center) / jnp.sqrt(spread + 1e-05) * ln_gain).astype(jnp.bfloat16)
    hidden = jax.nn.gelu(
        jnp.dot(normed, up_weight, preferred_element_type=jnp.float32), approximate=True
    ).astype(jnp.bfloat16)
    output = (jnp.dot(hidden, down_weight, preferred_element_type=jnp.float32) + rows).astype(
        jnp.bfloat16
    )
    return lax.all_to_all(
        output.reshape(count, span, channels), "chan", split_axis=2, concat_axis=1, tiled=True
    )


def on_device(*arguments):
    grid, basis = arguments[:2]
    cycles, nlon, width = grid.shape
    sides = lax.axis_size("chan")
    fits = (
        sides == 2
        and cycles % 8 == 0
        and cycles % sides == 0
        and cycles // sides % 4 == 0
        and basis.shape[0] // (sides * STEP) == 3
        and basis.shape[0] % (sides * STEP) == 0
        and nlon % 8 == 0
        and width % 128 == 0
    )
    return (fast if fits else plain)(*arguments)


def solution(mesh):
    return jax.shard_map(
        on_device,
        mesh=mesh,
        in_specs=(
            P("lat", None, "chan"),
            P("lat", None, None),
            P(None, None, "chan"),
            P(),
            P(None, "chan"),
            P(),
            P(),
            P(),
            P(),
            P(),
        ),
        out_specs=P("lat", None, "chan"),
        check_vma=False,
    )
```

```python
import functools
import math

import jax
import jax.numpy as jnp
import numpy as np
from jax import lax
from jax.experimental import pallas as pl
from jax.experimental.pallas import tpu as pltpu
from jax.sharding import PartitionSpec as P

MMAX = 384
L = 384
STEP = 4
LANES = 128
NEAR = 1
REACH = 3
BF = jnp.bfloat16
F32 = jnp.float32
SWAP = [(0, 1), (1, 0)]


def cycle_angle(rows, nlat):
    return math.pi * (rows.astype(F32) + 0.5) / nlat


def params(mib):
    return pltpu.CompilerParams(vmem_limit_bytes=mib * 1024 * 1024)


def cost(flops, nbytes):
    return pl.CostEstimate(flops=int(flops), bytes_accessed=int(nbytes), transcendentals=0)


def angle_table(nlon):
    phase = np.arange(nlon)[:, None] * np.arange(MMAX)[None, :] % nlon
    angle = (2.0 * math.pi * phase / nlon).astype(np.float32).astype(np.float64)
    return np.cos(angle), np.sin(angle)


def forward_kernel(scale, table_ref, grid_ref, *rest):
    out_ref, held = rest[-2:]
    few = grid_ref.shape[0]
    cycles = out_ref.shape[1]
    rows = table_ref.shape[0]
    step = pl.program_id(0)
    for t in range(few):
        value = jnp.dot(table_ref[...], grid_ref[t], preferred_element_type=F32)
        value = value * scale
        for at in range(held.shape[0]):
            part = value[:, at * LANES : (at + 1) * LANES]
            held[at, pl.ds(step * few + t, rows, stride=cycles), :] = part

    @pl.when(step == pl.num_programs(0) - 1)
    def _():
        for at in range(held.shape[0]):
            lanes = slice(at * LANES, (at + 1) * LANES)
            out_ref[:, :, lanes] = held[at].reshape(rows, cycles, LANES).astype(BF)


def forward_part(grid, table, first):
    cycles, nlon, width = grid.shape
    rows = table.shape[0]
    few = 4
    return pl.pallas_call(
        functools.partial(forward_kernel, 1.0 / nlon),
        out_shape=jax.ShapeDtypeStruct((rows, cycles, width), BF),
        grid=(cycles // few,),
        in_specs=[
            pl.BlockSpec(table.shape, lambda t: (0, 0)),
            pl.BlockSpec((few, nlon, width), lambda t: (t, 0, 0)),
        ]
        + [pl.BlockSpec(memory_space=pl.ANY)] * len(first),
        out_specs=pl.BlockSpec((rows, cycles, width), lambda t: (0, 0, 0)),
        scratch_shapes=[pltpu.VMEM((width // LANES, rows * cycles, LANES), F32)],
        compiler_params=params(60),
        cost_estimate=cost(2 * rows * nlon * cycles * width, grid.size * 2),
    )(table, grid, *first)


def middle_kernel(plan, at_ref, spec_ref, basis_ref, quad_ref, own_ref, other_ref, gain_ref, *rest):
    outs, mix_ref, held = (rest[-len(plan) - 2 : -2], rest[-2], rest[-1])
    mode = pl.program_id(0)
    groups, sides, _, _, cycles, width = spec_ref.shape

    @pl.when(mode == 0)
    def _():
        first = at_ref[1] == 0
        channels = sides * width
        own = own_ref[...].astype(F32)
        other = other_ref[...].astype(F32)
        low = jnp.where(first, own, other)
        high = jnp.where(first, other, own)
        whole = jnp.concatenate([low, high], axis=2).astype(BF)
        for at in range(sides):
            block = whole[:, at * width : (at + 1) * width]
            real = pl.ds(2 * at * width, width)
            imag = pl.ds((2 * at + 1) * width, width)
            mix_ref[real, 0:channels] = block[0]
            mix_ref[real, channels : 2 * channels] = block[1]
            mix_ref[imag, 0:channels] = -block[1]
            mix_ref[imag, channels : 2 * channels] = block[0]

    nlat = groups * cycles
    table = basis_ref[0]
    forward = (table * quad_ref[...]).astype(BF)
    pieces = []
    for side in range(sides):
        for part in range(2):
            piece = spec_ref[:, side, 0, part, :, :].astype(F32)
            pieces.append(piece.reshape(nlat, width).astype(BF))
    spec = jnp.concatenate(pieces, axis=1)
    coeff = jnp.dot(forward, spec, preferred_element_type=F32).astype(BF)
    mixed = jnp.dot(coeff, mix_ref[...], preferred_element_type=F32) * gain_ref[...]
    inverse = table.T.astype(BF)
    back = jnp.dot(inverse, mixed.astype(BF), preferred_element_type=F32)
    half = back.shape[1] // 2
    slots = 2 * STEP
    for part in range(2):
        for where in range(STEP):

            @pl.when(mode == where)
            def _():
                row = 2 * where + part
                for at in range(half // LANES):
                    low = part * half + at * LANES
                    held[at, pl.ds(row, nlat, stride=slots), :] = back[:, low : low + LANES]

    @pl.when(mode == STEP - 1)
    def _():
        for at in range(half // LANES):
            whole = held[at].reshape(groups * sides, nlat // (groups * sides), slots, LANES)
            start = 0
            for out, (_, _, count) in zip(outs, plan):
                part = whole[:, start : start + count].astype(BF)
                out[:, 0, :, :, at * LANES : (at + 1) * LANES] = part
                start += count


def middle_part(spec, basis, quad, mix, other, gain, offset, plan, filled):
    groups, sides, _, _, cycles, width = spec.shape
    nlat = groups * cycles
    channels = sides * width
    slots = 2 * STEP
    fixed = lambda m, at: (0, 0)
    specs = [
        pl.BlockSpec((groups, sides, 1, 2, cycles, width), lambda m, at: (0, 0, m, 0, 0, 0)),
        pl.BlockSpec((1, L, nlat), lambda m, at: (at[0] + m, 0, 0)),
        pl.BlockSpec((1, nlat), fixed),
        pl.BlockSpec(mix.shape, lambda m, at: (0, 0, 0)),
        pl.BlockSpec(mix.shape, lambda m, at: (0, 0, 0)),
        pl.BlockSpec((L, 1), fixed),
    ]
    arguments = [spec, basis, quad, mix, other, gain]
    aliases = {}
    for at, value in enumerate(filled):
        if value is not None:
            aliases[1 + len(arguments)] = at
            specs.append(pl.BlockSpec(memory_space=pl.ANY))
            arguments.append(value)
    return pl.pallas_call(
        functools.partial(middle_kernel, plan),
        out_shape=[
            jax.ShapeDtypeStruct((groups * sides, total, count, slots, channels), BF)
            for total, _, count in plan
        ],
        grid_spec=pltpu.PrefetchScalarGridSpec(
            num_scalar_prefetch=1,
            grid=(STEP,),
            in_specs=specs,
            out_specs=[
                pl.BlockSpec(
                    (groups * sides, 1, count, slots, channels),
                    functools.partial(lambda slot, m, at: (0, slot, 0, 0, 0), slot),
                )
                for _, slot, count in plan
            ],
            scratch_shapes=[
                pltpu.VMEM((2 * channels, 2 * channels), BF),
                pltpu.VMEM((channels // LANES, nlat * slots, LANES), F32),
            ],
        ),
        input_output_aliases=aliases,
        compiler_params=params(60),
        cost_estimate=cost(
            2 * STEP * (2 * L * nlat * 2 * channels + L * 4 * channels * channels),
            STEP * (L * nlat * 4 + nlat * channels * 8) + mix.size * 2,
        ),
    )(offset, *arguments)


def local_rows(base_ref, ratio_ref, weight_ref, prev_ref, here_ref, after_ref, edge_ref, tail_ref, out_ref, held):
    t = pl.program_id(0)
    cycle = base_ref[0] + t
    cycles = base_ref[1]
    _, nlon, width = out_ref.shape
    near = weight_ref.shape[0] // 2
    reach = weight_ref.shape[1] // 2
    pad = 8
    block = max(size for size in range(8, 73, 8) if nlon % size == 0)
    wide = block + 2 * pad

    def fill(slot, row):
        held[slot, pl.ds(pad, nlon), :] = row
        held[slot, pl.ds(0, pad), :] = row[nlon - pad :]
        held[slot, pl.ds(pad + nlon, pad), :] = row[:pad]

    @pl.when(t == 0)
    def _():
        fill(0, here_ref[0].astype(F32))

        @pl.when(cycle == 0)
        def _():
            fill(2, edge_ref[0].astype(F32))

        @pl.when(cycle > 0)
        def _():
            fill(2, prev_ref[0].astype(F32))

    after = lax.rem(t + 1, 3)

    @pl.when(cycle < cycles - 1)
    def _():
        fill(after, after_ref[0].astype(F32))

    @pl.when(cycle == cycles - 1)
    def _():
        fill(after, tail_ref[0].astype(F32))

    slots = [lax.rem(t + 2 + a, 3) for a in range(2 * near + 1)]
    for low in range(0, width, LANES):
        lanes = slice(low, low + LANES)
        weights = [
            [weight_ref[a, b : b + 1, lanes] * ratio_ref[cycle, a] for b in range(2 * reach + 1)]
            for a in range(2 * near + 1)
        ]

        def body(at, carry):
            start = pl.multiple_of(at * block, 8)
            rows = [held[slot, pl.ds(start, wide), lanes] for slot in slots]
            total = rows[near][pad : pad + block]
            for b in range(2 * reach + 1):
                value = rows[0] * weights[0][b]
                for a in range(1, 2 * near + 1):
                    value = value + rows[a] * weights[a][b]
                if b != reach:
                    value = pltpu.roll(value, (wide + reach - b) % wide, 0)
                total = total + value[pad : pad + block]
            out_ref[0, pl.ds(start, block), lanes] = total.astype(BF)
            return carry

        lax.fori_loop(0, nlon // block, body, 0)


def local_part(grid, before, after, ratio, weight, base, span):
    cycles, nlon, width = grid.shape
    row = (1, nlon, width)
    edge = lambda t, *_: (0, 0, 0)
    return pl.pallas_call(
        local_rows,
        out_shape=jax.ShapeDtypeStruct((span, nlon, width), BF),
        grid_spec=pltpu.PrefetchScalarGridSpec(
            num_scalar_prefetch=2,
            grid=(span,),
            in_specs=[
                pl.BlockSpec(weight.shape, edge),
                pl.BlockSpec(row, lambda t, at, _: (jnp.maximum(at[0] - 1, 0), 0, 0)),
                pl.BlockSpec(row, lambda t, at, _: (at[0] + t, 0, 0)),
                pl.BlockSpec(row, lambda t, at, _: (jnp.minimum(at[0] + t + 1, cycles - 1), 0, 0)),
                pl.BlockSpec(row, edge),
                pl.BlockSpec(row, edge),
            ],
            out_specs=pl.BlockSpec(row, lambda t, *_: (t, 0, 0)),
            scratch_shapes=[pltpu.VMEM((3, nlon + 16, width), F32)],
        ),
        compiler_params=params(60),
        cost_estimate=cost(span * nlon * width * 400, span * nlon * width * 6),
    )(jnp.stack([base, cycles]).astype(jnp.int32), ratio, weight, grid, grid, grid, before, after)


def exchanged(value, counts):
    got = []
    start = 0
    for count in counts:
        piece = lax.slice_in_dim(value, start, start + count, axis=0)
        got.append(lax.ppermute(piece, "chan", SWAP))
        start += count
    return got


def tail_kernel(pieces, place_ref, own_ref, got_ref, gain_ref, up_ref, down_ref, *rest):
    mine_ref, theirs_ref = rest[-2:]
    first = place_ref[1] == 0
    channels = up_ref.shape[0]
    width = own_ref.shape[2]
    spectral = 0.0
    for back_ref, table_ref in zip(rest[:pieces], rest[pieces : 2 * pieces]):
        back = back_ref[:, :, 0].astype(F32).reshape(table_ref.shape[1], channels).astype(BF)
        spectral += jnp.dot(table_ref[...], back, preferred_element_type=F32)
    own = own_ref[0].astype(F32)
    got = got_ref[0].astype(F32)
    low = jnp.where(first, own, got)
    high = jnp.where(first, got, own)
    local = jnp.concatenate([low, high], axis=1)
    rows = (spectral + local).astype(BF).astype(F32)
    center = jnp.mean(rows, axis=-1, keepdims=True)
    moved = rows - center
    spread = jnp.mean(moved * moved, axis=-1, keepdims=True)
    normed = (moved * lax.rsqrt(spread + 1e-05) * gain_ref[...]).astype(BF)
    hidden = jax.nn.gelu(jnp.dot(normed, up_ref[...], preferred_element_type=F32), approximate=True)
    output = jnp.dot(hidden.astype(BF), down_ref[...], preferred_element_type=F32) + rows
    low = output[:, :width]
    high = output[:, width:]
    mine_ref[0] = jnp.where(first, low, high).astype(BF)
    theirs_ref[0] = jnp.where(first, high, low).astype(BF)


def tail_part(backs, tables, own, got, start, ln_gain, up_weight, down_weight, place, result, cycles):
    count = backs[0].shape[2]
    channels = backs[0].shape[4]
    _, nlon, width = own.shape
    fixed = lambda t, at: (0, 0)
    row = (1, nlon, width)
    specs = [
        pl.BlockSpec(row, lambda t, at: (start + t, 0, 0)),
        pl.BlockSpec(row, lambda t, at: (t, 0, 0)),
        pl.BlockSpec(ln_gain.shape, fixed),
        pl.BlockSpec(up_weight.shape, fixed),
        pl.BlockSpec(down_weight.shape, fixed),
    ]
    for back in backs:
        block = back.shape[:2] + (1,) + back.shape[3:]
        specs.append(pl.BlockSpec(block, lambda t, at: (0, 0, t, 0, 0)))
    specs += [pl.BlockSpec(table.shape, fixed) for table in tables]
    arguments = [own, got, ln_gain, up_weight, down_weight, *backs, *tables]
    aliases = {}
    if result is not None:
        aliases[1 + len(arguments)] = 0
        specs.append(pl.BlockSpec(memory_space=pl.ANY))
        arguments.append(result)
    return pl.pallas_call(
        functools.partial(tail_kernel, len(backs)),
        out_shape=[
            jax.ShapeDtypeStruct((cycles, nlon, width), BF),
            jax.ShapeDtypeStruct((count, nlon, width), BF),
        ],
        grid_spec=pltpu.PrefetchScalarGridSpec(
            num_scalar_prefetch=1,
            grid=(count,),
            in_specs=specs,
            out_specs=[
                pl.BlockSpec(row, lambda t, at: (at[0] + start + t, 0, 0)),
                pl.BlockSpec(row, lambda t, at: (t, 0, 0)),
            ],
        ),
        input_output_aliases=aliases,
        compiler_params=params(60),
        cost_estimate=cost(
            2 * count * nlon * channels * (sum(table.shape[1] for table in tables) + 2 * channels),
            count * nlon * channels * 8,
        ),
    )(place, *arguments)


def fast(grid, basis, mix_weight, spectral_gain, conv_weight, lat_offsets, lon_offsets, ln_gain, up_weight, down_weight):
    cycles, nlon, width = grid.shape
    groups = lax.axis_size("lat")
    sides = lax.axis_size("chan")
    rank = lax.axis_index("lat")
    side = lax.axis_index("chan")
    nlat = cycles * groups
    modes = basis.shape[0]
    few = modes // sides
    parts = few // STEP
    span = cycles // sides
    third = span // 3
    counts = [third + 1, third, span - 2 * third - 1]

    cosine, sine = angle_table(nlon)
    both = np.stack([cosine, -sine], axis=-1)
    fwd_table = np.ascontiguousarray(
        both.reshape(nlon, groups * sides, parts, STEP * 2).transpose(2, 1, 3, 0)
    ).reshape(parts, groups * sides * STEP * 2, nlon)
    weight_m = np.where(np.arange(MMAX) == 0, 1.0, 2.0)[None, :, None]
    inv_table = (both * weight_m).reshape(nlon, groups * sides, parts, STEP * 2)

    def inverse(low, high):
        return jnp.asarray(inv_table[:, :, low:high].reshape(nlon, -1), BF)


    up = [(i, i + 1) for i in range(groups - 1)]
    down = [(j, i) for i, j in up]
    before = lax.ppermute(grid[-1:], "lat", up)
    after = lax.ppermute(grid[:1], "lat", down)
    own_cycles = rank * cycles + jnp.arange(cycles, dtype=jnp.int32)
    moved = own_cycles[:, None] + jnp.arange(-NEAR, NEAR + 1, dtype=jnp.int32)[None, :]
    ratio = jnp.sin(cycle_angle(moved, nlat)) / jnp.sin(cycle_angle(own_cycles, nlat))[:, None]
    by_lat = lat_offsets[None, :] == jnp.arange(-NEAR, NEAR + 1, dtype=jnp.int32)[:, None]
    by_lon = lon_offsets[None, :] == jnp.arange(-REACH, REACH + 1, dtype=jnp.int32)[:, None]
    hit = (by_lat[:, None, :] & by_lon[None, :, :])[..., None]
    weight = jnp.sum(jnp.where(hit, conv_weight[None, None], 0.0), axis=2)

    other = lax.ppermute(mix_weight, "chan", SWAP)
    gathered = []
    for part in range(parts):
        spec = forward_part(grid, jnp.asarray(fwd_table[part], BF), [])
        spec = spec.reshape(groups * sides, STEP, 2, cycles, width)
        if part == 0:
            spec, before, after, other = lax.optimization_barrier((spec, before, after, other))
            asked = local_part(grid, before, after, ratio, weight, (1 - side) * span, span)
            got = exchanged(asked, counts)
        elif part == 1:
            spec, got[2] = lax.optimization_barrier((spec, got[2]))
            own = local_part(grid, before, after, ratio, weight, side * span, span)
        elif part == 2:
            spec, got[1], own = lax.optimization_barrier((spec, got[1], own))
        spec = lax.all_to_all(spec, ("lat", "chan"), 0, 0, tiled=True)
        gathered.append(spec.reshape(groups, sides, STEP, 2, cycles, width))

    theta = cycle_angle(jnp.arange(nlat, dtype=jnp.int32), nlat)
    quad = (math.pi / nlat * jnp.sin(theta))[None, :]
    gain = spectral_gain[:, None]

    begin, filled = (None, [None] * 2)
    for part in range(parts):
        offset = jnp.stack([side * few + part * STEP, side]).astype(jnp.int32)
        late = part == parts - 1
        plan = [(1, 0, counts[0]) if late else (parts - 1, part, counts[0])]
        plan += [(parts, part, count) for count in counts[1:]]
        value = None if late else begin
        ready = middle_part(
            gathered[part], basis, quad, mix_weight, other, gain, offset, plan, [value] + filled
        )
        if late:
            end = ready[0]
        else:
            begin = ready[0]
        filled = list(ready[1:])

    def shuffled(value):
        return lax.all_to_all(value, ("lat", "chan"), 0, 0, tiled=True)

    place = jnp.stack([side * span, side]).astype(jnp.int32)

    def finished(at, backs, tables, result):
        result, theirs = tail_part(
            backs, tables, own, got[at], sum(counts[:at]), ln_gain[None, :], up_weight,
            down_weight, place, result, cycles,
        )
        return (result, theirs)

    begin, _ = lax.optimization_barrier((begin, gathered[-1]))
    begin = shuffled(begin)
    end, begin, got[0] = lax.optimization_barrier((end, begin, got[0]))
    end = shuffled(end)
    second, end = lax.optimization_barrier((filled[0], end))
    second = shuffled(second)
    result, theirs = finished(
        0, [begin, end], [inverse(0, parts - 1), inverse(parts - 1, parts)], None
    )
    sent = [lax.ppermute(theirs[: counts[2]], "chan", SWAP)]
    rest = lax.ppermute(theirs[counts[2] :], "chan", SWAP)
    third, second, _ = lax.optimization_barrier((filled[1], second, sent[0]))
    third = shuffled(third)
    result, theirs = finished(1, [second], [inverse(0, parts)], result)
    sent += [rest, lax.ppermute(theirs, "chan", SWAP)]
    third, sent[1] = lax.optimization_barrier((third, sent[1]))
    result, theirs = finished(2, [third], [inverse(0, parts)], result)
    sent.append(lax.ppermute(theirs, "chan", SWAP))
    start = 0
    for value in sent:
        count = value.shape[0]
        result = lax.dynamic_update_slice_in_dim(result, value, (1 - side) * span + start, 0)
        start += count
    return result


def padded_2(value, sides, width):
    for axis, dim in sides:
        size, length = (lax.axis_size(axis), value.shape[dim])
        up = [(i, (i + 1) % size) for i in range(size - 1)]
        down = [(j, i) for i, j in up]
        last = lax.slice_in_dim(value, length - width, length, axis=dim)
        first = lax.slice_in_dim(value, 0, width, axis=dim)
        before = lax.ppermute(last, axis, up)
        after = lax.ppermute(first, axis, down)
        value = jnp.concatenate([before, value, after], axis=dim)
    return value


def complex_mix(real_in, imag_in, real_w, imag_w):
    real_out = jnp.dot(real_in, real_w, preferred_element_type=jnp.float32) - jnp.dot(
        imag_in, imag_w, preferred_element_type=jnp.float32
    )
    imag_out = jnp.dot(real_in, imag_w, preferred_element_type=jnp.float32) + jnp.dot(
        imag_in, real_w, preferred_element_type=jnp.float32
    )
    return (real_out, imag_out)


def plain(
    grid,
    basis,
    mix_weight,
    spectral_gain,
    conv_weight,
    lat_offsets,
    lon_offsets,
    ln_gain,
    up_weight,
    down_weight,
):
    cycles, nlon, width = grid.shape
    groups = lax.axis_size("lat")
    rank = lax.axis_index("lat")
    nlat = cycles * groups
    modes = basis.shape[0]
    points = jnp.arange(nlon, dtype=jnp.int32)
    all_orders = jnp.arange(MMAX, dtype=jnp.int32)
    phase = points[:, None] * all_orders[None, :] % nlon
    angle = 2.0 * math.pi * phase.astype(jnp.float32) / nlon
    fwd_table = (
        jnp.stack([jnp.cos(angle), -jnp.sin(angle)], axis=-1)
        .reshape(nlon, 2 * MMAX)
        .astype(jnp.bfloat16)
    )
    weight_m = jnp.where(all_orders == 0, 1.0, 2.0).astype(jnp.float32)[None, :]
    inv_table = (
        jnp.stack([weight_m * jnp.cos(angle), -weight_m * jnp.sin(angle)], axis=-1)
        .reshape(nlon, 2 * MMAX)
        .T.astype(jnp.bfloat16)
    )
    spec = jnp.einsum("tpc,pk->tkc", grid, fwd_table, preferred_element_type=jnp.float32) * (
        1.0 / nlon
    )
    spec = spec.astype(jnp.bfloat16).reshape(cycles, groups, modes, 2, width)
    gathered = lax.all_to_all(spec, "lat", split_axis=1, concat_axis=0, tiled=True).reshape(
        nlat, modes, 2 * width
    )
    theta = cycle_angle(jnp.arange(nlat, dtype=jnp.int32), nlat)
    quad = math.pi / nlat * jnp.sin(theta)
    fwd_leg = (basis * quad[None, None, :]).astype(jnp.bfloat16)
    inv_leg = basis.astype(jnp.bfloat16)
    coeff = jnp.einsum(
        "jlt,tjk->jlk", fwd_leg, gathered, preferred_element_type=jnp.float32
    ).astype(jnp.bfloat16)
    coeff = coeff.reshape(modes, L, 2, width)
    piece = lax.all_gather(coeff, "chan", axis=3, tiled=True)
    count = piece.shape[3]
    real_w = mix_weight[0]
    imag_w = mix_weight[1]
    real_out, imag_out = complex_mix(
        piece[:, :, 0, :].reshape(-1, count), piece[:, :, 1, :].reshape(-1, count), real_w, imag_w
    )
    summed_modes = jnp.concatenate([real_out, imag_out], axis=1)
    mixed = (summed_modes.reshape(modes, L, 2 * width) * spectral_gain[None, :, None]).astype(
        jnp.bfloat16
    )
    back = jnp.einsum("jlt,jlk->tjk", inv_leg, mixed, preferred_element_type=jnp.float32).astype(
        jnp.bfloat16
    )
    back = lax.all_to_all(
        back.reshape(nlat, 1, modes, 2, width), "lat", split_axis=0, concat_axis=1, tiled=True
    )
    back = back.reshape(cycles, 2 * MMAX, width)
    spectral = jnp.einsum("tkc,kp->tpc", back, inv_table, preferred_element_type=jnp.float32)
    padded = padded_2(grid, (("lat", 0),), 1)
    own_cycles = rank * cycles + jnp.arange(cycles, dtype=jnp.int32)
    here = jnp.sin(cycle_angle(own_cycles, nlat))
    local = jnp.zeros((cycles, nlon, width), jnp.float32)
    for tap in range(conv_weight.shape[0]):
        shift = lat_offsets[tap]
        source = lax.dynamic_slice_in_dim(padded, 1 + shift, cycles, 0)
        source = jnp.roll(source, -lon_offsets[tap], axis=1)
        ratio = (jnp.sin(cycle_angle(own_cycles + shift, nlat)) / here)[:, None, None]
        local = local + conv_weight[tap][None, None, :] * ratio * source.astype(jnp.float32)
    summed = (spectral + local + grid.astype(jnp.float32)).astype(jnp.bfloat16)
    block = lax.all_to_all(summed, "chan", split_axis=1, concat_axis=2, tiled=True)
    count, span, channels = block.shape
    rows = block.reshape(-1, channels).astype(jnp.float32)
    center = jnp.mean(rows, axis=-1, keepdims=True)
    spread = jnp.mean((rows - center) ** 2, axis=-1, keepdims=True)
    normed = ((rows - center) / jnp.sqrt(spread + 1e-05) * ln_gain).astype(jnp.bfloat16)
    hidden = jax.nn.gelu(
        jnp.dot(normed, up_weight, preferred_element_type=jnp.float32), approximate=True
    ).astype(jnp.bfloat16)
    output = (jnp.dot(hidden, down_weight, preferred_element_type=jnp.float32) + rows).astype(
        jnp.bfloat16
    )
    return lax.all_to_all(
        output.reshape(count, span, channels), "chan", split_axis=2, concat_axis=1, tiled=True
    )


def on_device(*arguments):
    grid, basis = arguments[:2]
    cycles, nlon, width = grid.shape
    sides = lax.axis_size("chan")
    fits = (
        sides == 2
        and cycles % 8 == 0
        and cycles % sides == 0
        and cycles // sides >= 6
        and basis.shape[0] // (sides * STEP) == 3
        and basis.shape[0] % (sides * STEP) == 0
        and nlon % 8 == 0
        and width % 128 == 0
    )
    return (fast if fits else plain)(*arguments)


def solution(mesh):
    return jax.shard_map(
        on_device,
        mesh=mesh,
        in_specs=(
            P("lat", None, "chan"),
            P("lat", None, None),
            P(None, None, "chan"),
            P(),
            P(None, "chan"),
            P(),
            P(),
            P(),
            P(),
            P(),
        ),
        out_specs=P("lat", None, "chan"),
        check_vma=False,
    )
```

```python
import functools
import math

import jax
import jax.numpy as jnp
import numpy as np
from jax import lax
from jax.experimental import pallas as pl
from jax.experimental.pallas import tpu as pltpu
from jax.sharding import PartitionSpec as P

MMAX = 384
L = 384
STEP = 4
LANES = 128
NEAR = 1
REACH = 3
BF = jnp.bfloat16
F32 = jnp.float32
SWAP = [(0, 1), (1, 0)]


def cycle_angle(rows, nlat):
    return math.pi * (rows.astype(F32) + 0.5) / nlat


def params(mib):
    return pltpu.CompilerParams(vmem_limit_bytes=mib * 1024 * 1024)


def cost(flops, nbytes):
    return pl.CostEstimate(flops=int(flops), bytes_accessed=int(nbytes), transcendentals=0)


def angle_table(nlon):
    phase = np.arange(nlon)[:, None] * np.arange(MMAX)[None, :] % nlon
    angle = (2.0 * math.pi * phase / nlon).astype(np.float32).astype(np.float64)
    return np.cos(angle), np.sin(angle)


def forward_kernel(scale, table_ref, grid_ref, out_ref, held):
    few = grid_ref.shape[0]
    cycles = out_ref.shape[1]
    rows = table_ref.shape[0]
    step = pl.program_id(0)
    for t in range(few):
        value = jnp.dot(table_ref[...], grid_ref[t], preferred_element_type=F32)
        value = value * scale
        for at in range(held.shape[0]):
            part = value[:, at * LANES : (at + 1) * LANES]
            held[at, pl.ds(step * few + t, rows, stride=cycles), :] = part

    @pl.when(step == pl.num_programs(0) - 1)
    def _():
        for at in range(held.shape[0]):
            lanes = slice(at * LANES, (at + 1) * LANES)
            out_ref[:, :, lanes] = held[at].reshape(rows, cycles, LANES).astype(BF)


def forward_part(grid, table):
    cycles, nlon, width = grid.shape
    rows = table.shape[0]
    few = 4
    return pl.pallas_call(
        functools.partial(forward_kernel, 1.0 / nlon),
        out_shape=jax.ShapeDtypeStruct((rows, cycles, width), BF),
        grid=(cycles // few,),
        in_specs=[
            pl.BlockSpec(table.shape, lambda t: (0, 0)),
            pl.BlockSpec((few, nlon, width), lambda t: (t, 0, 0)),
        ],
        out_specs=pl.BlockSpec((rows, cycles, width), lambda t: (0, 0, 0)),
        scratch_shapes=[pltpu.VMEM((width // LANES, rows * cycles, LANES), F32)],
        compiler_params=params(60),
        cost_estimate=cost(2 * rows * nlon * cycles * width, grid.size * 2),
    )(table, grid)


def middle_kernel(plan, at_ref, spec_ref, basis_ref, quad_ref, own_ref, other_ref, gain_ref, *rest):
    outs, mix_ref, held = (rest[-len(plan) - 2 : -2], rest[-2], rest[-1])
    mode = pl.program_id(0)
    groups, sides, _, _, cycles, width = spec_ref.shape

    @pl.when(mode == 0)
    def _():
        first = at_ref[1] == 0
        channels = sides * width
        own = own_ref[...].astype(F32)
        other = other_ref[...].astype(F32)
        low = jnp.where(first, own, other)
        high = jnp.where(first, other, own)
        whole = jnp.concatenate([low, high], axis=2).astype(BF)
        for at in range(sides):
            block = whole[:, at * width : (at + 1) * width]
            real = pl.ds(2 * at * width, width)
            imag = pl.ds((2 * at + 1) * width, width)
            mix_ref[real, 0:channels] = block[0]
            mix_ref[real, channels : 2 * channels] = block[1]
            mix_ref[imag, 0:channels] = -block[1]
            mix_ref[imag, channels : 2 * channels] = block[0]

    nlat = groups * cycles
    table = basis_ref[0]
    forward = (table * quad_ref[...]).astype(BF)
    pieces = []
    for side in range(sides):
        for part in range(2):
            piece = spec_ref[:, side, 0, part, :, :].astype(F32)
            pieces.append(piece.reshape(nlat, width).astype(BF))
    spec = jnp.concatenate(pieces, axis=1)
    coeff = jnp.dot(forward, spec, preferred_element_type=F32).astype(BF)
    mixed = jnp.dot(coeff, mix_ref[...], preferred_element_type=F32) * gain_ref[...]
    inverse = table.T.astype(BF)
    back = jnp.dot(inverse, mixed.astype(BF), preferred_element_type=F32)
    half = back.shape[1] // 2
    slots = 2 * STEP
    for part in range(2):
        for where in range(STEP):

            @pl.when(mode == where)
            def _():
                row = 2 * where + part
                for at in range(half // LANES):
                    low = part * half + at * LANES
                    held[at, pl.ds(row, nlat, stride=slots), :] = back[:, low : low + LANES]

    @pl.when(mode == STEP - 1)
    def _():
        for at in range(half // LANES):
            whole = held[at].reshape(groups * sides, nlat // (groups * sides), slots, LANES)
            start = 0
            for out, (_, _, count) in zip(outs, plan):
                part = whole[:, start : start + count].astype(BF)
                out[:, 0, :, :, at * LANES : (at + 1) * LANES] = part
                start += count


def middle_part(spec, skip, basis, quad, mix, other, gain, offset, plan, filled):
    groups, sides, _, _, cycles, width = spec.shape
    nlat = groups * cycles
    channels = sides * width
    slots = 2 * STEP
    fixed = lambda m, at: (0, 0)
    specs = [
        pl.BlockSpec((groups, sides, 1, 2, cycles, width), lambda m, at: (0, 0, skip + m, 0, 0, 0)),
        pl.BlockSpec((1, L, nlat), lambda m, at: (at[0] + m, 0, 0)),
        pl.BlockSpec((1, nlat), fixed),
        pl.BlockSpec(mix.shape, lambda m, at: (0, 0, 0)),
        pl.BlockSpec(mix.shape, lambda m, at: (0, 0, 0)),
        pl.BlockSpec((L, 1), fixed),
    ]
    arguments = [spec, basis, quad, mix, other, gain]
    aliases = {}
    for at, value in enumerate(filled):
        if value is not None:
            aliases[1 + len(arguments)] = at
            specs.append(pl.BlockSpec(memory_space=pl.ANY))
            arguments.append(value)
    return pl.pallas_call(
        functools.partial(middle_kernel, plan),
        out_shape=[
            jax.ShapeDtypeStruct((groups * sides, total, count, slots, channels), BF)
            for total, _, count in plan
        ],
        grid_spec=pltpu.PrefetchScalarGridSpec(
            num_scalar_prefetch=1,
            grid=(STEP,),
            in_specs=specs,
            out_specs=[
                pl.BlockSpec(
                    (groups * sides, 1, count, slots, channels),
                    functools.partial(lambda slot, m, at: (0, slot, 0, 0, 0), slot),
                )
                for _, slot, count in plan
            ],
            scratch_shapes=[
                pltpu.VMEM((2 * channels, 2 * channels), BF),
                pltpu.VMEM((channels // LANES, nlat * slots, LANES), F32),
            ],
        ),
        input_output_aliases=aliases,
        compiler_params=params(60),
        cost_estimate=cost(
            2 * STEP * (2 * L * nlat * 2 * channels + L * 4 * channels * channels),
            STEP * (L * nlat * 4 + nlat * channels * 8) + mix.size * 2,
        ),
    )(offset, *arguments)


def local_rows(base_ref, ratio_ref, weight_ref, prev_ref, here_ref, after_ref, edge_ref, tail_ref, out_ref, held):
    t = pl.program_id(0)
    cycle = base_ref[0] + t
    cycles = base_ref[1]
    _, nlon, width = out_ref.shape
    near = weight_ref.shape[0] // 2
    reach = weight_ref.shape[1] // 2
    pad = 8
    block = max(size for size in range(8, 73, 8) if nlon % size == 0)
    wide = block + 2 * pad

    def fill(slot, row):
        held[slot, pl.ds(pad, nlon), :] = row
        held[slot, pl.ds(0, pad), :] = row[nlon - pad :]
        held[slot, pl.ds(pad + nlon, pad), :] = row[:pad]

    @pl.when(t == 0)
    def _():
        fill(0, here_ref[0].astype(F32))

        @pl.when(cycle == 0)
        def _():
            fill(2, edge_ref[0].astype(F32))

        @pl.when(cycle > 0)
        def _():
            fill(2, prev_ref[0].astype(F32))

    after = lax.rem(t + 1, 3)

    @pl.when(cycle < cycles - 1)
    def _():
        fill(after, after_ref[0].astype(F32))

    @pl.when(cycle == cycles - 1)
    def _():
        fill(after, tail_ref[0].astype(F32))

    slots = [lax.rem(t + 2 + a, 3) for a in range(2 * near + 1)]
    for low in range(0, width, LANES):
        lanes = slice(low, low + LANES)
        weights = [
            [weight_ref[a, b : b + 1, lanes] * ratio_ref[cycle, a] for b in range(2 * reach + 1)]
            for a in range(2 * near + 1)
        ]

        def body(at, carry):
            start = pl.multiple_of(at * block, 8)
            rows = [held[slot, pl.ds(start, wide), lanes] for slot in slots]
            total = rows[near][pad : pad + block]
            for b in range(2 * reach + 1):
                value = rows[0] * weights[0][b]
                for a in range(1, 2 * near + 1):
                    value = value + rows[a] * weights[a][b]
                if b != reach:
                    value = pltpu.roll(value, (wide + reach - b) % wide, 0)
                total = total + value[pad : pad + block]
            out_ref[0, pl.ds(start, block), lanes] = total.astype(BF)
            return carry

        lax.fori_loop(0, nlon // block, body, 0)


def local_part(grid, before, after, ratio, weight, base, span):
    cycles, nlon, width = grid.shape
    row = (1, nlon, width)
    edge = lambda t, *_: (0, 0, 0)
    return pl.pallas_call(
        local_rows,
        out_shape=jax.ShapeDtypeStruct((span, nlon, width), BF),
        grid_spec=pltpu.PrefetchScalarGridSpec(
            num_scalar_prefetch=2,
            grid=(span,),
            in_specs=[
                pl.BlockSpec(weight.shape, edge),
                pl.BlockSpec(row, lambda t, at, _: (jnp.maximum(at[0] - 1, 0), 0, 0)),
                pl.BlockSpec(row, lambda t, at, _: (at[0] + t, 0, 0)),
                pl.BlockSpec(row, lambda t, at, _: (jnp.minimum(at[0] + t + 1, cycles - 1), 0, 0)),
                pl.BlockSpec(row, edge),
                pl.BlockSpec(row, edge),
            ],
            out_specs=pl.BlockSpec(row, lambda t, *_: (t, 0, 0)),
            scratch_shapes=[pltpu.VMEM((3, nlon + 16, width), F32)],
        ),
        compiler_params=params(60),
        cost_estimate=cost(span * nlon * width * 400, span * nlon * width * 6),
    )(jnp.stack([base, cycles]).astype(jnp.int32), ratio, weight, grid, grid, grid, before, after)


def exchanged(value, counts):
    got = []
    start = 0
    for count in counts:
        piece = lax.slice_in_dim(value, start, start + count, axis=0)
        got.append(lax.ppermute(piece, "chan", SWAP))
        start += count
    return got


def tail_kernel(pieces, place_ref, own_ref, got_ref, gain_ref, up_ref, down_ref, *rest):
    mine_ref, theirs_ref = rest[-2:]
    first = place_ref[1] == 0
    channels = up_ref.shape[0]
    width = own_ref.shape[2]
    spectral = 0.0
    for back_ref, table_ref in zip(rest[:pieces], rest[pieces : 2 * pieces]):
        back = back_ref[:, :, 0].astype(F32).reshape(table_ref.shape[1], channels).astype(BF)
        spectral += jnp.dot(table_ref[...], back, preferred_element_type=F32)
    own = own_ref[0].astype(F32)
    got = got_ref[0].astype(F32)
    low = jnp.where(first, own, got)
    high = jnp.where(first, got, own)
    local = jnp.concatenate([low, high], axis=1)
    rows = (spectral + local).astype(BF).astype(F32)
    center = jnp.mean(rows, axis=-1, keepdims=True)
    moved = rows - center
    spread = jnp.mean(moved * moved, axis=-1, keepdims=True)
    normed = (moved * lax.rsqrt(spread + 1e-05) * gain_ref[...]).astype(BF)
    hidden = jax.nn.gelu(jnp.dot(normed, up_ref[...], preferred_element_type=F32), approximate=True)
    output = jnp.dot(hidden.astype(BF), down_ref[...], preferred_element_type=F32) + rows
    low = output[:, :width]
    high = output[:, width:]
    mine_ref[0] = jnp.where(first, low, high).astype(BF)
    theirs_ref[0] = jnp.where(first, high, low).astype(BF)


def tail_part(backs, tables, own, got, start, ln_gain, up_weight, down_weight, place, result, cycles):
    count = backs[0].shape[2]
    channels = backs[0].shape[4]
    _, nlon, width = own.shape
    fixed = lambda t, at: (0, 0)
    row = (1, nlon, width)
    specs = [
        pl.BlockSpec(row, lambda t, at: (start + t, 0, 0)),
        pl.BlockSpec(row, lambda t, at: (t, 0, 0)),
        pl.BlockSpec(ln_gain.shape, fixed),
        pl.BlockSpec(up_weight.shape, fixed),
        pl.BlockSpec(down_weight.shape, fixed),
    ]
    for back in backs:
        block = back.shape[:2] + (1,) + back.shape[3:]
        specs.append(pl.BlockSpec(block, lambda t, at: (0, 0, t, 0, 0)))
    specs += [pl.BlockSpec(table.shape, fixed) for table in tables]
    arguments = [own, got, ln_gain, up_weight, down_weight, *backs, *tables]
    aliases = {}
    if result is not None:
        aliases[1 + len(arguments)] = 0
        specs.append(pl.BlockSpec(memory_space=pl.ANY))
        arguments.append(result)
    return pl.pallas_call(
        functools.partial(tail_kernel, len(backs)),
        out_shape=[
            jax.ShapeDtypeStruct((cycles, nlon, width), BF),
            jax.ShapeDtypeStruct((count, nlon, width), BF),
        ],
        grid_spec=pltpu.PrefetchScalarGridSpec(
            num_scalar_prefetch=1,
            grid=(count,),
            in_specs=specs,
            out_specs=[
                pl.BlockSpec(row, lambda t, at: (at[0] + start + t, 0, 0)),
                pl.BlockSpec(row, lambda t, at: (t, 0, 0)),
            ],
        ),
        input_output_aliases=aliases,
        compiler_params=params(60),
        cost_estimate=cost(
            2 * count * nlon * channels * (sum(table.shape[1] for table in tables) + 2 * channels),
            count * nlon * channels * 8,
        ),
    )(place, *arguments)


def fast(grid, basis, mix_weight, spectral_gain, conv_weight, lat_offsets, lon_offsets, ln_gain, up_weight, down_weight):
    cycles, nlon, width = grid.shape
    groups = lax.axis_size("lat")
    sides = lax.axis_size("chan")
    rank = lax.axis_index("lat")
    side = lax.axis_index("chan")
    nlat = cycles * groups
    modes = basis.shape[0]
    few = modes // sides
    parts = few // STEP
    span = cycles // sides
    third = span // 3
    counts = [third, third, span - 2 * third - 1, 1]

    cosine, sine = angle_table(nlon)
    both = np.stack([cosine, -sine], axis=-1)
    fwd_table = both.reshape(nlon, groups * sides, few, 2).transpose(1, 2, 3, 0)
    weight_m = np.where(np.arange(MMAX) == 0, 1.0, 2.0)[None, :, None]
    inv_table = (both * weight_m).reshape(nlon, groups * sides, parts, STEP * 2)

    def inverse(low, high):
        return jnp.asarray(inv_table[:, :, low:high].reshape(nlon, -1), BF)


    up = [(i, i + 1) for i in range(groups - 1)]
    down = [(j, i) for i, j in up]
    before = lax.ppermute(grid[-1:], "lat", up)
    after = lax.ppermute(grid[:1], "lat", down)
    own_cycles = rank * cycles + jnp.arange(cycles, dtype=jnp.int32)
    moved = own_cycles[:, None] + jnp.arange(-NEAR, NEAR + 1, dtype=jnp.int32)[None, :]
    ratio = jnp.sin(cycle_angle(moved, nlat)) / jnp.sin(cycle_angle(own_cycles, nlat))[:, None]
    by_lat = lat_offsets[None, :] == jnp.arange(-NEAR, NEAR + 1, dtype=jnp.int32)[:, None]
    by_lon = lon_offsets[None, :] == jnp.arange(-REACH, REACH + 1, dtype=jnp.int32)[:, None]
    hit = (by_lat[:, None, :] & by_lon[None, :, :])[..., None]
    weight = jnp.sum(jnp.where(hit, conv_weight[None, None], 0.0), axis=2)

    other = lax.ppermute(mix_weight, "chan", SWAP)
    gathered = []
    bounds = [(0, STEP), (STEP, few)]
    for part, (low, high) in enumerate(bounds):
        table = jnp.asarray(fwd_table[:, low:high].reshape(-1, nlon), BF)
        spec = forward_part(grid, table)
        spec = spec.reshape(groups * sides, high - low, 2, cycles, width)
        if part == 0:
            spec, before, after, other = lax.optimization_barrier((spec, before, after, other))
            asked = local_part(grid, before, after, ratio, weight, (1 - side) * span, span)
            got = exchanged(asked, counts)
        else:
            spec, got[2] = lax.optimization_barrier((spec, got[2]))
            own = local_part(grid, before, after, ratio, weight, side * span, span)
        spec = lax.all_to_all(spec, ("lat", "chan"), 0, 0, tiled=True)
        gathered.append(spec.reshape(groups, sides, high - low, 2, cycles, width))

    theta = cycle_angle(jnp.arange(nlat, dtype=jnp.int32), nlat)
    quad = (math.pi / nlat * jnp.sin(theta))[None, :]
    gain = spectral_gain[:, None]

    filled = [None] * (len(counts) - 1)
    heads = []
    for part in range(parts):
        offset = jnp.stack([side * few + part * STEP, side]).astype(jnp.int32)
        plan = [(parts - 1, part - 1, counts[0]) if part else (1, 0, counts[0])]
        plan += [(parts, part, count) for count in counts[1:]]
        head = heads[-1] if part > 1 else None
        ready = middle_part(
            gathered[min(part, 1)], max(part - 1, 0) * STEP, basis, quad, mix_weight, other, gain,
            offset, plan, [head] + filled,
        )
        heads.append(ready[0])
        filled = list(ready[1:])

    def shuffled(value):
        return lax.all_to_all(value, ("lat", "chan"), 0, 0, tiled=True)

    place = jnp.stack([side * span, side]).astype(jnp.int32)

    def finished(at, backs, tables, result):
        result, theirs = tail_part(
            backs, tables, own, got[at], sum(counts[:at]), ln_gain[None, :], up_weight,
            down_weight, place, result, cycles,
        )
        cut = theirs.shape[0] * 3 // 4 if at == 1 else theirs.shape[0]
        pieces = [theirs[:cut], theirs[cut:]] if cut < theirs.shape[0] else [theirs]
        return (result, [lax.ppermute(piece, "chan", SWAP) for piece in pieces])

    begin, end = (heads[0], heads[-1])
    begin, _, own, got[0], got[1] = lax.optimization_barrier(
        (begin, gathered[1], own, got[0], got[1])
    )
    begin = shuffled(begin)
    end, begin = lax.optimization_barrier((end, begin))
    end = shuffled(end)
    backs = [[begin, end]]
    tables = [[inverse(0, 1), inverse(1, parts)]] + [[inverse(0, parts)]] * 3
    last = end
    result = None
    sent = []
    for at, value in enumerate(filled):
        if at == 0:
            value, last = lax.optimization_barrier((value, last))
            backs[0][1] = last
        else:
            value, last = lax.optimization_barrier((value, last))
            backs[-1] = [last]
        if at == 1:
            value, sent[0], got[3] = lax.optimization_barrier((value, sent[0], got[3]))
        if at > 1:
            value, sent[1] = lax.optimization_barrier((value, sent[1]))
        last = shuffled(value)
        result, values = finished(at, backs[-1], tables[at], result)
        sent += values
        backs.append([last])
    last, sent[2] = lax.optimization_barrier((last, sent[2]))
    result, values = finished(len(filled), [last], tables[-1], result)
    sent += values
    start = 0
    for value in sent:
        count = value.shape[0]
        result = lax.dynamic_update_slice_in_dim(result, value, (1 - side) * span + start, 0)
        start += count
    return result


def padded_2(value, sides, width):
    for axis, dim in sides:
        size, length = (lax.axis_size(axis), value.shape[dim])
        up = [(i, (i + 1) % size) for i in range(size - 1)]
        down = [(j, i) for i, j in up]
        last = lax.slice_in_dim(value, length - width, length, axis=dim)
        first = lax.slice_in_dim(value, 0, width, axis=dim)
        before = lax.ppermute(last, axis, up)
        after = lax.ppermute(first, axis, down)
        value = jnp.concatenate([before, value, after], axis=dim)
    return value


def complex_mix(real_in, imag_in, real_w, imag_w):
    real_out = jnp.dot(real_in, real_w, preferred_element_type=jnp.float32) - jnp.dot(
        imag_in, imag_w, preferred_element_type=jnp.float32
    )
    imag_out = jnp.dot(real_in, imag_w, preferred_element_type=jnp.float32) + jnp.dot(
        imag_in, real_w, preferred_element_type=jnp.float32
    )
    return (real_out, imag_out)


def plain(
    grid,
    basis,
    mix_weight,
    spectral_gain,
    conv_weight,
    lat_offsets,
    lon_offsets,
    ln_gain,
    up_weight,
    down_weight,
):
    cycles, nlon, width = grid.shape
    groups = lax.axis_size("lat")
    rank = lax.axis_index("lat")
    nlat = cycles * groups
    modes = basis.shape[0]
    points = jnp.arange(nlon, dtype=jnp.int32)
    all_orders = jnp.arange(MMAX, dtype=jnp.int32)
    phase = points[:, None] * all_orders[None, :] % nlon
    angle = 2.0 * math.pi * phase.astype(jnp.float32) / nlon
    fwd_table = (
        jnp.stack([jnp.cos(angle), -jnp.sin(angle)], axis=-1)
        .reshape(nlon, 2 * MMAX)
        .astype(jnp.bfloat16)
    )
    weight_m = jnp.where(all_orders == 0, 1.0, 2.0).astype(jnp.float32)[None, :]
    inv_table = (
        jnp.stack([weight_m * jnp.cos(angle), -weight_m * jnp.sin(angle)], axis=-1)
        .reshape(nlon, 2 * MMAX)
        .T.astype(jnp.bfloat16)
    )
    spec = jnp.einsum("tpc,pk->tkc", grid, fwd_table, preferred_element_type=jnp.float32) * (
        1.0 / nlon
    )
    spec = spec.astype(jnp.bfloat16).reshape(cycles, groups, modes, 2, width)
    gathered = lax.all_to_all(spec, "lat", split_axis=1, concat_axis=0, tiled=True).reshape(
        nlat, modes, 2 * width
    )
    theta = cycle_angle(jnp.arange(nlat, dtype=jnp.int32), nlat)
    quad = math.pi / nlat * jnp.sin(theta)
    fwd_leg = (basis * quad[None, None, :]).astype(jnp.bfloat16)
    inv_leg = basis.astype(jnp.bfloat16)
    coeff = jnp.einsum(
        "jlt,tjk->jlk", fwd_leg, gathered, preferred_element_type=jnp.float32
    ).astype(jnp.bfloat16)
    coeff = coeff.reshape(modes, L, 2, width)
    piece = lax.all_gather(coeff, "chan", axis=3, tiled=True)
    count = piece.shape[3]
    real_w = mix_weight[0]
    imag_w = mix_weight[1]
    real_out, imag_out = complex_mix(
        piece[:, :, 0, :].reshape(-1, count), piece[:, :, 1, :].reshape(-1, count), real_w, imag_w
    )
    summed_modes = jnp.concatenate([real_out, imag_out], axis=1)
    mixed = (summed_modes.reshape(modes, L, 2 * width) * spectral_gain[None, :, None]).astype(
        jnp.bfloat16
    )
    back = jnp.einsum("jlt,jlk->tjk", inv_leg, mixed, preferred_element_type=jnp.float32).astype(
        jnp.bfloat16
    )
    back = lax.all_to_all(
        back.reshape(nlat, 1, modes, 2, width), "lat", split_axis=0, concat_axis=1, tiled=True
    )
    back = back.reshape(cycles, 2 * MMAX, width)
    spectral = jnp.einsum("tkc,kp->tpc", back, inv_table, preferred_element_type=jnp.float32)
    padded = padded_2(grid, (("lat", 0),), 1)
    own_cycles = rank * cycles + jnp.arange(cycles, dtype=jnp.int32)
    here = jnp.sin(cycle_angle(own_cycles, nlat))
    local = jnp.zeros((cycles, nlon, width), jnp.float32)
    for tap in range(conv_weight.shape[0]):
        shift = lat_offsets[tap]
        source = lax.dynamic_slice_in_dim(padded, 1 + shift, cycles, 0)
        source = jnp.roll(source, -lon_offsets[tap], axis=1)
        ratio = (jnp.sin(cycle_angle(own_cycles + shift, nlat)) / here)[:, None, None]
        local = local + conv_weight[tap][None, None, :] * ratio * source.astype(jnp.float32)
    summed = (spectral + local + grid.astype(jnp.float32)).astype(jnp.bfloat16)
    block = lax.all_to_all(summed, "chan", split_axis=1, concat_axis=2, tiled=True)
    count, span, channels = block.shape
    rows = block.reshape(-1, channels).astype(jnp.float32)
    center = jnp.mean(rows, axis=-1, keepdims=True)
    spread = jnp.mean((rows - center) ** 2, axis=-1, keepdims=True)
    normed = ((rows - center) / jnp.sqrt(spread + 1e-05) * ln_gain).astype(jnp.bfloat16)
    hidden = jax.nn.gelu(
        jnp.dot(normed, up_weight, preferred_element_type=jnp.float32), approximate=True
    ).astype(jnp.bfloat16)
    output = (jnp.dot(hidden, down_weight, preferred_element_type=jnp.float32) + rows).astype(
        jnp.bfloat16
    )
    return lax.all_to_all(
        output.reshape(count, span, channels), "chan", split_axis=2, concat_axis=1, tiled=True
    )


def on_device(*arguments):
    grid, basis = arguments[:2]
    cycles, nlon, width = grid.shape
    sides = lax.axis_size("chan")
    fits = (
        sides == 2
        and cycles % 8 == 0
        and cycles % sides == 0
        and cycles // sides >= 6
        and basis.shape[0] // (sides * STEP) == 3
        and basis.shape[0] % (sides * STEP) == 0
        and nlon % 8 == 0
        and width % 128 == 0
    )
    return (fast if fits else plain)(*arguments)


def solution(mesh):
    return jax.shard_map(
        on_device,
        mesh=mesh,
        in_specs=(
            P("lat", None, "chan"),
            P("lat", None, None),
            P(None, None, "chan"),
            P(),
            P(None, "chan"),
            P(),
            P(),
            P(),
            P(),
            P(),
        ),
        out_specs=P("lat", None, "chan"),
        check_vma=False,
    )
```

```python
import functools
import math

import jax
import jax.numpy as jnp
import numpy as np
from jax import lax
from jax.experimental import pallas as pl
from jax.experimental.pallas import tpu as pltpu
from jax.sharding import PartitionSpec as P

MMAX = 384
L = 384
STEP = 4
LANES = 128
NEAR = 1
REACH = 3
BF = jnp.bfloat16
F32 = jnp.float32
SWAP = [(0, 1), (1, 0)]


def cycle_angle(rows, nlat):
    return math.pi * (rows.astype(F32) + 0.5) / nlat


def params(mib):
    return pltpu.CompilerParams(vmem_limit_bytes=mib * 1024 * 1024)


def cost(flops, nbytes):
    return pl.CostEstimate(flops=int(flops), bytes_accessed=int(nbytes), transcendentals=0)


def angle_table(nlon):
    phase = np.arange(nlon)[:, None] * np.arange(MMAX)[None, :] % nlon
    angle = (2.0 * math.pi * phase / nlon).astype(np.float32).astype(np.float64)
    return np.cos(angle), np.sin(angle)


def forward_kernel(scale, table_ref, grid_ref, out_ref, held):
    few = grid_ref.shape[0]
    cycles = out_ref.shape[1]
    rows = table_ref.shape[0]
    step = pl.program_id(0)
    for t in range(few):
        value = jnp.dot(table_ref[...], grid_ref[t], preferred_element_type=F32)
        value = value * scale
        for at in range(held.shape[0]):
            part = value[:, at * LANES : (at + 1) * LANES]
            held[at, pl.ds(step * few + t, rows, stride=cycles), :] = part

    @pl.when(step == pl.num_programs(0) - 1)
    def _():
        for at in range(held.shape[0]):
            lanes = slice(at * LANES, (at + 1) * LANES)
            out_ref[:, :, lanes] = held[at].reshape(rows, cycles, LANES).astype(BF)


def forward_part(grid, table):
    cycles, nlon, width = grid.shape
    rows = table.shape[0]
    few = 4
    return pl.pallas_call(
        functools.partial(forward_kernel, 1.0 / nlon),
        out_shape=jax.ShapeDtypeStruct((rows, cycles, width), BF),
        grid=(cycles // few,),
        in_specs=[
            pl.BlockSpec(table.shape, lambda t: (0, 0)),
            pl.BlockSpec((few, nlon, width), lambda t: (t, 0, 0)),
        ],
        out_specs=pl.BlockSpec((rows, cycles, width), lambda t: (0, 0, 0)),
        scratch_shapes=[pltpu.VMEM((width // LANES, rows * cycles, LANES), F32)],
        compiler_params=params(60),
        cost_estimate=cost(2 * rows * nlon * cycles * width, grid.size * 2),
    )(table, grid)


def middle_kernel(plan, at_ref, spec_ref, basis_ref, quad_ref, own_ref, other_ref, gain_ref, *rest):
    outs, mix_ref, held = (rest[-len(plan) - 2 : -2], rest[-2], rest[-1])
    mode = pl.program_id(0)
    groups, sides, _, _, cycles, width = spec_ref.shape

    @pl.when(mode == 0)
    def _():
        first = at_ref[1] == 0
        channels = sides * width
        own = own_ref[...].astype(F32)
        other = other_ref[...].astype(F32)
        low = jnp.where(first, own, other)
        high = jnp.where(first, other, own)
        whole = jnp.concatenate([low, high], axis=2).astype(BF)
        for at in range(sides):
            block = whole[:, at * width : (at + 1) * width]
            real = pl.ds(2 * at * width, width)
            imag = pl.ds((2 * at + 1) * width, width)
            mix_ref[real, 0:channels] = block[0]
            mix_ref[real, channels : 2 * channels] = block[1]
            mix_ref[imag, 0:channels] = -block[1]
            mix_ref[imag, channels : 2 * channels] = block[0]

    nlat = groups * cycles
    table = basis_ref[0]
    forward = (table * quad_ref[...]).astype(BF)
    pieces = []
    for side in range(sides):
        for part in range(2):
            piece = spec_ref[:, side, 0, part, :, :].astype(F32)
            pieces.append(piece.reshape(nlat, width).astype(BF))
    spec = jnp.concatenate(pieces, axis=1)
    coeff = jnp.dot(forward, spec, preferred_element_type=F32).astype(BF)
    mixed = jnp.dot(coeff, mix_ref[...], preferred_element_type=F32) * gain_ref[...]
    inverse = table.T.astype(BF)
    back = jnp.dot(inverse, mixed.astype(BF), preferred_element_type=F32)
    half = back.shape[1] // 2
    slots = 2 * STEP
    for part in range(2):
        for where in range(STEP):

            @pl.when(mode == where)
            def _():
                row = 2 * where + part
                for at in range(half // LANES):
                    low = part * half + at * LANES
                    held[at, pl.ds(row, nlat, stride=slots), :] = back[:, low : low + LANES]

    @pl.when(mode == STEP - 1)
    def _():
        for at in range(half // LANES):
            whole = held[at].reshape(groups * sides, nlat // (groups * sides), slots, LANES)
            start = 0
            for out, (_, _, count) in zip(outs, plan):
                part = whole[:, start : start + count].astype(BF)
                out[:, 0, :, :, at * LANES : (at + 1) * LANES] = part
                start += count


def middle_part(spec, skip, basis, quad, mix, other, gain, offset, plan, filled):
    groups, sides, _, _, cycles, width = spec.shape
    nlat = groups * cycles
    channels = sides * width
    slots = 2 * STEP
    fixed = lambda m, at: (0, 0)
    specs = [
        pl.BlockSpec((groups, sides, 1, 2, cycles, width), lambda m, at: (0, 0, skip + m, 0, 0, 0)),
        pl.BlockSpec((1, L, nlat), lambda m, at: (at[0] + m, 0, 0)),
        pl.BlockSpec((1, nlat), fixed),
        pl.BlockSpec(mix.shape, lambda m, at: (0, 0, 0)),
        pl.BlockSpec(mix.shape, lambda m, at: (0, 0, 0)),
        pl.BlockSpec((L, 1), fixed),
    ]
    arguments = [spec, basis, quad, mix, other, gain]
    aliases = {}
    for at, value in enumerate(filled):
        if value is not None:
            aliases[1 + len(arguments)] = at
            specs.append(pl.BlockSpec(memory_space=pl.ANY))
            arguments.append(value)
    return pl.pallas_call(
        functools.partial(middle_kernel, plan),
        out_shape=[
            jax.ShapeDtypeStruct((groups * sides, total, count, slots, channels), BF)
            for total, _, count in plan
        ],
        grid_spec=pltpu.PrefetchScalarGridSpec(
            num_scalar_prefetch=1,
            grid=(STEP,),
            in_specs=specs,
            out_specs=[
                pl.BlockSpec(
                    (groups * sides, 1, count, slots, channels),
                    functools.partial(lambda slot, m, at: (0, slot, 0, 0, 0), slot),
                )
                for _, slot, count in plan
            ],
            scratch_shapes=[
                pltpu.VMEM((2 * channels, 2 * channels), BF),
                pltpu.VMEM((channels // LANES, nlat * slots, LANES), F32),
            ],
        ),
        input_output_aliases=aliases,
        compiler_params=params(60),
        cost_estimate=cost(
            2 * STEP * (2 * L * nlat * 2 * channels + L * 4 * channels * channels),
            STEP * (L * nlat * 4 + nlat * channels * 8) + mix.size * 2,
        ),
    )(offset, *arguments)


def local_rows(base_ref, ratio_ref, weight_ref, prev_ref, here_ref, after_ref, edge_ref, tail_ref, out_ref, held):
    t = pl.program_id(0)
    cycle = base_ref[0] + t
    cycles = base_ref[1]
    _, nlon, width = out_ref.shape
    near = weight_ref.shape[0] // 2
    reach = weight_ref.shape[1] // 2
    pad = 8
    block = max(size for size in range(8, 73, 8) if nlon % size == 0)
    wide = block + 2 * pad

    def fill(slot, row):
        held[slot, pl.ds(pad, nlon), :] = row
        held[slot, pl.ds(0, pad), :] = row[nlon - pad :]
        held[slot, pl.ds(pad + nlon, pad), :] = row[:pad]

    @pl.when(t == 0)
    def _():
        fill(0, here_ref[0].astype(F32))

        @pl.when(cycle == 0)
        def _():
            fill(2, edge_ref[0].astype(F32))

        @pl.when(cycle > 0)
        def _():
            fill(2, prev_ref[0].astype(F32))

    after = lax.rem(t + 1, 3)

    @pl.when(cycle < cycles - 1)
    def _():
        fill(after, after_ref[0].astype(F32))

    @pl.when(cycle == cycles - 1)
    def _():
        fill(after, tail_ref[0].astype(F32))

    slots = [lax.rem(t + 2 + a, 3) for a in range(2 * near + 1)]
    for low in range(0, width, LANES):
        lanes = slice(low, low + LANES)
        weights = [
            [weight_ref[a, b : b + 1, lanes] * ratio_ref[cycle, a] for b in range(2 * reach + 1)]
            for a in range(2 * near + 1)
        ]

        def body(at, carry):
            start = pl.multiple_of(at * block, 8)
            rows = [held[slot, pl.ds(start, wide), lanes] for slot in slots]
            total = rows[near][pad : pad + block]
            for b in range(2 * reach + 1):
                value = rows[0] * weights[0][b]
                for a in range(1, 2 * near + 1):
                    value = value + rows[a] * weights[a][b]
                if b != reach:
                    value = pltpu.roll(value, (wide + reach - b) % wide, 0)
                total = total + value[pad : pad + block]
            out_ref[0, pl.ds(start, block), lanes] = total.astype(BF)
            return carry

        lax.fori_loop(0, nlon // block, body, 0)


def local_part(grid, before, after, ratio, weight, base, span):
    cycles, nlon, width = grid.shape
    row = (1, nlon, width)
    edge = lambda t, *_: (0, 0, 0)
    return pl.pallas_call(
        local_rows,
        out_shape=jax.ShapeDtypeStruct((span, nlon, width), BF),
        grid_spec=pltpu.PrefetchScalarGridSpec(
            num_scalar_prefetch=2,
            grid=(span,),
            in_specs=[
                pl.BlockSpec(weight.shape, edge),
                pl.BlockSpec(row, lambda t, at, _: (jnp.maximum(at[0] - 1, 0), 0, 0)),
                pl.BlockSpec(row, lambda t, at, _: (at[0] + t, 0, 0)),
                pl.BlockSpec(row, lambda t, at, _: (jnp.minimum(at[0] + t + 1, cycles - 1), 0, 0)),
                pl.BlockSpec(row, edge),
                pl.BlockSpec(row, edge),
            ],
            out_specs=pl.BlockSpec(row, lambda t, *_: (t, 0, 0)),
            scratch_shapes=[pltpu.VMEM((3, nlon + 16, width), F32)],
        ),
        compiler_params=params(60),
        cost_estimate=cost(span * nlon * width * 400, span * nlon * width * 6),
    )(jnp.stack([base, cycles]).astype(jnp.int32), ratio, weight, grid, grid, grid, before, after)


def exchanged(value, counts):
    got = []
    start = 0
    for count in counts:
        piece = lax.slice_in_dim(value, start, start + count, axis=0)
        got.append(lax.ppermute(piece, "chan", SWAP))
        start += count
    return got


def tail_kernel(pieces, place_ref, own_ref, got_ref, gain_ref, up_ref, down_ref, *rest):
    mine_ref, theirs_ref = rest[-2:]
    first = place_ref[1] == 0
    channels = up_ref.shape[0]
    width = own_ref.shape[2]
    spectral = 0.0
    for back_ref, table_ref in zip(rest[:pieces], rest[pieces : 2 * pieces]):
        back = back_ref[:, :, 0].astype(F32).reshape(table_ref.shape[1], channels).astype(BF)
        spectral += jnp.dot(table_ref[...], back, preferred_element_type=F32)
    own = own_ref[0].astype(F32)
    got = got_ref[0].astype(F32)
    low = jnp.where(first, own, got)
    high = jnp.where(first, got, own)
    local = jnp.concatenate([low, high], axis=1)
    rows = (spectral + local).astype(BF).astype(F32)
    center = jnp.mean(rows, axis=-1, keepdims=True)
    moved = rows - center
    spread = jnp.mean(moved * moved, axis=-1, keepdims=True)
    normed = (moved * lax.rsqrt(spread + 1e-05) * gain_ref[...]).astype(BF)
    hidden = jax.nn.gelu(jnp.dot(normed, up_ref[...], preferred_element_type=F32), approximate=True)
    output = jnp.dot(hidden.astype(BF), down_ref[...], preferred_element_type=F32) + rows
    low = output[:, :width]
    high = output[:, width:]
    mine_ref[0] = jnp.where(first, low, high).astype(BF)
    theirs_ref[0] = jnp.where(first, high, low).astype(BF)


def tail_part(backs, tables, own, got, start, ln_gain, up_weight, down_weight, place, result, cycles):
    count = backs[0].shape[2]
    channels = backs[0].shape[4]
    _, nlon, width = own.shape
    fixed = lambda t, at: (0, 0)
    row = (1, nlon, width)
    specs = [
        pl.BlockSpec(row, lambda t, at: (start + t, 0, 0)),
        pl.BlockSpec(row, lambda t, at: (t, 0, 0)),
        pl.BlockSpec(ln_gain.shape, fixed),
        pl.BlockSpec(up_weight.shape, fixed),
        pl.BlockSpec(down_weight.shape, fixed),
    ]
    for back in backs:
        block = back.shape[:2] + (1,) + back.shape[3:]
        specs.append(pl.BlockSpec(block, lambda t, at: (0, 0, t, 0, 0)))
    specs += [pl.BlockSpec(table.shape, fixed) for table in tables]
    arguments = [own, got, ln_gain, up_weight, down_weight, *backs, *tables]
    aliases = {}
    if result is not None:
        aliases[1 + len(arguments)] = 0
        specs.append(pl.BlockSpec(memory_space=pl.ANY))
        arguments.append(result)
    return pl.pallas_call(
        functools.partial(tail_kernel, len(backs)),
        out_shape=[
            jax.ShapeDtypeStruct((cycles, nlon, width), BF),
            jax.ShapeDtypeStruct((count, nlon, width), BF),
        ],
        grid_spec=pltpu.PrefetchScalarGridSpec(
            num_scalar_prefetch=1,
            grid=(count,),
            in_specs=specs,
            out_specs=[
                pl.BlockSpec(row, lambda t, at: (at[0] + start + t, 0, 0)),
                pl.BlockSpec(row, lambda t, at: (t, 0, 0)),
            ],
        ),
        input_output_aliases=aliases,
        compiler_params=params(60),
        cost_estimate=cost(
            2 * count * nlon * channels * (sum(table.shape[1] for table in tables) + 2 * channels),
            count * nlon * channels * 8,
        ),
    )(place, *arguments)


def fast(grid, basis, mix_weight, spectral_gain, conv_weight, lat_offsets, lon_offsets, ln_gain, up_weight, down_weight):
    cycles, nlon, width = grid.shape
    groups = lax.axis_size("lat")
    sides = lax.axis_size("chan")
    rank = lax.axis_index("lat")
    side = lax.axis_index("chan")
    nlat = cycles * groups
    modes = basis.shape[0]
    few = modes // sides
    parts = few // STEP
    span = cycles // sides
    third = span // 3
    counts = [third - 1, third, third - 1, span - 3 * third + 2]

    cosine, sine = angle_table(nlon)
    both = np.stack([cosine, -sine], axis=-1)
    fwd_table = both.reshape(nlon, groups * sides, few, 2).transpose(1, 2, 3, 0)
    weight_m = np.where(np.arange(MMAX) == 0, 1.0, 2.0)[None, :, None]
    inv_table = (both * weight_m).reshape(nlon, groups * sides, parts, STEP * 2)

    def inverse(low, high):
        return jnp.asarray(inv_table[:, :, low:high].reshape(nlon, -1), BF)


    up = [(i, i + 1) for i in range(groups - 1)]
    down = [(j, i) for i, j in up]
    before = lax.ppermute(grid[-1:], "lat", up)
    after = lax.ppermute(grid[:1], "lat", down)
    own_cycles = rank * cycles + jnp.arange(cycles, dtype=jnp.int32)
    moved = own_cycles[:, None] + jnp.arange(-NEAR, NEAR + 1, dtype=jnp.int32)[None, :]
    ratio = jnp.sin(cycle_angle(moved, nlat)) / jnp.sin(cycle_angle(own_cycles, nlat))[:, None]
    by_lat = lat_offsets[None, :] == jnp.arange(-NEAR, NEAR + 1, dtype=jnp.int32)[:, None]
    by_lon = lon_offsets[None, :] == jnp.arange(-REACH, REACH + 1, dtype=jnp.int32)[:, None]
    hit = (by_lat[:, None, :] & by_lon[None, :, :])[..., None]
    weight = jnp.sum(jnp.where(hit, conv_weight[None, None], 0.0), axis=2)

    other = lax.ppermute(mix_weight, "chan", SWAP)
    gathered = []
    bounds = [(0, few - STEP), (few - STEP, few)]
    for part, (low, high) in enumerate(bounds):
        table = jnp.asarray(fwd_table[:, low:high].reshape(-1, nlon), BF)
        spec = forward_part(grid, table)
        spec = spec.reshape(groups * sides, high - low, 2, cycles, width)
        if part == 0:
            spec, before, after = lax.optimization_barrier((spec, before, after))
            asked = local_part(grid, before, after, ratio, weight, (1 - side) * span, span)
            got = exchanged(asked, counts)
        else:
            own = local_part(grid, before, after, ratio, weight, side * span, span)
            spec, own, other, got[1] = lax.optimization_barrier((spec, own, other, got[1]))
        spec = lax.all_to_all(spec, ("lat", "chan"), 0, 0, tiled=True)
        gathered.append(spec.reshape(groups, sides, high - low, 2, cycles, width))

    theta = cycle_angle(jnp.arange(nlat, dtype=jnp.int32), nlat)
    quad = (math.pi / nlat * jnp.sin(theta))[None, :]
    gain = spectral_gain[:, None]

    filled = [None] * (len(counts) - 1)
    heads = []
    for part in range(parts):
        offset = jnp.stack([side * few + part * STEP, side]).astype(jnp.int32)
        late = part == parts - 1
        plan = [(1, 0, counts[0]) if late else (parts - 1, part, counts[0])]
        plan += [(parts, part, count) for count in counts[1:]]
        head = heads[-1] if heads and not late else None
        ready = middle_part(
            gathered[int(late)], 0 if late else part * STEP, basis, quad, mix_weight, other, gain,
            offset, plan, [head] + filled,
        )
        heads.append(ready[0])
        filled = list(ready[1:])

    def shuffled(value):
        return lax.all_to_all(value, ("lat", "chan"), 0, 0, tiled=True)

    place = jnp.stack([side * span, side]).astype(jnp.int32)

    kept = []

    def finished(at, backs, tables, result):
        result, theirs = tail_part(
            backs, tables, own, got[at], sum(counts[:at]), ln_gain[None, :], up_weight,
            down_weight, place, result, cycles,
        )
        if at == 1:
            cut = max(theirs.shape[0] - 1, 1)
            kept.append(theirs[cut:])
            theirs = theirs[:cut]
        elif at == 2:
            theirs = jnp.concatenate([kept[0], theirs], axis=0)
        return (result, lax.ppermute(theirs, "chan", SWAP))

    begin, end = heads[-2:]
    begin, _, got[2], got[3] = lax.optimization_barrier((begin, gathered[1], got[2], got[3]))
    begin = shuffled(begin)
    end, begin, got[0] = lax.optimization_barrier((end, begin, got[0]))
    end = shuffled(end)
    backs = [[begin, end]]
    tables = [[inverse(0, parts - 1), inverse(parts - 1, parts)]] + [[inverse(0, parts)]] * 3
    last = end
    result = None
    sent = []
    for at, value in enumerate(filled):
        if at == 0:
            value, last = lax.optimization_barrier((value, last))
            backs[0][1] = last
        else:
            value, last = lax.optimization_barrier((value, last))
            backs[-1] = [last]
        if at == 1:
            value, sent[0] = lax.optimization_barrier((value, sent[0]))
        if at > 1:
            value, sent[1] = lax.optimization_barrier((value, sent[1]))
        last = shuffled(value)
        result, value = finished(at, backs[-1], tables[at], result)
        sent.append(value)
        backs.append([last])
    result, value = finished(len(filled), [last], tables[-1], result)
    sent.append(value)
    start = 0
    for value in sent:
        count = value.shape[0]
        result = lax.dynamic_update_slice_in_dim(result, value, (1 - side) * span + start, 0)
        start += count
    return result


def padded_2(value, sides, width):
    for axis, dim in sides:
        size, length = (lax.axis_size(axis), value.shape[dim])
        up = [(i, (i + 1) % size) for i in range(size - 1)]
        down = [(j, i) for i, j in up]
        last = lax.slice_in_dim(value, length - width, length, axis=dim)
        first = lax.slice_in_dim(value, 0, width, axis=dim)
        before = lax.ppermute(last, axis, up)
        after = lax.ppermute(first, axis, down)
        value = jnp.concatenate([before, value, after], axis=dim)
    return value


def complex_mix(real_in, imag_in, real_w, imag_w):
    real_out = jnp.dot(real_in, real_w, preferred_element_type=jnp.float32) - jnp.dot(
        imag_in, imag_w, preferred_element_type=jnp.float32
    )
    imag_out = jnp.dot(real_in, imag_w, preferred_element_type=jnp.float32) + jnp.dot(
        imag_in, real_w, preferred_element_type=jnp.float32
    )
    return (real_out, imag_out)


def plain(
    grid,
    basis,
    mix_weight,
    spectral_gain,
    conv_weight,
    lat_offsets,
    lon_offsets,
    ln_gain,
    up_weight,
    down_weight,
):
    cycles, nlon, width = grid.shape
    groups = lax.axis_size("lat")
    rank = lax.axis_index("lat")
    nlat = cycles * groups
    modes = basis.shape[0]
    points = jnp.arange(nlon, dtype=jnp.int32)
    all_orders = jnp.arange(MMAX, dtype=jnp.int32)
    phase = points[:, None] * all_orders[None, :] % nlon
    angle = 2.0 * math.pi * phase.astype(jnp.float32) / nlon
    fwd_table = (
        jnp.stack([jnp.cos(angle), -jnp.sin(angle)], axis=-1)
        .reshape(nlon, 2 * MMAX)
        .astype(jnp.bfloat16)
    )
    weight_m = jnp.where(all_orders == 0, 1.0, 2.0).astype(jnp.float32)[None, :]
    inv_table = (
        jnp.stack([weight_m * jnp.cos(angle), -weight_m * jnp.sin(angle)], axis=-1)
        .reshape(nlon, 2 * MMAX)
        .T.astype(jnp.bfloat16)
    )
    spec = jnp.einsum("tpc,pk->tkc", grid, fwd_table, preferred_element_type=jnp.float32) * (
        1.0 / nlon
    )
    spec = spec.astype(jnp.bfloat16).reshape(cycles, groups, modes, 2, width)
    gathered = lax.all_to_all(spec, "lat", split_axis=1, concat_axis=0, tiled=True).reshape(
        nlat, modes, 2 * width
    )
    theta = cycle_angle(jnp.arange(nlat, dtype=jnp.int32), nlat)
    quad = math.pi / nlat * jnp.sin(theta)
    fwd_leg = (basis * quad[None, None, :]).astype(jnp.bfloat16)
    inv_leg = basis.astype(jnp.bfloat16)
    coeff = jnp.einsum(
        "jlt,tjk->jlk", fwd_leg, gathered, preferred_element_type=jnp.float32
    ).astype(jnp.bfloat16)
    coeff = coeff.reshape(modes, L, 2, width)
    piece = lax.all_gather(coeff, "chan", axis=3, tiled=True)
    count = piece.shape[3]
    real_w = mix_weight[0]
    imag_w = mix_weight[1]
    real_out, imag_out = complex_mix(
        piece[:, :, 0, :].reshape(-1, count), piece[:, :, 1, :].reshape(-1, count), real_w, imag_w
    )
    summed_modes = jnp.concatenate([real_out, imag_out], axis=1)
    mixed = (summed_modes.reshape(modes, L, 2 * width) * spectral_gain[None, :, None]).astype(
        jnp.bfloat16
    )
    back = jnp.einsum("jlt,jlk->tjk", inv_leg, mixed, preferred_element_type=jnp.float32).astype(
        jnp.bfloat16
    )
    back = lax.all_to_all(
        back.reshape(nlat, 1, modes, 2, width), "lat", split_axis=0, concat_axis=1, tiled=True
    )
    back = back.reshape(cycles, 2 * MMAX, width)
    spectral = jnp.einsum("tkc,kp->tpc", back, inv_table, preferred_element_type=jnp.float32)
    padded = padded_2(grid, (("lat", 0),), 1)
    own_cycles = rank * cycles + jnp.arange(cycles, dtype=jnp.int32)
    here = jnp.sin(cycle_angle(own_cycles, nlat))
    local = jnp.zeros((cycles, nlon, width), jnp.float32)
    for tap in range(conv_weight.shape[0]):
        shift = lat_offsets[tap]
        source = lax.dynamic_slice_in_dim(padded, 1 + shift, cycles, 0)
        source = jnp.roll(source, -lon_offsets[tap], axis=1)
        ratio = (jnp.sin(cycle_angle(own_cycles + shift, nlat)) / here)[:, None, None]
        local = local + conv_weight[tap][None, None, :] * ratio * source.astype(jnp.float32)
    summed = (spectral + local + grid.astype(jnp.float32)).astype(jnp.bfloat16)
    block = lax.all_to_all(summed, "chan", split_axis=1, concat_axis=2, tiled=True)
    count, span, channels = block.shape
    rows = block.reshape(-1, channels).astype(jnp.float32)
    center = jnp.mean(rows, axis=-1, keepdims=True)
    spread = jnp.mean((rows - center) ** 2, axis=-1, keepdims=True)
    normed = ((rows - center) / jnp.sqrt(spread + 1e-05) * ln_gain).astype(jnp.bfloat16)
    hidden = jax.nn.gelu(
        jnp.dot(normed, up_weight, preferred_element_type=jnp.float32), approximate=True
    ).astype(jnp.bfloat16)
    output = (jnp.dot(hidden, down_weight, preferred_element_type=jnp.float32) + rows).astype(
        jnp.bfloat16
    )
    return lax.all_to_all(
        output.reshape(count, span, channels), "chan", split_axis=2, concat_axis=1, tiled=True
    )


def on_device(*arguments):
    grid, basis = arguments[:2]
    cycles, nlon, width = grid.shape
    sides = lax.axis_size("chan")
    fits = (
        sides == 2
        and cycles % 8 == 0
        and cycles % sides == 0
        and cycles // sides >= 6
        and basis.shape[0] // (sides * STEP) >= 2
        and basis.shape[0] % (sides * STEP) == 0
        and nlon % 8 == 0
        and width % 128 == 0
    )
    return (fast if fits else plain)(*arguments)


def solution(mesh):
    return jax.shard_map(
        on_device,
        mesh=mesh,
        in_specs=(
            P("lat", None, "chan"),
            P("lat", None, None),
            P(None, None, "chan"),
            P(),
            P(None, "chan"),
            P(),
            P(),
            P(),
            P(),
            P(),
        ),
        out_specs=P("lat", None, "chan"),
        check_vma=False,
    )
```

```python
import functools
import math

import jax
import jax.numpy as jnp
import numpy as np
from jax import lax
from jax.experimental import pallas as pl
from jax.experimental.pallas import tpu as pltpu
from jax.sharding import PartitionSpec as P

MMAX = 384
L = 384
STEP = 4
LANES = 128
NEAR = 1
REACH = 3
BF = jnp.bfloat16
F32 = jnp.float32
SWAP = [(0, 1), (1, 0)]


def cycle_angle(rows, nlat):
    return math.pi * (rows.astype(F32) + 0.5) / nlat


def params(mib):
    return pltpu.CompilerParams(vmem_limit_bytes=mib * 1024 * 1024)


def cost(flops, nbytes):
    return pl.CostEstimate(flops=int(flops), bytes_accessed=int(nbytes), transcendentals=0)


def angle_table(nlon):
    phase = np.arange(nlon)[:, None] * np.arange(MMAX)[None, :] % nlon
    angle = (2.0 * math.pi * phase / nlon).astype(np.float32).astype(np.float64)
    return np.cos(angle), np.sin(angle)


def forward_kernel(scale, table_ref, grid_ref, out_ref):
    places, blocks, few, slots, width = out_ref.shape
    for t in range(few):
        value = jnp.dot(table_ref[...], grid_ref[t], preferred_element_type=F32) * scale
        out_ref[:, :, t] = value.reshape(places, blocks, slots, width).astype(BF)


def forward_part(grid, table, places):
    cycles, nlon, width = grid.shape
    rows = table.shape[0]
    slots = 2 * STEP
    blocks = rows // places // slots
    few = 4
    return pl.pallas_call(
        functools.partial(forward_kernel, 1.0 / nlon),
        out_shape=jax.ShapeDtypeStruct((places, blocks, cycles, slots, width), BF),
        grid=(cycles // few,),
        in_specs=[
            pl.BlockSpec(table.shape, lambda t: (0, 0)),
            pl.BlockSpec((few, nlon, width), lambda t: (t, 0, 0)),
        ],
        out_specs=pl.BlockSpec((places, blocks, few, slots, width), lambda t: (0, 0, t, 0, 0)),
        compiler_params=params(60),
        cost_estimate=cost(2 * rows * nlon * cycles * width, grid.size * 2),
    )(table, grid)


def middle_kernel(plan, at_ref, spec_ref, basis_ref, quad_ref, own_ref, other_ref, gain_ref, *rest):
    outs, mix_ref, held, loose = (rest[-len(plan) - 3 : -3], *rest[-3:])
    mode = pl.program_id(0)
    groups, sides, _, cycles, slots, width = spec_ref.shape
    lanes = width // LANES

    @pl.when(mode == 0)
    def _():
        for at in range(sides * lanes):
            low = at % lanes * LANES
            piece = spec_ref[:, at // lanes, 0, :, :, low : low + LANES].astype(F32)
            loose[at] = piece.reshape(groups * cycles * slots, LANES)
        first = at_ref[1] == 0
        channels = sides * width
        own = own_ref[...].astype(F32)
        other = other_ref[...].astype(F32)
        low = jnp.where(first, own, other)
        high = jnp.where(first, other, own)
        whole = jnp.concatenate([low, high], axis=2).astype(BF)
        for at in range(sides):
            block = whole[:, at * width : (at + 1) * width]
            real = pl.ds(2 * at * width, width)
            imag = pl.ds((2 * at + 1) * width, width)
            mix_ref[real, 0:channels] = block[0]
            mix_ref[real, channels : 2 * channels] = block[1]
            mix_ref[imag, 0:channels] = -block[1]
            mix_ref[imag, channels : 2 * channels] = block[0]

    nlat = groups * cycles
    table = basis_ref[0]
    forward = (table * quad_ref[...]).astype(BF)
    pieces = []
    for side in range(sides):
        for part in range(2):
            for at in range(side * lanes, (side + 1) * lanes):
                rows = pl.ds(2 * mode + part, nlat, stride=slots)
                pieces.append(loose[at, rows, :].astype(BF))
    spec = jnp.concatenate(pieces, axis=1)
    coeff = jnp.dot(forward, spec, preferred_element_type=F32).astype(BF)
    mixed = jnp.dot(coeff, mix_ref[...], preferred_element_type=F32) * gain_ref[...]
    inverse = table.T.astype(BF)
    back = jnp.dot(inverse, mixed.astype(BF), preferred_element_type=F32)
    half = back.shape[1] // 2
    for part in range(2):
        for where in range(STEP):

            @pl.when(mode == where)
            def _():
                row = 2 * where + part
                for at in range(half // LANES):
                    low = part * half + at * LANES
                    held[at, pl.ds(row, nlat, stride=slots), :] = back[:, low : low + LANES]

    @pl.when(mode == STEP - 1)
    def _():
        for at in range(half // LANES):
            whole = held[at].reshape(groups * sides, nlat // (groups * sides), slots, LANES)
            start = 0
            for out, (_, _, count) in zip(outs, plan):
                part = whole[:, start : start + count].astype(BF)
                out[:, 0, :, :, at * LANES : (at + 1) * LANES] = part
                start += count


def middle_part(spec, skip, basis, quad, mix, other, gain, offset, plan, filled):
    groups, sides, _, cycles, slots, width = spec.shape
    nlat = groups * cycles
    channels = sides * width
    fixed = lambda m, at: (0, 0)
    specs = [
        pl.BlockSpec((groups, sides, 1, cycles, slots, width), lambda m, at: (0, 0, skip, 0, 0, 0)),
        pl.BlockSpec((1, L, nlat), lambda m, at: (at[0] + m, 0, 0)),
        pl.BlockSpec((1, nlat), fixed),
        pl.BlockSpec(mix.shape, lambda m, at: (0, 0, 0)),
        pl.BlockSpec(mix.shape, lambda m, at: (0, 0, 0)),
        pl.BlockSpec((L, 1), fixed),
    ]
    arguments = [spec, basis, quad, mix, other, gain]
    aliases = {}
    for at, value in enumerate(filled):
        if value is not None:
            aliases[1 + len(arguments)] = at
            specs.append(pl.BlockSpec(memory_space=pl.ANY))
            arguments.append(value)
    return pl.pallas_call(
        functools.partial(middle_kernel, plan),
        out_shape=[
            jax.ShapeDtypeStruct((groups * sides, total, count, slots, channels), BF)
            for total, _, count in plan
        ],
        grid_spec=pltpu.PrefetchScalarGridSpec(
            num_scalar_prefetch=1,
            grid=(STEP,),
            in_specs=specs,
            out_specs=[
                pl.BlockSpec(
                    (groups * sides, 1, count, slots, channels),
                    functools.partial(lambda slot, m, at: (0, slot, 0, 0, 0), slot),
                )
                for _, slot, count in plan
            ],
            scratch_shapes=[
                pltpu.VMEM((2 * channels, 2 * channels), BF),
                pltpu.VMEM((channels // LANES, nlat * slots, LANES), F32),
                pltpu.VMEM((channels // LANES, nlat * slots, LANES), F32),
            ],
        ),
        input_output_aliases=aliases,
        compiler_params=params(60),
        cost_estimate=cost(
            2 * STEP * (2 * L * nlat * 2 * channels + L * 4 * channels * channels),
            STEP * (L * nlat * 4 + nlat * channels * 8) + mix.size * 2,
        ),
    )(offset, *arguments)


def local_rows(base_ref, ratio_ref, weight_ref, prev_ref, here_ref, after_ref, edge_ref, tail_ref, out_ref, held):
    t = pl.program_id(0)
    cycle = base_ref[0] + t
    cycles = base_ref[1]
    _, nlon, width = out_ref.shape
    near = weight_ref.shape[0] // 2
    reach = weight_ref.shape[1] // 2
    pad = 8
    block = max(size for size in range(8, 73, 8) if nlon % size == 0)
    wide = block + 2 * pad

    def fill(slot, row):
        held[slot, pl.ds(pad, nlon), :] = row
        held[slot, pl.ds(0, pad), :] = row[nlon - pad :]
        held[slot, pl.ds(pad + nlon, pad), :] = row[:pad]

    @pl.when(t == 0)
    def _():
        fill(0, here_ref[0].astype(F32))

        @pl.when(cycle == 0)
        def _():
            fill(2, edge_ref[0].astype(F32))

        @pl.when(cycle > 0)
        def _():
            fill(2, prev_ref[0].astype(F32))

    after = lax.rem(t + 1, 3)

    @pl.when(cycle < cycles - 1)
    def _():
        fill(after, after_ref[0].astype(F32))

    @pl.when(cycle == cycles - 1)
    def _():
        fill(after, tail_ref[0].astype(F32))

    slots = [lax.rem(t + 2 + a, 3) for a in range(2 * near + 1)]
    for low in range(0, width, LANES):
        lanes = slice(low, low + LANES)
        weights = [
            [weight_ref[a, b : b + 1, lanes] * ratio_ref[cycle, a] for b in range(2 * reach + 1)]
            for a in range(2 * near + 1)
        ]

        def body(at, carry):
            start = pl.multiple_of(at * block, 8)
            rows = [held[slot, pl.ds(start, wide), lanes] for slot in slots]
            total = rows[near][pad : pad + block]
            for b in range(2 * reach + 1):
                value = rows[0] * weights[0][b]
                for a in range(1, 2 * near + 1):
                    value = value + rows[a] * weights[a][b]
                if b != reach:
                    value = pltpu.roll(value, (wide + reach - b) % wide, 0)
                total = total + value[pad : pad + block]
            out_ref[0, pl.ds(start, block), lanes] = total.astype(BF)
            return carry

        lax.fori_loop(0, nlon // block, body, 0)


def local_part(grid, before, after, ratio, weight, base, span):
    cycles, nlon, width = grid.shape
    row = (1, nlon, width)
    edge = lambda t, *_: (0, 0, 0)
    return pl.pallas_call(
        local_rows,
        out_shape=jax.ShapeDtypeStruct((span, nlon, width), BF),
        grid_spec=pltpu.PrefetchScalarGridSpec(
            num_scalar_prefetch=2,
            grid=(span,),
            in_specs=[
                pl.BlockSpec(weight.shape, edge),
                pl.BlockSpec(row, lambda t, at, _: (jnp.maximum(at[0] - 1, 0), 0, 0)),
                pl.BlockSpec(row, lambda t, at, _: (at[0] + t, 0, 0)),
                pl.BlockSpec(row, lambda t, at, _: (jnp.minimum(at[0] + t + 1, cycles - 1), 0, 0)),
                pl.BlockSpec(row, edge),
                pl.BlockSpec(row, edge),
            ],
            out_specs=pl.BlockSpec(row, lambda t, *_: (t, 0, 0)),
            scratch_shapes=[pltpu.VMEM((3, nlon + 16, width), F32)],
        ),
        compiler_params=params(60),
        cost_estimate=cost(span * nlon * width * 400, span * nlon * width * 6),
    )(jnp.stack([base, cycles]).astype(jnp.int32), ratio, weight, grid, grid, grid, before, after)


def exchanged(value, counts):
    got = []
    start = 0
    for count in counts:
        piece = lax.slice_in_dim(value, start, start + count, axis=0)
        got.append(lax.ppermute(piece, "chan", SWAP))
        start += count
    return got


def tail_kernel(pieces, place_ref, own_ref, got_ref, gain_ref, up_ref, down_ref, *rest):
    mine_ref, theirs_ref = rest[-2:]
    first = place_ref[1] == 0
    channels = up_ref.shape[0]
    width = own_ref.shape[2]
    spectral = 0.0
    for back_ref, table_ref in zip(rest[:pieces], rest[pieces : 2 * pieces]):
        back = back_ref[:, :, 0].astype(F32).reshape(table_ref.shape[1], channels).astype(BF)
        spectral += jnp.dot(table_ref[...], back, preferred_element_type=F32)
    own = own_ref[0].astype(F32)
    got = got_ref[0].astype(F32)
    low = jnp.where(first, own, got)
    high = jnp.where(first, got, own)
    local = jnp.concatenate([low, high], axis=1)
    rows = (spectral + local).astype(BF).astype(F32)
    center = jnp.mean(rows, axis=-1, keepdims=True)
    moved = rows - center
    spread = jnp.mean(moved * moved, axis=-1, keepdims=True)
    normed = (moved * lax.rsqrt(spread + 1e-05) * gain_ref[...]).astype(BF)
    hidden = jax.nn.gelu(jnp.dot(normed, up_ref[...], preferred_element_type=F32), approximate=True)
    output = jnp.dot(hidden.astype(BF), down_ref[...], preferred_element_type=F32) + rows
    low = output[:, :width]
    high = output[:, width:]
    mine_ref[0] = jnp.where(first, low, high).astype(BF)
    theirs_ref[0] = jnp.where(first, high, low).astype(BF)


def tail_part(backs, tables, own, got, start, ln_gain, up_weight, down_weight, place, result, cycles):
    count = backs[0].shape[2]
    channels = backs[0].shape[4]
    _, nlon, width = own.shape
    fixed = lambda t, at: (0, 0)
    row = (1, nlon, width)
    specs = [
        pl.BlockSpec(row, lambda t, at: (start + t, 0, 0)),
        pl.BlockSpec(row, lambda t, at: (t, 0, 0)),
        pl.BlockSpec(ln_gain.shape, fixed),
        pl.BlockSpec(up_weight.shape, fixed),
        pl.BlockSpec(down_weight.shape, fixed),
    ]
    for back in backs:
        block = back.shape[:2] + (1,) + back.shape[3:]
        specs.append(pl.BlockSpec(block, lambda t, at: (0, 0, t, 0, 0)))
    specs += [pl.BlockSpec(table.shape, fixed) for table in tables]
    arguments = [own, got, ln_gain, up_weight, down_weight, *backs, *tables]
    aliases = {}
    if result is not None:
        aliases[1 + len(arguments)] = 0
        specs.append(pl.BlockSpec(memory_space=pl.ANY))
        arguments.append(result)
    return pl.pallas_call(
        functools.partial(tail_kernel, len(backs)),
        out_shape=[
            jax.ShapeDtypeStruct((cycles, nlon, width), BF),
            jax.ShapeDtypeStruct((count, nlon, width), BF),
        ],
        grid_spec=pltpu.PrefetchScalarGridSpec(
            num_scalar_prefetch=1,
            grid=(count,),
            in_specs=specs,
            out_specs=[
                pl.BlockSpec(row, lambda t, at: (at[0] + start + t, 0, 0)),
                pl.BlockSpec(row, lambda t, at: (t, 0, 0)),
            ],
        ),
        input_output_aliases=aliases,
        compiler_params=params(60),
        cost_estimate=cost(
            2 * count * nlon * channels * (sum(table.shape[1] for table in tables) + 2 * channels),
            count * nlon * channels * 8,
        ),
    )(place, *arguments)


def fast(grid, basis, mix_weight, spectral_gain, conv_weight, lat_offsets, lon_offsets, ln_gain, up_weight, down_weight):
    cycles, nlon, width = grid.shape
    groups = lax.axis_size("lat")
    sides = lax.axis_size("chan")
    rank = lax.axis_index("lat")
    side = lax.axis_index("chan")
    nlat = cycles * groups
    modes = basis.shape[0]
    few = modes // sides
    parts = few // STEP
    span = cycles // sides
    third = span // 3
    counts = [third - 1, third, third - 1, span - 3 * third + 2]

    cosine, sine = angle_table(nlon)
    both = np.stack([cosine, -sine], axis=-1)
    fwd_table = both.reshape(nlon, groups * sides, few, 2).transpose(1, 2, 3, 0)
    weight_m = np.where(np.arange(MMAX) == 0, 1.0, 2.0)[None, :, None]
    inv_table = (both * weight_m).reshape(nlon, groups * sides, parts, STEP * 2)

    def inverse(low, high):
        return jnp.asarray(inv_table[:, :, low:high].reshape(nlon, -1), BF)


    up = [(i, i + 1) for i in range(groups - 1)]
    down = [(j, i) for i, j in up]
    before = lax.ppermute(grid[-1:], "lat", up)
    after = lax.ppermute(grid[:1], "lat", down)
    own_cycles = rank * cycles + jnp.arange(cycles, dtype=jnp.int32)
    moved = own_cycles[:, None] + jnp.arange(-NEAR, NEAR + 1, dtype=jnp.int32)[None, :]
    ratio = jnp.sin(cycle_angle(moved, nlat)) / jnp.sin(cycle_angle(own_cycles, nlat))[:, None]
    by_lat = lat_offsets[None, :] == jnp.arange(-NEAR, NEAR + 1, dtype=jnp.int32)[:, None]
    by_lon = lon_offsets[None, :] == jnp.arange(-REACH, REACH + 1, dtype=jnp.int32)[:, None]
    hit = (by_lat[:, None, :] & by_lon[None, :, :])[..., None]
    weight = jnp.sum(jnp.where(hit, conv_weight[None, None], 0.0), axis=2)

    other = lax.ppermute(mix_weight, "chan", SWAP)
    gathered = []
    bounds = [(0, few - STEP), (few - STEP, few)]
    for part, (low, high) in enumerate(bounds):
        table = jnp.asarray(fwd_table[:, low:high].reshape(-1, nlon), BF)
        spec = forward_part(grid, table, groups * sides)
        if part == 0:
            spec, before, after, other = lax.optimization_barrier((spec, before, after, other))
            asked = local_part(grid, before, after, ratio, weight, (1 - side) * span, span)
            got = exchanged(asked, counts)
        else:
            own = local_part(grid, before, after, ratio, weight, side * span, span)
            spec, own, got[1], got[3] = lax.optimization_barrier((spec, own, got[1], got[3]))
        spec = lax.all_to_all(spec, ("lat", "chan"), 0, 0, tiled=True)
        gathered.append(spec.reshape((groups, sides) + spec.shape[1:]))

    theta = cycle_angle(jnp.arange(nlat, dtype=jnp.int32), nlat)
    quad = (math.pi / nlat * jnp.sin(theta))[None, :]
    gain = spectral_gain[:, None]

    filled = [None] * (len(counts) - 1)
    heads = []
    for part in range(parts):
        offset = jnp.stack([side * few + part * STEP, side]).astype(jnp.int32)
        late = part == parts - 1
        plan = [(1, 0, counts[0]) if late else (parts - 1, part, counts[0])]
        plan += [(parts, part, count) for count in counts[1:]]
        head = heads[-1] if heads and not late else None
        ready = middle_part(
            gathered[int(late)], 0 if late else part, basis, quad, mix_weight, other, gain,
            offset, plan, [head] + filled,
        )
        heads.append(ready[0])
        filled = list(ready[1:])

    def shuffled(value):
        return lax.all_to_all(value, ("lat", "chan"), 0, 0, tiled=True)

    place = jnp.stack([side * span, side]).astype(jnp.int32)

    kept = []

    def finished(at, backs, tables, result):
        result, theirs = tail_part(
            backs, tables, own, got[at], sum(counts[:at]), ln_gain[None, :], up_weight,
            down_weight, place, result, cycles,
        )
        if at == 1:
            cut = max(theirs.shape[0] - 1, 1)
            kept.append(theirs[cut:])
            theirs = theirs[:cut]
        elif at == 2:
            theirs = jnp.concatenate([kept[0], theirs], axis=0)
        return (result, lax.ppermute(theirs, "chan", SWAP))

    begin, end = heads[-2:]
    begin, _, got[2] = lax.optimization_barrier((begin, gathered[1], got[2]))
    begin = shuffled(begin)
    end, begin, got[0] = lax.optimization_barrier((end, begin, got[0]))
    end = shuffled(end)
    backs = [[begin, end]]
    tables = [[inverse(0, parts - 1), inverse(parts - 1, parts)]] + [[inverse(0, parts)]] * 3
    last = end
    result = None
    sent = []
    for at, value in enumerate(filled):
        if at == 0:
            value, last = lax.optimization_barrier((value, last))
            backs[0][1] = last
        else:
            value, last = lax.optimization_barrier((value, last))
            backs[-1] = [last]
        if at == 1:
            value, sent[0] = lax.optimization_barrier((value, sent[0]))
        if at > 1:
            value, sent[1] = lax.optimization_barrier((value, sent[1]))
        last = shuffled(value)
        result, value = finished(at, backs[-1], tables[at], result)
        sent.append(value)
        backs.append([last])
    result, value = finished(len(filled), [last], tables[-1], result)
    sent.append(value)
    start = 0
    for value in sent:
        count = value.shape[0]
        result = lax.dynamic_update_slice_in_dim(result, value, (1 - side) * span + start, 0)
        start += count
    return result


def padded_2(value, sides, width):
    for axis, dim in sides:
        size, length = (lax.axis_size(axis), value.shape[dim])
        up = [(i, (i + 1) % size) for i in range(size - 1)]
        down = [(j, i) for i, j in up]
        last = lax.slice_in_dim(value, length - width, length, axis=dim)
        first = lax.slice_in_dim(value, 0, width, axis=dim)
        before = lax.ppermute(last, axis, up)
        after = lax.ppermute(first, axis, down)
        value = jnp.concatenate([before, value, after], axis=dim)
    return value


def complex_mix(real_in, imag_in, real_w, imag_w):
    real_out = jnp.dot(real_in, real_w, preferred_element_type=jnp.float32) - jnp.dot(
        imag_in, imag_w, preferred_element_type=jnp.float32
    )
    imag_out = jnp.dot(real_in, imag_w, preferred_element_type=jnp.float32) + jnp.dot(
        imag_in, real_w, preferred_element_type=jnp.float32
    )
    return (real_out, imag_out)


def plain(
    grid,
    basis,
    mix_weight,
    spectral_gain,
    conv_weight,
    lat_offsets,
    lon_offsets,
    ln_gain,
    up_weight,
    down_weight,
):
    cycles, nlon, width = grid.shape
    groups = lax.axis_size("lat")
    rank = lax.axis_index("lat")
    nlat = cycles * groups
    modes = basis.shape[0]
    points = jnp.arange(nlon, dtype=jnp.int32)
    all_orders = jnp.arange(MMAX, dtype=jnp.int32)
    phase = points[:, None] * all_orders[None, :] % nlon
    angle = 2.0 * math.pi * phase.astype(jnp.float32) / nlon
    fwd_table = (
        jnp.stack([jnp.cos(angle), -jnp.sin(angle)], axis=-1)
        .reshape(nlon, 2 * MMAX)
        .astype(jnp.bfloat16)
    )
    weight_m = jnp.where(all_orders == 0, 1.0, 2.0).astype(jnp.float32)[None, :]
    inv_table = (
        jnp.stack([weight_m * jnp.cos(angle), -weight_m * jnp.sin(angle)], axis=-1)
        .reshape(nlon, 2 * MMAX)
        .T.astype(jnp.bfloat16)
    )
    spec = jnp.einsum("tpc,pk->tkc", grid, fwd_table, preferred_element_type=jnp.float32) * (
        1.0 / nlon
    )
    spec = spec.astype(jnp.bfloat16).reshape(cycles, groups, modes, 2, width)
    gathered = lax.all_to_all(spec, "lat", split_axis=1, concat_axis=0, tiled=True).reshape(
        nlat, modes, 2 * width
    )
    theta = cycle_angle(jnp.arange(nlat, dtype=jnp.int32), nlat)
    quad = math.pi / nlat * jnp.sin(theta)
    fwd_leg = (basis * quad[None, None, :]).astype(jnp.bfloat16)
    inv_leg = basis.astype(jnp.bfloat16)
    coeff = jnp.einsum(
        "jlt,tjk->jlk", fwd_leg, gathered, preferred_element_type=jnp.float32
    ).astype(jnp.bfloat16)
    coeff = coeff.reshape(modes, L, 2, width)
    piece = lax.all_gather(coeff, "chan", axis=3, tiled=True)
    count = piece.shape[3]
    real_w = mix_weight[0]
    imag_w = mix_weight[1]
    real_out, imag_out = complex_mix(
        piece[:, :, 0, :].reshape(-1, count), piece[:, :, 1, :].reshape(-1, count), real_w, imag_w
    )
    summed_modes = jnp.concatenate([real_out, imag_out], axis=1)
    mixed = (summed_modes.reshape(modes, L, 2 * width) * spectral_gain[None, :, None]).astype(
        jnp.bfloat16
    )
    back = jnp.einsum("jlt,jlk->tjk", inv_leg, mixed, preferred_element_type=jnp.float32).astype(
        jnp.bfloat16
    )
    back = lax.all_to_all(
        back.reshape(nlat, 1, modes, 2, width), "lat", split_axis=0, concat_axis=1, tiled=True
    )
    back = back.reshape(cycles, 2 * MMAX, width)
    spectral = jnp.einsum("tkc,kp->tpc", back, inv_table, preferred_element_type=jnp.float32)
    padded = padded_2(grid, (("lat", 0),), 1)
    own_cycles = rank * cycles + jnp.arange(cycles, dtype=jnp.int32)
    here = jnp.sin(cycle_angle(own_cycles, nlat))
    local = jnp.zeros((cycles, nlon, width), jnp.float32)
    for tap in range(conv_weight.shape[0]):
        shift = lat_offsets[tap]
        source = lax.dynamic_slice_in_dim(padded, 1 + shift, cycles, 0)
        source = jnp.roll(source, -lon_offsets[tap], axis=1)
        ratio = (jnp.sin(cycle_angle(own_cycles + shift, nlat)) / here)[:, None, None]
        local = local + conv_weight[tap][None, None, :] * ratio * source.astype(jnp.float32)
    summed = (spectral + local + grid.astype(jnp.float32)).astype(jnp.bfloat16)
    block = lax.all_to_all(summed, "chan", split_axis=1, concat_axis=2, tiled=True)
    count, span, channels = block.shape
    rows = block.reshape(-1, channels).astype(jnp.float32)
    center = jnp.mean(rows, axis=-1, keepdims=True)
    spread = jnp.mean((rows - center) ** 2, axis=-1, keepdims=True)
    normed = ((rows - center) / jnp.sqrt(spread + 1e-05) * ln_gain).astype(jnp.bfloat16)
    hidden = jax.nn.gelu(
        jnp.dot(normed, up_weight, preferred_element_type=jnp.float32), approximate=True
    ).astype(jnp.bfloat16)
    output = (jnp.dot(hidden, down_weight, preferred_element_type=jnp.float32) + rows).astype(
        jnp.bfloat16
    )
    return lax.all_to_all(
        output.reshape(count, span, channels), "chan", split_axis=2, concat_axis=1, tiled=True
    )


def on_device(*arguments):
    grid, basis = arguments[:2]
    cycles, nlon, width = grid.shape
    sides = lax.axis_size("chan")
    fits = (
        sides == 2
        and cycles % 8 == 0
        and cycles % sides == 0
        and cycles // sides >= 6
        and basis.shape[0] // (sides * STEP) >= 2
        and basis.shape[0] % (sides * STEP) == 0
        and nlon % 8 == 0
        and width % 128 == 0
    )
    return (fast if fits else plain)(*arguments)


def solution(mesh):
    return jax.shard_map(
        on_device,
        mesh=mesh,
        in_specs=(
            P("lat", None, "chan"),
            P("lat", None, None),
            P(None, None, "chan"),
            P(),
            P(None, "chan"),
            P(),
            P(),
            P(),
            P(),
            P(),
        ),
        out_specs=P("lat", None, "chan"),
        check_vma=False,
    )
```

```python
import functools
import math

import jax
import jax.numpy as jnp
import numpy as np
from jax import lax
from jax.experimental import pallas as pl
from jax.experimental.pallas import tpu as pltpu
from jax.sharding import PartitionSpec as P

MMAX = 384
L = 384
STEP = 4
LANES = 128
NEAR = 1
REACH = 3
BF = jnp.bfloat16
F32 = jnp.float32
SWAP = [(0, 1), (1, 0)]


def cycle_angle(rows, nlat):
    return math.pi * (rows.astype(F32) + 0.5) / nlat


def params(mib):
    return pltpu.CompilerParams(vmem_limit_bytes=mib * 1024 * 1024)


def cost(flops, nbytes):
    return pl.CostEstimate(flops=int(flops), bytes_accessed=int(nbytes), transcendentals=0)


def angle_table(nlon):
    phase = np.arange(nlon)[:, None] * np.arange(MMAX)[None, :] % nlon
    angle = (2.0 * math.pi * phase / nlon).astype(np.float32).astype(np.float64)
    return np.cos(angle), np.sin(angle)


def forward_kernel(scale, table_ref, grid_ref, out_ref):
    places, blocks, few, slots, width = out_ref.shape
    for t in range(few):
        value = jnp.dot(table_ref[...], grid_ref[t], preferred_element_type=F32) * scale
        out_ref[:, :, t] = value.reshape(places, blocks, slots, width).astype(BF)


def forward_part(grid, table, places):
    cycles, nlon, width = grid.shape
    rows = table.shape[0]
    slots = 2 * STEP
    blocks = rows // places // slots
    few = 4
    return pl.pallas_call(
        functools.partial(forward_kernel, 1.0 / nlon),
        out_shape=jax.ShapeDtypeStruct((places, blocks, cycles, slots, width), BF),
        grid=(cycles // few,),
        in_specs=[
            pl.BlockSpec(table.shape, lambda t: (0, 0)),
            pl.BlockSpec((few, nlon, width), lambda t: (t, 0, 0)),
        ],
        out_specs=pl.BlockSpec((places, blocks, few, slots, width), lambda t: (0, 0, t, 0, 0)),
        compiler_params=params(60),
        cost_estimate=cost(2 * rows * nlon * cycles * width, grid.size * 2),
    )(table, grid)


def middle_kernel(plan, at_ref, spec_ref, basis_ref, quad_ref, own_ref, other_ref, gain_ref, *rest):
    outs, mix_ref, held, loose = (rest[-len(plan) - 3 : -3], *rest[-3:])
    mode = pl.program_id(0)
    groups, sides, _, cycles, slots, width = spec_ref.shape
    lanes = width // LANES

    @pl.when(mode == 0)
    def _():
        for at in range(sides * lanes):
            low = at % lanes * LANES
            piece = spec_ref[:, at // lanes, 0, :, :, low : low + LANES].astype(F32)
            loose[at] = piece.reshape(groups * cycles * slots, LANES)
        first = at_ref[1] == 0
        channels = sides * width
        own = own_ref[...].astype(F32)
        other = other_ref[...].astype(F32)
        low = jnp.where(first, own, other)
        high = jnp.where(first, other, own)
        whole = jnp.concatenate([low, high], axis=2).astype(BF)
        for at in range(sides):
            block = whole[:, at * width : (at + 1) * width]
            real = pl.ds(2 * at * width, width)
            imag = pl.ds((2 * at + 1) * width, width)
            mix_ref[real, 0:channels] = block[0]
            mix_ref[real, channels : 2 * channels] = block[1]
            mix_ref[imag, 0:channels] = -block[1]
            mix_ref[imag, channels : 2 * channels] = block[0]

    nlat = groups * cycles
    table = basis_ref[0]
    forward = (table * quad_ref[...]).astype(BF)
    pieces = []
    for side in range(sides):
        for part in range(2):
            for at in range(side * lanes, (side + 1) * lanes):
                rows = pl.ds(2 * mode + part, nlat, stride=slots)
                pieces.append(loose[at, rows, :].astype(BF))
    spec = jnp.concatenate(pieces, axis=1)
    coeff = jnp.dot(forward, spec, preferred_element_type=F32).astype(BF)
    mixed = jnp.dot(coeff, mix_ref[...], preferred_element_type=F32) * gain_ref[...]
    inverse = table.T.astype(BF)
    back = jnp.dot(inverse, mixed.astype(BF), preferred_element_type=F32)
    half = back.shape[1] // 2
    for part in range(2):
        for where in range(STEP):

            @pl.when(mode == where)
            def _():
                row = 2 * where + part
                for at in range(half // LANES):
                    low = part * half + at * LANES
                    held[at, pl.ds(row, nlat, stride=slots), :] = back[:, low : low + LANES]

    @pl.when(mode == STEP - 1)
    def _():
        for at in range(half // LANES):
            whole = held[at].reshape(groups * sides, nlat // (groups * sides), slots, LANES)
            start = 0
            for out, (_, _, count) in zip(outs, plan):
                part = whole[:, start : start + count].astype(BF)
                out[:, 0, :, :, at * LANES : (at + 1) * LANES] = part
                start += count


def middle_part(spec, skip, basis, quad, mix, other, gain, offset, plan, filled):
    groups, sides, _, cycles, slots, width = spec.shape
    nlat = groups * cycles
    channels = sides * width
    fixed = lambda m, at: (0, 0)
    specs = [
        pl.BlockSpec((groups, sides, 1, cycles, slots, width), lambda m, at: (0, 0, skip, 0, 0, 0)),
        pl.BlockSpec((1, L, nlat), lambda m, at: (at[0] + m, 0, 0)),
        pl.BlockSpec((1, nlat), fixed),
        pl.BlockSpec(mix.shape, lambda m, at: (0, 0, 0)),
        pl.BlockSpec(mix.shape, lambda m, at: (0, 0, 0)),
        pl.BlockSpec((L, 1), fixed),
    ]
    arguments = [spec, basis, quad, mix, other, gain]
    aliases = {}
    for at, value in enumerate(filled):
        if value is not None:
            aliases[1 + len(arguments)] = at
            specs.append(pl.BlockSpec(memory_space=pl.ANY))
            arguments.append(value)
    return pl.pallas_call(
        functools.partial(middle_kernel, plan),
        out_shape=[
            jax.ShapeDtypeStruct((groups * sides, total, count, slots, channels), BF)
            for total, _, count in plan
        ],
        grid_spec=pltpu.PrefetchScalarGridSpec(
            num_scalar_prefetch=1,
            grid=(STEP,),
            in_specs=specs,
            out_specs=[
                pl.BlockSpec(
                    (groups * sides, 1, count, slots, channels),
                    functools.partial(lambda slot, m, at: (0, slot, 0, 0, 0), slot),
                )
                for _, slot, count in plan
            ],
            scratch_shapes=[
                pltpu.VMEM((2 * channels, 2 * channels), BF),
                pltpu.VMEM((channels // LANES, nlat * slots, LANES), F32),
                pltpu.VMEM((channels // LANES, nlat * slots, LANES), F32),
            ],
        ),
        input_output_aliases=aliases,
        compiler_params=params(60),
        cost_estimate=cost(
            2 * STEP * (2 * L * nlat * 2 * channels + L * 4 * channels * channels),
            STEP * (L * nlat * 4 + nlat * channels * 8) + mix.size * 2,
        ),
    )(offset, *arguments)


def local_rows(base_ref, ratio_ref, weight_ref, prev_ref, here_ref, after_ref, edge_ref, tail_ref, out_ref, held):
    t = pl.program_id(0)
    cycle = base_ref[0] + t
    cycles = base_ref[1]
    _, nlon, width = out_ref.shape
    near = weight_ref.shape[0] // 2
    reach = weight_ref.shape[1] // 2
    pad = 8
    block = max(size for size in range(8, 73, 8) if nlon % size == 0)
    wide = block + 2 * pad

    def fill(slot, row):
        held[slot, pl.ds(pad, nlon), :] = row
        held[slot, pl.ds(0, pad), :] = row[nlon - pad :]
        held[slot, pl.ds(pad + nlon, pad), :] = row[:pad]

    @pl.when(t == 0)
    def _():
        fill(0, here_ref[0].astype(F32))

        @pl.when(cycle == 0)
        def _():
            fill(2, edge_ref[0].astype(F32))

        @pl.when(cycle > 0)
        def _():
            fill(2, prev_ref[0].astype(F32))

    after = lax.rem(t + 1, 3)

    @pl.when(cycle < cycles - 1)
    def _():
        fill(after, after_ref[0].astype(F32))

    @pl.when(cycle == cycles - 1)
    def _():
        fill(after, tail_ref[0].astype(F32))

    slots = [lax.rem(t + 2 + a, 3) for a in range(2 * near + 1)]
    for low in range(0, width, LANES):
        lanes = slice(low, low + LANES)
        weights = [
            [weight_ref[a, b : b + 1, lanes] * ratio_ref[cycle, a] for b in range(2 * reach + 1)]
            for a in range(2 * near + 1)
        ]

        def body(at, carry):
            start = pl.multiple_of(at * block, 8)
            rows = [held[slot, pl.ds(start, wide), lanes] for slot in slots]
            total = rows[near][pad : pad + block]
            for b in range(2 * reach + 1):
                value = rows[0] * weights[0][b]
                for a in range(1, 2 * near + 1):
                    value = value + rows[a] * weights[a][b]
                if b != reach:
                    value = pltpu.roll(value, (wide + reach - b) % wide, 0)
                total = total + value[pad : pad + block]
            out_ref[0, pl.ds(start, block), lanes] = total.astype(BF)
            return carry

        lax.fori_loop(0, nlon // block, body, 0)


def local_part(grid, before, after, ratio, weight, base, span):
    cycles, nlon, width = grid.shape
    row = (1, nlon, width)
    edge = lambda t, *_: (0, 0, 0)
    return pl.pallas_call(
        local_rows,
        out_shape=jax.ShapeDtypeStruct((span, nlon, width), BF),
        grid_spec=pltpu.PrefetchScalarGridSpec(
            num_scalar_prefetch=2,
            grid=(span,),
            in_specs=[
                pl.BlockSpec(weight.shape, edge),
                pl.BlockSpec(row, lambda t, at, _: (jnp.maximum(at[0] - 1, 0), 0, 0)),
                pl.BlockSpec(row, lambda t, at, _: (at[0] + t, 0, 0)),
                pl.BlockSpec(row, lambda t, at, _: (jnp.minimum(at[0] + t + 1, cycles - 1), 0, 0)),
                pl.BlockSpec(row, edge),
                pl.BlockSpec(row, edge),
            ],
            out_specs=pl.BlockSpec(row, lambda t, *_: (t, 0, 0)),
            scratch_shapes=[pltpu.VMEM((3, nlon + 16, width), F32)],
        ),
        compiler_params=params(60),
        cost_estimate=cost(span * nlon * width * 400, span * nlon * width * 6),
    )(jnp.stack([base, cycles]).astype(jnp.int32), ratio, weight, grid, grid, grid, before, after)


def exchanged(value, counts):
    got = []
    start = 0
    for count in counts:
        piece = lax.slice_in_dim(value, start, start + count, axis=0)
        got.append(lax.ppermute(piece, "chan", SWAP))
        start += count
    return got


def tail_kernel(pieces, place_ref, own_ref, got_ref, gain_ref, up_ref, down_ref, *rest):
    mine_ref, theirs_ref = rest[-2:]
    first = place_ref[1] == 0
    channels = up_ref.shape[0]
    width = own_ref.shape[2]
    spectral = 0.0
    for back_ref, table_ref in zip(rest[:pieces], rest[pieces : 2 * pieces]):
        back = back_ref[:, :, 0].astype(F32).reshape(table_ref.shape[1], channels).astype(BF)
        spectral += jnp.dot(table_ref[...], back, preferred_element_type=F32)
    own = own_ref[0].astype(F32)
    got = got_ref[0].astype(F32)
    low = jnp.where(first, own, got)
    high = jnp.where(first, got, own)
    local = jnp.concatenate([low, high], axis=1)
    rows = (spectral + local).astype(BF).astype(F32)
    center = jnp.mean(rows, axis=-1, keepdims=True)
    moved = rows - center
    spread = jnp.mean(moved * moved, axis=-1, keepdims=True)
    normed = (moved * lax.rsqrt(spread + 1e-05) * gain_ref[...]).astype(BF)
    hidden = jax.nn.gelu(jnp.dot(normed, up_ref[...], preferred_element_type=F32), approximate=True)
    output = jnp.dot(hidden.astype(BF), down_ref[...], preferred_element_type=F32) + rows
    low = output[:, :width]
    high = output[:, width:]
    mine_ref[0] = jnp.where(first, low, high).astype(BF)
    theirs_ref[0] = jnp.where(first, high, low).astype(BF)


def tail_part(backs, tables, own, got, start, ln_gain, up_weight, down_weight, place, result, cycles):
    count = backs[0].shape[2]
    channels = backs[0].shape[4]
    _, nlon, width = own.shape
    fixed = lambda t, at: (0, 0)
    row = (1, nlon, width)
    specs = [
        pl.BlockSpec(row, lambda t, at: (start + t, 0, 0)),
        pl.BlockSpec(row, lambda t, at: (t, 0, 0)),
        pl.BlockSpec(ln_gain.shape, fixed),
        pl.BlockSpec(up_weight.shape, fixed),
        pl.BlockSpec(down_weight.shape, fixed),
    ]
    for back in backs:
        block = back.shape[:2] + (1,) + back.shape[3:]
        specs.append(pl.BlockSpec(block, lambda t, at: (0, 0, t, 0, 0)))
    specs += [pl.BlockSpec(table.shape, fixed) for table in tables]
    arguments = [own, got, ln_gain, up_weight, down_weight, *backs, *tables]
    aliases = {}
    if result is not None:
        aliases[1 + len(arguments)] = 0
        specs.append(pl.BlockSpec(memory_space=pl.ANY))
        arguments.append(result)
    return pl.pallas_call(
        functools.partial(tail_kernel, len(backs)),
        out_shape=[
            jax.ShapeDtypeStruct((cycles, nlon, width), BF),
            jax.ShapeDtypeStruct((count, nlon, width), BF),
        ],
        grid_spec=pltpu.PrefetchScalarGridSpec(
            num_scalar_prefetch=1,
            grid=(count,),
            in_specs=specs,
            out_specs=[
                pl.BlockSpec(row, lambda t, at: (at[0] + start + t, 0, 0)),
                pl.BlockSpec(row, lambda t, at: (t, 0, 0)),
            ],
        ),
        input_output_aliases=aliases,
        compiler_params=params(60),
        cost_estimate=cost(
            2 * count * nlon * channels * (sum(table.shape[1] for table in tables) + 2 * channels),
            count * nlon * channels * 8,
        ),
    )(place, *arguments)


def fast(grid, basis, mix_weight, spectral_gain, conv_weight, lat_offsets, lon_offsets, ln_gain, up_weight, down_weight):
    cycles, nlon, width = grid.shape
    groups = lax.axis_size("lat")
    sides = lax.axis_size("chan")
    rank = lax.axis_index("lat")
    side = lax.axis_index("chan")
    nlat = cycles * groups
    modes = basis.shape[0]
    few = modes // sides
    parts = few // STEP
    span = cycles // sides
    third = span // 3
    counts = [third, third - 1, third - 1, span - 3 * third + 2]

    cosine, sine = angle_table(nlon)
    both = np.stack([cosine, -sine], axis=-1)
    fwd_table = both.reshape(nlon, groups * sides, few, 2).transpose(1, 2, 3, 0)
    weight_m = np.where(np.arange(MMAX) == 0, 1.0, 2.0)[None, :, None]
    inv_table = (both * weight_m).reshape(nlon, groups * sides, parts, STEP * 2)

    def inverse(low, high):
        return jnp.asarray(inv_table[:, :, low:high].reshape(nlon, -1), BF)


    up = [(i, i + 1) for i in range(groups - 1)]
    down = [(j, i) for i, j in up]
    before = lax.ppermute(grid[-1:], "lat", up)
    after = lax.ppermute(grid[:1], "lat", down)
    own_cycles = rank * cycles + jnp.arange(cycles, dtype=jnp.int32)
    moved = own_cycles[:, None] + jnp.arange(-NEAR, NEAR + 1, dtype=jnp.int32)[None, :]
    ratio = jnp.sin(cycle_angle(moved, nlat)) / jnp.sin(cycle_angle(own_cycles, nlat))[:, None]
    by_lat = lat_offsets[None, :] == jnp.arange(-NEAR, NEAR + 1, dtype=jnp.int32)[:, None]
    by_lon = lon_offsets[None, :] == jnp.arange(-REACH, REACH + 1, dtype=jnp.int32)[:, None]
    hit = (by_lat[:, None, :] & by_lon[None, :, :])[..., None]
    weight = jnp.sum(jnp.where(hit, conv_weight[None, None], 0.0), axis=2)

    other = lax.ppermute(mix_weight, "chan", SWAP)
    gathered = []
    bounds = [(0, few - STEP), (few - STEP, few)]
    for part, (low, high) in enumerate(bounds):
        table = jnp.asarray(fwd_table[:, low:high].reshape(-1, nlon), BF)
        spec = forward_part(grid, table, groups * sides)
        if part == 0:
            spec, before, after = lax.optimization_barrier((spec, before, after))
            asked = local_part(grid, before, after, ratio, weight, (1 - side) * span, span)
            got = exchanged(asked, counts)
        else:
            own = local_part(grid, before, after, ratio, weight, side * span, span)
            spec, own, got[0], got[1] = lax.optimization_barrier((spec, own, got[0], got[1]))
        spec = lax.all_to_all(spec, ("lat", "chan"), 0, 0, tiled=True)
        gathered.append(spec.reshape((groups, sides) + spec.shape[1:]))

    theta = cycle_angle(jnp.arange(nlat, dtype=jnp.int32), nlat)
    quad = (math.pi / nlat * jnp.sin(theta))[None, :]
    gain = spectral_gain[:, None]

    filled = [None] * (len(counts) - 1)
    heads = []
    for part in range(parts):
        offset = jnp.stack([side * few + part * STEP, side]).astype(jnp.int32)
        late = part == parts - 1
        plan = [(1, 0, counts[0]) if late else (parts - 1, part, counts[0])]
        plan += [(parts, part, count) for count in counts[1:]]
        head = heads[-1] if heads and not late else None
        ready = middle_part(
            gathered[int(late)], 0 if late else part, basis, quad, mix_weight, other, gain,
            offset, plan, [head] + filled,
        )
        heads.append(ready[0])
        filled = list(ready[1:])

    def shuffled(value):
        return lax.all_to_all(value, ("lat", "chan"), 0, 0, tiled=True)

    place = jnp.stack([side * span, side]).astype(jnp.int32)

    sent = []

    def finished(at, backs, tables, result):
        early = at < 2
        result, theirs = tail_part(
            backs, tables, own, got[at], sum(counts[:at]), ln_gain[None, :], up_weight,
            down_weight, place, result, cycles,
        )
        if sent and at < 3:
            theirs, sent[-1] = lax.optimization_barrier((theirs, sent[-1]))
        cut = max(theirs.shape[0] - 1, 1) if early else theirs.shape[0]
        pieces = [theirs[:cut], theirs[cut:]] if cut < theirs.shape[0] else [theirs]
        sent.extend(lax.ppermute(piece, "chan", SWAP) for piece in pieces)
        return (result, sent[-len(pieces)])

    begin, end = heads[-2:]
    begin, _, got[2] = lax.optimization_barrier((begin, gathered[1], got[2]))
    begin = shuffled(begin)
    end, begin, got[3] = lax.optimization_barrier((end, begin, got[3]))
    end = shuffled(end)
    backs = [[begin, end]]
    tables = [[inverse(0, parts - 1), inverse(parts - 1, parts)]] + [[inverse(0, parts)]] * 3
    last = end
    result = None
    for at, value in enumerate(filled):
        if at == 0:
            value, last = lax.optimization_barrier((value, last))
            backs[0][1] = last
        else:
            value, last = lax.optimization_barrier((value, last))
            backs[-1] = [last]
        if at > 0:
            value, _ = lax.optimization_barrier((value, tied))
        last = shuffled(value)
        result, tied = finished(at, backs[-1], tables[at], result)
        backs.append([last])
    result, _ = finished(len(filled), [last], tables[-1], result)
    start = 0
    for value in sent:
        count = value.shape[0]
        result = lax.dynamic_update_slice_in_dim(result, value, (1 - side) * span + start, 0)
        start += count
    return result


def padded_2(value, sides, width):
    for axis, dim in sides:
        size, length = (lax.axis_size(axis), value.shape[dim])
        up = [(i, (i + 1) % size) for i in range(size - 1)]
        down = [(j, i) for i, j in up]
        last = lax.slice_in_dim(value, length - width, length, axis=dim)
        first = lax.slice_in_dim(value, 0, width, axis=dim)
        before = lax.ppermute(last, axis, up)
        after = lax.ppermute(first, axis, down)
        value = jnp.concatenate([before, value, after], axis=dim)
    return value


def complex_mix(real_in, imag_in, real_w, imag_w):
    real_out = jnp.dot(real_in, real_w, preferred_element_type=jnp.float32) - jnp.dot(
        imag_in, imag_w, preferred_element_type=jnp.float32
    )
    imag_out = jnp.dot(real_in, imag_w, preferred_element_type=jnp.float32) + jnp.dot(
        imag_in, real_w, preferred_element_type=jnp.float32
    )
    return (real_out, imag_out)


def plain(
    grid,
    basis,
    mix_weight,
    spectral_gain,
    conv_weight,
    lat_offsets,
    lon_offsets,
    ln_gain,
    up_weight,
    down_weight,
):
    cycles, nlon, width = grid.shape
    groups = lax.axis_size("lat")
    rank = lax.axis_index("lat")
    nlat = cycles * groups
    modes = basis.shape[0]
    points = jnp.arange(nlon, dtype=jnp.int32)
    all_orders = jnp.arange(MMAX, dtype=jnp.int32)
    phase = points[:, None] * all_orders[None, :] % nlon
    angle = 2.0 * math.pi * phase.astype(jnp.float32) / nlon
    fwd_table = (
        jnp.stack([jnp.cos(angle), -jnp.sin(angle)], axis=-1)
        .reshape(nlon, 2 * MMAX)
        .astype(jnp.bfloat16)
    )
    weight_m = jnp.where(all_orders == 0, 1.0, 2.0).astype(jnp.float32)[None, :]
    inv_table = (
        jnp.stack([weight_m * jnp.cos(angle), -weight_m * jnp.sin(angle)], axis=-1)
        .reshape(nlon, 2 * MMAX)
        .T.astype(jnp.bfloat16)
    )
    spec = jnp.einsum("tpc,pk->tkc", grid, fwd_table, preferred_element_type=jnp.float32) * (
        1.0 / nlon
    )
    spec = spec.astype(jnp.bfloat16).reshape(cycles, groups, modes, 2, width)
    gathered = lax.all_to_all(spec, "lat", split_axis=1, concat_axis=0, tiled=True).reshape(
        nlat, modes, 2 * width
    )
    theta = cycle_angle(jnp.arange(nlat, dtype=jnp.int32), nlat)
    quad = math.pi / nlat * jnp.sin(theta)
    fwd_leg = (basis * quad[None, None, :]).astype(jnp.bfloat16)
    inv_leg = basis.astype(jnp.bfloat16)
    coeff = jnp.einsum(
        "jlt,tjk->jlk", fwd_leg, gathered, preferred_element_type=jnp.float32
    ).astype(jnp.bfloat16)
    coeff = coeff.reshape(modes, L, 2, width)
    piece = lax.all_gather(coeff, "chan", axis=3, tiled=True)
    count = piece.shape[3]
    real_w = mix_weight[0]
    imag_w = mix_weight[1]
    real_out, imag_out = complex_mix(
        piece[:, :, 0, :].reshape(-1, count), piece[:, :, 1, :].reshape(-1, count), real_w, imag_w
    )
    summed_modes = jnp.concatenate([real_out, imag_out], axis=1)
    mixed = (summed_modes.reshape(modes, L, 2 * width) * spectral_gain[None, :, None]).astype(
        jnp.bfloat16
    )
    back = jnp.einsum("jlt,jlk->tjk", inv_leg, mixed, preferred_element_type=jnp.float32).astype(
        jnp.bfloat16
    )
    back = lax.all_to_all(
        back.reshape(nlat, 1, modes, 2, width), "lat", split_axis=0, concat_axis=1, tiled=True
    )
    back = back.reshape(cycles, 2 * MMAX, width)
    spectral = jnp.einsum("tkc,kp->tpc", back, inv_table, preferred_element_type=jnp.float32)
    padded = padded_2(grid, (("lat", 0),), 1)
    own_cycles = rank * cycles + jnp.arange(cycles, dtype=jnp.int32)
    here = jnp.sin(cycle_angle(own_cycles, nlat))
    local = jnp.zeros((cycles, nlon, width), jnp.float32)
    for tap in range(conv_weight.shape[0]):
        shift = lat_offsets[tap]
        source = lax.dynamic_slice_in_dim(padded, 1 + shift, cycles, 0)
        source = jnp.roll(source, -lon_offsets[tap], axis=1)
        ratio = (jnp.sin(cycle_angle(own_cycles + shift, nlat)) / here)[:, None, None]
        local = local + conv_weight[tap][None, None, :] * ratio * source.astype(jnp.float32)
    summed = (spectral + local + grid.astype(jnp.float32)).astype(jnp.bfloat16)
    block = lax.all_to_all(summed, "chan", split_axis=1, concat_axis=2, tiled=True)
    count, span, channels = block.shape
    rows = block.reshape(-1, channels).astype(jnp.float32)
    center = jnp.mean(rows, axis=-1, keepdims=True)
    spread = jnp.mean((rows - center) ** 2, axis=-1, keepdims=True)
    normed = ((rows - center) / jnp.sqrt(spread + 1e-05) * ln_gain).astype(jnp.bfloat16)
    hidden = jax.nn.gelu(
        jnp.dot(normed, up_weight, preferred_element_type=jnp.float32), approximate=True
    ).astype(jnp.bfloat16)
    output = (jnp.dot(hidden, down_weight, preferred_element_type=jnp.float32) + rows).astype(
        jnp.bfloat16
    )
    return lax.all_to_all(
        output.reshape(count, span, channels), "chan", split_axis=2, concat_axis=1, tiled=True
    )


def on_device(*arguments):
    grid, basis = arguments[:2]
    cycles, nlon, width = grid.shape
    sides = lax.axis_size("chan")
    fits = (
        sides == 2
        and cycles % 8 == 0
        and cycles % sides == 0
        and cycles // sides >= 6
        and basis.shape[0] // (sides * STEP) >= 2
        and basis.shape[0] % (sides * STEP) == 0
        and nlon % 8 == 0
        and width % 128 == 0
    )
    return (fast if fits else plain)(*arguments)


def solution(mesh):
    return jax.shard_map(
        on_device,
        mesh=mesh,
        in_specs=(
            P("lat", None, "chan"),
            P("lat", None, None),
            P(None, None, "chan"),
            P(),
            P(None, "chan"),
            P(),
            P(),
            P(),
            P(),
            P(),
        ),
        out_specs=P("lat", None, "chan"),
        check_vma=False,
    )
```

```python
import functools
import math

import jax
import jax.numpy as jnp
import numpy as np
from jax import lax
from jax.experimental import pallas as pl
from jax.experimental.pallas import tpu as pltpu
from jax.sharding import PartitionSpec as P

MMAX = 384
L = 384
STEP = 4
LANES = 128
NEAR = 1
REACH = 3
BF = jnp.bfloat16
F32 = jnp.float32
SWAP = [(0, 1), (1, 0)]


def cycle_angle(rows, nlat):
    return math.pi * (rows.astype(F32) + 0.5) / nlat


def params(mib):
    return pltpu.CompilerParams(vmem_limit_bytes=mib * 1024 * 1024)


def cost(flops, nbytes):
    return pl.CostEstimate(flops=int(flops), bytes_accessed=int(nbytes), transcendentals=0)


def angle_table(nlon):
    phase = np.arange(nlon)[:, None] * np.arange(MMAX)[None, :] % nlon
    angle = (2.0 * math.pi * phase / nlon).astype(np.float32).astype(np.float64)
    return np.cos(angle), np.sin(angle)


def forward_kernel(scale, table_ref, grid_ref, out_ref):
    places, blocks, few, slots, width = out_ref.shape
    for t in range(few):
        value = jnp.dot(table_ref[...], grid_ref[t], preferred_element_type=F32) * scale
        out_ref[:, :, t] = value.reshape(places, blocks, slots, width).astype(BF)


def forward_part(grid, table, places):
    cycles, nlon, width = grid.shape
    rows = table.shape[0]
    slots = 2 * STEP
    blocks = rows // places // slots
    few = 8
    return pl.pallas_call(
        functools.partial(forward_kernel, 1.0 / nlon),
        out_shape=jax.ShapeDtypeStruct((places, blocks, cycles, slots, width), BF),
        grid=(cycles // few,),
        in_specs=[
            pl.BlockSpec(table.shape, lambda t: (0, 0)),
            pl.BlockSpec((few, nlon, width), lambda t: (t, 0, 0)),
        ],
        out_specs=pl.BlockSpec((places, blocks, few, slots, width), lambda t: (0, 0, t, 0, 0)),
        compiler_params=params(60),
        cost_estimate=cost(2 * rows * nlon * cycles * width, grid.size * 2),
    )(table, grid)


def middle_kernel(plan, at_ref, spec_ref, basis_ref, quad_ref, own_ref, other_ref, gain_ref, *rest):
    outs, mix_ref, held, loose = (rest[-len(plan) - 3 : -3], *rest[-3:])
    mode = pl.program_id(0)
    groups, sides, _, cycles, slots, width = spec_ref.shape
    lanes = width // LANES

    @pl.when(mode == 0)
    def _():
        for at in range(sides * lanes):
            low = at % lanes * LANES
            piece = spec_ref[:, at // lanes, 0, :, :, low : low + LANES].astype(F32)
            loose[at] = piece.reshape(groups * cycles * slots, LANES)
        first = at_ref[1] == 0
        channels = sides * width
        own = own_ref[...].astype(F32)
        other = other_ref[...].astype(F32)
        low = jnp.where(first, own, other)
        high = jnp.where(first, other, own)
        whole = jnp.concatenate([low, high], axis=2).astype(BF)
        for at in range(sides):
            block = whole[:, at * width : (at + 1) * width]
            real = pl.ds(2 * at * width, width)
            imag = pl.ds((2 * at + 1) * width, width)
            mix_ref[real, 0:channels] = block[0]
            mix_ref[real, channels : 2 * channels] = block[1]
            mix_ref[imag, 0:channels] = -block[1]
            mix_ref[imag, channels : 2 * channels] = block[0]

    nlat = groups * cycles
    table = basis_ref[0]
    forward = (table * quad_ref[...]).astype(BF)
    pieces = []
    for side in range(sides):
        for part in range(2):
            for at in range(side * lanes, (side + 1) * lanes):
                rows = pl.ds(2 * mode + part, nlat, stride=slots)
                pieces.append(loose[at, rows, :].astype(BF))
    spec = jnp.concatenate(pieces, axis=1)
    coeff = jnp.dot(forward, spec, preferred_element_type=F32).astype(BF)
    mixed = jnp.dot(coeff, mix_ref[...], preferred_element_type=F32) * gain_ref[...]
    inverse = table.T.astype(BF)
    back = jnp.dot(inverse, mixed.astype(BF), preferred_element_type=F32)
    half = back.shape[1] // 2
    for part in range(2):
        for where in range(STEP):

            @pl.when(mode == where)
            def _():
                row = 2 * where + part
                for at in range(half // LANES):
                    low = part * half + at * LANES
                    held[at, pl.ds(row, nlat, stride=slots), :] = back[:, low : low + LANES]

    @pl.when(mode == STEP - 1)
    def _():
        for at in range(half // LANES):
            whole = held[at].reshape(groups * sides, nlat // (groups * sides), slots, LANES)
            start = 0
            for out, (_, _, count) in zip(outs, plan):
                part = whole[:, start : start + count].astype(BF)
                out[:, 0, :, :, at * LANES : (at + 1) * LANES] = part
                start += count


def middle_part(spec, skip, basis, quad, mix, other, gain, offset, plan, filled):
    groups, sides, _, cycles, slots, width = spec.shape
    nlat = groups * cycles
    channels = sides * width
    fixed = lambda m, at: (0, 0)
    specs = [
        pl.BlockSpec((groups, sides, 1, cycles, slots, width), lambda m, at: (0, 0, skip, 0, 0, 0)),
        pl.BlockSpec((1, L, nlat), lambda m, at: (at[0] + m, 0, 0)),
        pl.BlockSpec((1, nlat), fixed),
        pl.BlockSpec(mix.shape, lambda m, at: (0, 0, 0)),
        pl.BlockSpec(mix.shape, lambda m, at: (0, 0, 0)),
        pl.BlockSpec((L, 1), fixed),
    ]
    arguments = [spec, basis, quad, mix, other, gain]
    aliases = {}
    for at, value in enumerate(filled):
        if value is not None:
            aliases[1 + len(arguments)] = at
            specs.append(pl.BlockSpec(memory_space=pl.ANY))
            arguments.append(value)
    return pl.pallas_call(
        functools.partial(middle_kernel, plan),
        out_shape=[
            jax.ShapeDtypeStruct((groups * sides, total, count, slots, channels), BF)
            for total, _, count in plan
        ],
        grid_spec=pltpu.PrefetchScalarGridSpec(
            num_scalar_prefetch=1,
            grid=(STEP,),
            in_specs=specs,
            out_specs=[
                pl.BlockSpec(
                    (groups * sides, 1, count, slots, channels),
                    functools.partial(lambda slot, m, at: (0, slot, 0, 0, 0), slot),
                )
                for _, slot, count in plan
            ],
            scratch_shapes=[
                pltpu.VMEM((2 * channels, 2 * channels), BF),
                pltpu.VMEM((channels // LANES, nlat * slots, LANES), F32),
                pltpu.VMEM((channels // LANES, nlat * slots, LANES), F32),
            ],
        ),
        input_output_aliases=aliases,
        compiler_params=params(60),
        cost_estimate=cost(
            2 * STEP * (2 * L * nlat * 2 * channels + L * 4 * channels * channels),
            STEP * (L * nlat * 4 + nlat * channels * 8) + mix.size * 2,
        ),
    )(offset, *arguments)


def local_rows(base_ref, ratio_ref, weight_ref, prev_ref, here_ref, after_ref, edge_ref, tail_ref, out_ref, held):
    t = pl.program_id(0)
    cycle = base_ref[0] + t
    cycles = base_ref[1]
    _, nlon, width = out_ref.shape
    near = weight_ref.shape[0] // 2
    reach = weight_ref.shape[1] // 2
    pad = 8
    block = max(size for size in range(8, 73, 8) if nlon % size == 0)
    wide = block + 2 * pad

    def fill(slot, row):
        held[slot, pl.ds(pad, nlon), :] = row
        held[slot, pl.ds(0, pad), :] = row[nlon - pad :]
        held[slot, pl.ds(pad + nlon, pad), :] = row[:pad]

    @pl.when(t == 0)
    def _():
        fill(0, here_ref[0].astype(F32))

        @pl.when(cycle == 0)
        def _():
            fill(2, edge_ref[0].astype(F32))

        @pl.when(cycle > 0)
        def _():
            fill(2, prev_ref[0].astype(F32))

    after = lax.rem(t + 1, 3)

    @pl.when(cycle < cycles - 1)
    def _():
        fill(after, after_ref[0].astype(F32))

    @pl.when(cycle == cycles - 1)
    def _():
        fill(after, tail_ref[0].astype(F32))

    slots = [lax.rem(t + 2 + a, 3) for a in range(2 * near + 1)]
    for low in range(0, width, LANES):
        lanes = slice(low, low + LANES)
        weights = [
            [weight_ref[a, b : b + 1, lanes] * ratio_ref[cycle, a] for b in range(2 * reach + 1)]
            for a in range(2 * near + 1)
        ]

        def body(at, carry):
            start = pl.multiple_of(at * block, 8)
            rows = [held[slot, pl.ds(start, wide), lanes] for slot in slots]
            total = rows[near][pad : pad + block]
            for b in range(2 * reach + 1):
                value = rows[0] * weights[0][b]
                for a in range(1, 2 * near + 1):
                    value = value + rows[a] * weights[a][b]
                if b != reach:
                    value = pltpu.roll(value, (wide + reach - b) % wide, 0)
                total = total + value[pad : pad + block]
            out_ref[0, pl.ds(start, block), lanes] = total.astype(BF)
            return carry

        lax.fori_loop(0, nlon // block, body, 0)


def local_part(grid, before, after, ratio, weight, base, span):
    cycles, nlon, width = grid.shape
    row = (1, nlon, width)
    edge = lambda t, *_: (0, 0, 0)
    return pl.pallas_call(
        local_rows,
        out_shape=jax.ShapeDtypeStruct((span, nlon, width), BF),
        grid_spec=pltpu.PrefetchScalarGridSpec(
            num_scalar_prefetch=2,
            grid=(span,),
            in_specs=[
                pl.BlockSpec(weight.shape, edge),
                pl.BlockSpec(row, lambda t, at, _: (jnp.maximum(at[0] - 1, 0), 0, 0)),
                pl.BlockSpec(row, lambda t, at, _: (at[0] + t, 0, 0)),
                pl.BlockSpec(row, lambda t, at, _: (jnp.minimum(at[0] + t + 1, cycles - 1), 0, 0)),
                pl.BlockSpec(row, edge),
                pl.BlockSpec(row, edge),
            ],
            out_specs=pl.BlockSpec(row, lambda t, *_: (t, 0, 0)),
            scratch_shapes=[pltpu.VMEM((3, nlon + 16, width), F32)],
        ),
        compiler_params=params(60),
        cost_estimate=cost(span * nlon * width * 400, span * nlon * width * 6),
    )(jnp.stack([base, cycles]).astype(jnp.int32), ratio, weight, grid, grid, grid, before, after)


def exchanged(value, counts):
    got = []
    start = 0
    for count in counts:
        piece = lax.slice_in_dim(value, start, start + count, axis=0)
        got.append(lax.ppermute(piece, "chan", SWAP))
        start += count
    return got


def tail_kernel(pieces, place_ref, own_ref, got_ref, gain_ref, up_ref, down_ref, *rest):
    mine_ref, theirs_ref = rest[-2:]
    first = place_ref[1] == 0
    channels = up_ref.shape[0]
    width = own_ref.shape[2]
    spectral = 0.0
    for back_ref, table_ref in zip(rest[:pieces], rest[pieces : 2 * pieces]):
        back = back_ref[:, :, 0].astype(F32).reshape(table_ref.shape[1], channels).astype(BF)
        spectral += jnp.dot(table_ref[...], back, preferred_element_type=F32)
    own = own_ref[0].astype(F32)
    got = got_ref[0].astype(F32)
    low = jnp.where(first, own, got)
    high = jnp.where(first, got, own)
    local = jnp.concatenate([low, high], axis=1)
    rows = (spectral + local).astype(BF).astype(F32)
    center = jnp.mean(rows, axis=-1, keepdims=True)
    moved = rows - center
    spread = jnp.mean(moved * moved, axis=-1, keepdims=True)
    normed = (moved * lax.rsqrt(spread + 1e-05) * gain_ref[...]).astype(BF)
    hidden = jax.nn.gelu(jnp.dot(normed, up_ref[...], preferred_element_type=F32), approximate=True)
    output = jnp.dot(hidden.astype(BF), down_ref[...], preferred_element_type=F32) + rows
    low = output[:, :width]
    high = output[:, width:]
    mine_ref[0] = jnp.where(first, low, high).astype(BF)
    theirs_ref[0] = jnp.where(first, high, low).astype(BF)


def tail_part(backs, tables, own, got, start, low, count, ln_gain, up_weight, down_weight, place, result, cycles):
    channels = backs[0].shape[4]
    _, nlon, width = own.shape
    fixed = lambda t, at: (0, 0)
    row = (1, nlon, width)
    specs = [
        pl.BlockSpec(row, lambda t, at: (start + low + t, 0, 0)),
        pl.BlockSpec(row, lambda t, at: (low + t, 0, 0)),
        pl.BlockSpec(ln_gain.shape, fixed),
        pl.BlockSpec(up_weight.shape, fixed),
        pl.BlockSpec(down_weight.shape, fixed),
    ]
    for back in backs:
        block = back.shape[:2] + (1,) + back.shape[3:]
        specs.append(pl.BlockSpec(block, lambda t, at: (0, 0, low + t, 0, 0)))
    specs += [pl.BlockSpec(table.shape, fixed) for table in tables]
    arguments = [own, got, ln_gain, up_weight, down_weight, *backs, *tables]
    aliases = {}
    if result is not None:
        aliases[1 + len(arguments)] = 0
        specs.append(pl.BlockSpec(memory_space=pl.ANY))
        arguments.append(result)
    return pl.pallas_call(
        functools.partial(tail_kernel, len(backs)),
        out_shape=[
            jax.ShapeDtypeStruct((cycles, nlon, width), BF),
            jax.ShapeDtypeStruct((count, nlon, width), BF),
        ],
        grid_spec=pltpu.PrefetchScalarGridSpec(
            num_scalar_prefetch=1,
            grid=(count,),
            in_specs=specs,
            out_specs=[
                pl.BlockSpec(row, lambda t, at: (at[0] + start + low + t, 0, 0)),
                pl.BlockSpec(row, lambda t, at: (t, 0, 0)),
            ],
        ),
        input_output_aliases=aliases,
        compiler_params=params(60),
        cost_estimate=cost(
            2 * count * nlon * channels * (sum(table.shape[1] for table in tables) + 2 * channels),
            count * nlon * channels * 8,
        ),
    )(place, *arguments)


def fast(grid, basis, mix_weight, spectral_gain, conv_weight, lat_offsets, lon_offsets, ln_gain, up_weight, down_weight):
    cycles, nlon, width = grid.shape
    groups = lax.axis_size("lat")
    sides = lax.axis_size("chan")
    rank = lax.axis_index("lat")
    side = lax.axis_index("chan")
    nlat = cycles * groups
    modes = basis.shape[0]
    few = modes // sides
    parts = few // STEP
    span = cycles // sides
    third = span // 3
    counts = [third, third - 1, third - 1, span - 3 * third + 2]

    cosine, sine = angle_table(nlon)
    both = np.stack([cosine, -sine], axis=-1)
    fwd_table = both.reshape(nlon, groups * sides, few, 2).transpose(1, 2, 3, 0)
    weight_m = np.where(np.arange(MMAX) == 0, 1.0, 2.0)[None, :, None]
    inv_table = (both * weight_m).reshape(nlon, groups * sides, parts, STEP * 2)

    def inverse(low, high):
        return jnp.asarray(inv_table[:, :, low:high].reshape(nlon, -1), BF)


    up = [(i, i + 1) for i in range(groups - 1)]
    down = [(j, i) for i, j in up]
    before = lax.ppermute(grid[-1:], "lat", up)
    after = lax.ppermute(grid[:1], "lat", down)
    own_cycles = rank * cycles + jnp.arange(cycles, dtype=jnp.int32)
    moved = own_cycles[:, None] + jnp.arange(-NEAR, NEAR + 1, dtype=jnp.int32)[None, :]
    ratio = jnp.sin(cycle_angle(moved, nlat)) / jnp.sin(cycle_angle(own_cycles, nlat))[:, None]
    by_lat = lat_offsets[None, :] == jnp.arange(-NEAR, NEAR + 1, dtype=jnp.int32)[:, None]
    by_lon = lon_offsets[None, :] == jnp.arange(-REACH, REACH + 1, dtype=jnp.int32)[:, None]
    hit = (by_lat[:, None, :] & by_lon[None, :, :])[..., None]
    weight = jnp.sum(jnp.where(hit, conv_weight[None, None], 0.0), axis=2)

    other = lax.ppermute(mix_weight, "chan", SWAP)
    gathered = []
    bounds = [(0, few - STEP), (few - STEP, few)]
    for part, (low, high) in enumerate(bounds):
        table = jnp.asarray(fwd_table[:, low:high].reshape(-1, nlon), BF)
        spec = forward_part(grid, table, groups * sides)
        if part == 0:
            spec, before, after = lax.optimization_barrier((spec, before, after))
            asked = local_part(grid, before, after, ratio, weight, (1 - side) * span, span)
            got = exchanged(asked, counts)
        else:
            own = local_part(grid, before, after, ratio, weight, side * span, span)
            spec, own, got[0], got[1] = lax.optimization_barrier((spec, own, got[0], got[1]))
        spec = lax.all_to_all(spec, ("lat", "chan"), 0, 0, tiled=True)
        gathered.append(spec.reshape((groups, sides) + spec.shape[1:]))

    theta = cycle_angle(jnp.arange(nlat, dtype=jnp.int32), nlat)
    quad = (math.pi / nlat * jnp.sin(theta))[None, :]
    gain = spectral_gain[:, None]

    filled = [None] * (len(counts) - 1)
    heads = []
    for part in range(parts):
        offset = jnp.stack([side * few + part * STEP, side]).astype(jnp.int32)
        late = part == parts - 1
        plan = [(1, 0, counts[0]) if late else (parts - 1, part, counts[0])]
        plan += [(parts, part, count) for count in counts[1:]]
        head = heads[-1] if heads and not late else None
        ready = middle_part(
            gathered[int(late)], 0 if late else part, basis, quad, mix_weight, other, gain,
            offset, plan, [head] + filled,
        )
        heads.append(ready[0])
        filled = list(ready[1:])

    def shuffled(value):
        return lax.all_to_all(value, ("lat", "chan"), 0, 0, tiled=True)

    place = jnp.stack([side * span, side]).astype(jnp.int32)

    sent = []

    def finished(at, backs, tables, result):
        pieces = [counts[at]]
        low = 0
        needed = []
        for count in pieces:
            result, theirs = tail_part(
                backs, tables, own, got[at], sum(counts[:at]), low, count, ln_gain[None, :],
                up_weight, down_weight, place, result, cycles,
            )
            sent.append(lax.ppermute(theirs, "chan", SWAP))
            needed.append(theirs if low else sent[-1])
            low += count
        return (result, needed)

    begin, end = heads[-2:]
    begin, _, got[2] = lax.optimization_barrier((begin, gathered[1], got[2]))
    begin = shuffled(begin)
    end, begin, got[3] = lax.optimization_barrier((end, begin, got[3]))
    end = shuffled(end)
    backs = [[begin, end]]
    tables = [[inverse(0, parts - 1), inverse(parts - 1, parts)]] + [[inverse(0, parts)]] * 3
    last = end
    result = None
    for at, value in enumerate(filled):
        if at == 0:
            value, last = lax.optimization_barrier((value, last))
            backs[0][1] = last
        else:
            value, last = lax.optimization_barrier((value, last))
            backs[-1] = [last]
        if at > 0:
            value, *_ = lax.optimization_barrier((value, *tied))
        last = shuffled(value)
        result, tied = finished(at, backs[-1], tables[at], result)
        backs.append([last])
    result, _ = finished(len(filled), [last], tables[-1], result)
    start = 0
    for value in sent:
        count = value.shape[0]
        result = lax.dynamic_update_slice_in_dim(result, value, (1 - side) * span + start, 0)
        start += count
    return result


def padded_2(value, sides, width):
    for axis, dim in sides:
        size, length = (lax.axis_size(axis), value.shape[dim])
        up = [(i, (i + 1) % size) for i in range(size - 1)]
        down = [(j, i) for i, j in up]
        last = lax.slice_in_dim(value, length - width, length, axis=dim)
        first = lax.slice_in_dim(value, 0, width, axis=dim)
        before = lax.ppermute(last, axis, up)
        after = lax.ppermute(first, axis, down)
        value = jnp.concatenate([before, value, after], axis=dim)
    return value


def complex_mix(real_in, imag_in, real_w, imag_w):
    real_out = jnp.dot(real_in, real_w, preferred_element_type=jnp.float32) - jnp.dot(
        imag_in, imag_w, preferred_element_type=jnp.float32
    )
    imag_out = jnp.dot(real_in, imag_w, preferred_element_type=jnp.float32) + jnp.dot(
        imag_in, real_w, preferred_element_type=jnp.float32
    )
    return (real_out, imag_out)


def plain(
    grid,
    basis,
    mix_weight,
    spectral_gain,
    conv_weight,
    lat_offsets,
    lon_offsets,
    ln_gain,
    up_weight,
    down_weight,
):
    cycles, nlon, width = grid.shape
    groups = lax.axis_size("lat")
    rank = lax.axis_index("lat")
    nlat = cycles * groups
    modes = basis.shape[0]
    points = jnp.arange(nlon, dtype=jnp.int32)
    all_orders = jnp.arange(MMAX, dtype=jnp.int32)
    phase = points[:, None] * all_orders[None, :] % nlon
    angle = 2.0 * math.pi * phase.astype(jnp.float32) / nlon
    fwd_table = (
        jnp.stack([jnp.cos(angle), -jnp.sin(angle)], axis=-1)
        .reshape(nlon, 2 * MMAX)
        .astype(jnp.bfloat16)
    )
    weight_m = jnp.where(all_orders == 0, 1.0, 2.0).astype(jnp.float32)[None, :]
    inv_table = (
        jnp.stack([weight_m * jnp.cos(angle), -weight_m * jnp.sin(angle)], axis=-1)
        .reshape(nlon, 2 * MMAX)
        .T.astype(jnp.bfloat16)
    )
    spec = jnp.einsum("tpc,pk->tkc", grid, fwd_table, preferred_element_type=jnp.float32) * (
        1.0 / nlon
    )
    spec = spec.astype(jnp.bfloat16).reshape(cycles, groups, modes, 2, width)
    gathered = lax.all_to_all(spec, "lat", split_axis=1, concat_axis=0, tiled=True).reshape(
        nlat, modes, 2 * width
    )
    theta = cycle_angle(jnp.arange(nlat, dtype=jnp.int32), nlat)
    quad = math.pi / nlat * jnp.sin(theta)
    fwd_leg = (basis * quad[None, None, :]).astype(jnp.bfloat16)
    inv_leg = basis.astype(jnp.bfloat16)
    coeff = jnp.einsum(
        "jlt,tjk->jlk", fwd_leg, gathered, preferred_element_type=jnp.float32
    ).astype(jnp.bfloat16)
    coeff = coeff.reshape(modes, L, 2, width)
    piece = lax.all_gather(coeff, "chan", axis=3, tiled=True)
    count = piece.shape[3]
    real_w = mix_weight[0]
    imag_w = mix_weight[1]
    real_out, imag_out = complex_mix(
        piece[:, :, 0, :].reshape(-1, count), piece[:, :, 1, :].reshape(-1, count), real_w, imag_w
    )
    summed_modes = jnp.concatenate([real_out, imag_out], axis=1)
    mixed = (summed_modes.reshape(modes, L, 2 * width) * spectral_gain[None, :, None]).astype(
        jnp.bfloat16
    )
    back = jnp.einsum("jlt,jlk->tjk", inv_leg, mixed, preferred_element_type=jnp.float32).astype(
        jnp.bfloat16
    )
    back = lax.all_to_all(
        back.reshape(nlat, 1, modes, 2, width), "lat", split_axis=0, concat_axis=1, tiled=True
    )
    back = back.reshape(cycles, 2 * MMAX, width)
    spectral = jnp.einsum("tkc,kp->tpc", back, inv_table, preferred_element_type=jnp.float32)
    padded = padded_2(grid, (("lat", 0),), 1)
    own_cycles = rank * cycles + jnp.arange(cycles, dtype=jnp.int32)
    here = jnp.sin(cycle_angle(own_cycles, nlat))
    local = jnp.zeros((cycles, nlon, width), jnp.float32)
    for tap in range(conv_weight.shape[0]):
        shift = lat_offsets[tap]
        source = lax.dynamic_slice_in_dim(padded, 1 + shift, cycles, 0)
        source = jnp.roll(source, -lon_offsets[tap], axis=1)
        ratio = (jnp.sin(cycle_angle(own_cycles + shift, nlat)) / here)[:, None, None]
        local = local + conv_weight[tap][None, None, :] * ratio * source.astype(jnp.float32)
    summed = (spectral + local + grid.astype(jnp.float32)).astype(jnp.bfloat16)
    block = lax.all_to_all(summed, "chan", split_axis=1, concat_axis=2, tiled=True)
    count, span, channels = block.shape
    rows = block.reshape(-1, channels).astype(jnp.float32)
    center = jnp.mean(rows, axis=-1, keepdims=True)
    spread = jnp.mean((rows - center) ** 2, axis=-1, keepdims=True)
    normed = ((rows - center) / jnp.sqrt(spread + 1e-05) * ln_gain).astype(jnp.bfloat16)
    hidden = jax.nn.gelu(
        jnp.dot(normed, up_weight, preferred_element_type=jnp.float32), approximate=True
    ).astype(jnp.bfloat16)
    output = (jnp.dot(hidden, down_weight, preferred_element_type=jnp.float32) + rows).astype(
        jnp.bfloat16
    )
    return lax.all_to_all(
        output.reshape(count, span, channels), "chan", split_axis=2, concat_axis=1, tiled=True
    )


def on_device(*arguments):
    grid, basis = arguments[:2]
    cycles, nlon, width = grid.shape
    sides = lax.axis_size("chan")
    fits = (
        sides == 2
        and cycles % 8 == 0
        and cycles % sides == 0
        and cycles // sides >= 6
        and basis.shape[0] // (sides * STEP) >= 2
        and basis.shape[0] % (sides * STEP) == 0
        and nlon % 8 == 0
        and width % 128 == 0
    )
    return (fast if fits else plain)(*arguments)


def solution(mesh):
    return jax.shard_map(
        on_device,
        mesh=mesh,
        in_specs=(
            P("lat", None, "chan"),
            P("lat", None, None),
            P(None, None, "chan"),
            P(),
            P(None, "chan"),
            P(),
            P(),
            P(),
            P(),
            P(),
        ),
        out_specs=P("lat", None, "chan"),
        check_vma=False,
    )
```

```python
import functools
import math

import jax
import jax.numpy as jnp
import numpy as np
from jax import lax
from jax.experimental import pallas as pl
from jax.experimental.pallas import tpu as pltpu
from jax.sharding import PartitionSpec as P

MMAX = 384
L = 384
STEP = 4
LANES = 128
NEAR = 1
REACH = 3
BF = jnp.bfloat16
F32 = jnp.float32
SWAP = [(0, 1), (1, 0)]


def cycle_angle(rows, nlat):
    return math.pi * (rows.astype(F32) + 0.5) / nlat


def params(mib):
    return pltpu.CompilerParams(vmem_limit_bytes=mib * 1024 * 1024)


def cost(flops, nbytes):
    return pl.CostEstimate(flops=int(flops), bytes_accessed=int(nbytes), transcendentals=0)


def angle_table(nlon):
    phase = np.arange(nlon)[:, None] * np.arange(MMAX)[None, :] % nlon
    angle = (2.0 * math.pi * phase / nlon).astype(np.float32).astype(np.float64)
    return np.cos(angle), np.sin(angle)


def forward_kernel(scale, table_ref, grid_ref, out_ref):
    places, blocks, few, slots, width = out_ref.shape
    for t in range(few):
        value = jnp.dot(table_ref[...], grid_ref[t], preferred_element_type=F32) * scale
        out_ref[:, :, t] = value.reshape(places, blocks, slots, width).astype(BF)


def forward_part(grid, table, places):
    cycles, nlon, width = grid.shape
    rows = table.shape[0]
    slots = 2 * STEP
    blocks = rows // places // slots
    few = 8
    return pl.pallas_call(
        functools.partial(forward_kernel, 1.0 / nlon),
        out_shape=jax.ShapeDtypeStruct((places, blocks, cycles, slots, width), BF),
        grid=(cycles // few,),
        in_specs=[
            pl.BlockSpec(table.shape, lambda t: (0, 0)),
            pl.BlockSpec((few, nlon, width), lambda t: (t, 0, 0)),
        ],
        out_specs=pl.BlockSpec((places, blocks, few, slots, width), lambda t: (0, 0, t, 0, 0)),
        compiler_params=params(60),
        cost_estimate=cost(2 * rows * nlon * cycles * width, grid.size * 2),
    )(table, grid)


def middle_kernel(plan, at_ref, spec_ref, basis_ref, quad_ref, own_ref, other_ref, gain_ref, *rest):
    outs, mix_ref, held, loose = (rest[-len(plan) - 3 : -3], *rest[-3:])
    mode = pl.program_id(0)
    groups, sides, _, cycles, slots, width = spec_ref.shape
    lanes = width // LANES

    @pl.when(mode == 0)
    def _():
        for at in range(sides * lanes):
            low = at % lanes * LANES
            piece = spec_ref[:, at // lanes, 0, :, :, low : low + LANES].astype(F32)
            loose[at] = piece.reshape(groups * cycles * slots, LANES)
        first = at_ref[1] == 0
        channels = sides * width
        own = own_ref[...].astype(F32)
        other = other_ref[...].astype(F32)
        low = jnp.where(first, own, other)
        high = jnp.where(first, other, own)
        whole = jnp.concatenate([low, high], axis=2).astype(BF)
        for at in range(sides):
            block = whole[:, at * width : (at + 1) * width]
            real = pl.ds(2 * at * width, width)
            imag = pl.ds((2 * at + 1) * width, width)
            mix_ref[real, 0:channels] = block[0]
            mix_ref[real, channels : 2 * channels] = block[1]
            mix_ref[imag, 0:channels] = -block[1]
            mix_ref[imag, channels : 2 * channels] = block[0]

    nlat = groups * cycles
    table = basis_ref[0]
    forward = (table * quad_ref[...]).astype(BF)
    pieces = []
    for side in range(sides):
        for part in range(2):
            for at in range(side * lanes, (side + 1) * lanes):
                rows = pl.ds(2 * mode + part, nlat, stride=slots)
                pieces.append(loose[at, rows, :].astype(BF))
    spec = jnp.concatenate(pieces, axis=1)
    coeff = jnp.dot(forward, spec, preferred_element_type=F32).astype(BF)
    mixed = jnp.dot(coeff, mix_ref[...], preferred_element_type=F32) * gain_ref[...]
    inverse = table.T.astype(BF)
    back = jnp.dot(inverse, mixed.astype(BF), preferred_element_type=F32)
    half = back.shape[1] // 2
    for part in range(2):
        for where in range(STEP):

            @pl.when(mode == where)
            def _():
                row = 2 * where + part
                for at in range(half // LANES):
                    low = part * half + at * LANES
                    held[at, pl.ds(row, nlat, stride=slots), :] = back[:, low : low + LANES]

    @pl.when(mode == STEP - 1)
    def _():
        for at in range(half // LANES):
            whole = held[at].reshape(groups * sides, nlat // (groups * sides), slots, LANES)
            start = 0
            for out, (_, _, count) in zip(outs, plan):
                part = whole[:, start : start + count].astype(BF)
                out[:, 0, :, :, at * LANES : (at + 1) * LANES] = part
                start += count


def middle_part(spec, skip, basis, quad, mix, other, gain, offset, plan, filled):
    groups, sides, _, cycles, slots, width = spec.shape
    nlat = groups * cycles
    channels = sides * width
    fixed = lambda m, at: (0, 0)
    specs = [
        pl.BlockSpec((groups, sides, 1, cycles, slots, width), lambda m, at: (0, 0, skip, 0, 0, 0)),
        pl.BlockSpec((1, L, nlat), lambda m, at: (at[0] + m, 0, 0)),
        pl.BlockSpec((1, nlat), fixed),
        pl.BlockSpec(mix.shape, lambda m, at: (0, 0, 0)),
        pl.BlockSpec(mix.shape, lambda m, at: (0, 0, 0)),
        pl.BlockSpec((L, 1), fixed),
    ]
    arguments = [spec, basis, quad, mix, other, gain]
    aliases = {}
    for at, value in enumerate(filled):
        if value is not None:
            aliases[1 + len(arguments)] = at
            specs.append(pl.BlockSpec(memory_space=pl.ANY))
            arguments.append(value)
    return pl.pallas_call(
        functools.partial(middle_kernel, plan),
        out_shape=[
            jax.ShapeDtypeStruct((groups * sides, total, count, slots, channels), BF)
            for total, _, count in plan
        ],
        grid_spec=pltpu.PrefetchScalarGridSpec(
            num_scalar_prefetch=1,
            grid=(STEP,),
            in_specs=specs,
            out_specs=[
                pl.BlockSpec(
                    (groups * sides, 1, count, slots, channels),
                    functools.partial(lambda slot, m, at: (0, slot, 0, 0, 0), slot),
                )
                for _, slot, count in plan
            ],
            scratch_shapes=[
                pltpu.VMEM((2 * channels, 2 * channels), BF),
                pltpu.VMEM((channels // LANES, nlat * slots, LANES), F32),
                pltpu.VMEM((channels // LANES, nlat * slots, LANES), F32),
            ],
        ),
        input_output_aliases=aliases,
        compiler_params=params(60),
        cost_estimate=cost(
            2 * STEP * (2 * L * nlat * 2 * channels + L * 4 * channels * channels),
            STEP * (L * nlat * 4 + nlat * channels * 8) + mix.size * 2,
        ),
    )(offset, *arguments)


def local_rows(base_ref, ratio_ref, weight_ref, prev_ref, here_ref, after_ref, edge_ref, tail_ref, out_ref, held):
    t = pl.program_id(0)
    cycle = base_ref[0] + t
    cycles = base_ref[1]
    _, nlon, width = out_ref.shape
    near = weight_ref.shape[0] // 2
    reach = weight_ref.shape[1] // 2
    pad = 8
    block = max(size for size in range(8, 73, 8) if nlon % size == 0)
    wide = block + 2 * pad

    def fill(slot, row):
        held[slot, pl.ds(pad, nlon), :] = row
        held[slot, pl.ds(0, pad), :] = row[nlon - pad :]
        held[slot, pl.ds(pad + nlon, pad), :] = row[:pad]

    @pl.when(t == 0)
    def _():
        fill(0, here_ref[0].astype(F32))

        @pl.when(cycle == 0)
        def _():
            fill(2, edge_ref[0].astype(F32))

        @pl.when(cycle > 0)
        def _():
            fill(2, prev_ref[0].astype(F32))

    after = lax.rem(t + 1, 3)

    @pl.when(cycle < cycles - 1)
    def _():
        fill(after, after_ref[0].astype(F32))

    @pl.when(cycle == cycles - 1)
    def _():
        fill(after, tail_ref[0].astype(F32))

    slots = [lax.rem(t + 2 + a, 3) for a in range(2 * near + 1)]
    for low in range(0, width, LANES):
        lanes = slice(low, low + LANES)
        weights = [
            [weight_ref[a, b : b + 1, lanes] * ratio_ref[cycle, a] for b in range(2 * reach + 1)]
            for a in range(2 * near + 1)
        ]

        def body(at, carry):
            start = pl.multiple_of(at * block, 8)
            rows = [held[slot, pl.ds(start, wide), lanes] for slot in slots]
            total = rows[near][pad : pad + block]
            for b in range(2 * reach + 1):
                value = rows[0] * weights[0][b]
                for a in range(1, 2 * near + 1):
                    value = value + rows[a] * weights[a][b]
                if b != reach:
                    value = pltpu.roll(value, (wide + reach - b) % wide, 0)
                total = total + value[pad : pad + block]
            out_ref[0, pl.ds(start, block), lanes] = total.astype(BF)
            return carry

        lax.fori_loop(0, nlon // block, body, 0)


def local_part(grid, before, after, ratio, weight, base, span):
    cycles, nlon, width = grid.shape
    row = (1, nlon, width)
    edge = lambda t, *_: (0, 0, 0)
    return pl.pallas_call(
        local_rows,
        out_shape=jax.ShapeDtypeStruct((span, nlon, width), BF),
        grid_spec=pltpu.PrefetchScalarGridSpec(
            num_scalar_prefetch=2,
            grid=(span,),
            in_specs=[
                pl.BlockSpec(weight.shape, edge),
                pl.BlockSpec(row, lambda t, at, _: (jnp.maximum(at[0] - 1, 0), 0, 0)),
                pl.BlockSpec(row, lambda t, at, _: (at[0] + t, 0, 0)),
                pl.BlockSpec(row, lambda t, at, _: (jnp.minimum(at[0] + t + 1, cycles - 1), 0, 0)),
                pl.BlockSpec(row, edge),
                pl.BlockSpec(row, edge),
            ],
            out_specs=pl.BlockSpec(row, lambda t, *_: (t, 0, 0)),
            scratch_shapes=[pltpu.VMEM((3, nlon + 16, width), F32)],
        ),
        compiler_params=params(60),
        cost_estimate=cost(span * nlon * width * 400, span * nlon * width * 6),
    )(jnp.stack([base, cycles]).astype(jnp.int32), ratio, weight, grid, grid, grid, before, after)


def exchanged(value, counts):
    got = []
    start = 0
    for count in counts:
        piece = lax.slice_in_dim(value, start, start + count, axis=0)
        got.append(lax.ppermute(piece, "chan", SWAP))
        start += count
    return got


def tail_kernel(pieces, place_ref, own_ref, got_ref, gain_ref, up_ref, down_ref, *rest):
    mine_ref, theirs_ref = rest[-2:]
    first = place_ref[1] == 0
    channels = up_ref.shape[0]
    width = own_ref.shape[2]
    spectral = 0.0
    for back_ref, table_ref in zip(rest[:pieces], rest[pieces : 2 * pieces]):
        back = back_ref[:, :, 0].astype(F32).reshape(table_ref.shape[1], channels).astype(BF)
        spectral += jnp.dot(table_ref[...], back, preferred_element_type=F32)
    own = own_ref[0].astype(F32)
    got = got_ref[0].astype(F32)
    low = jnp.where(first, own, got)
    high = jnp.where(first, got, own)
    local = jnp.concatenate([low, high], axis=1)
    rows = (spectral + local).astype(BF).astype(F32)
    center = jnp.mean(rows, axis=-1, keepdims=True)
    moved = rows - center
    spread = jnp.mean(moved * moved, axis=-1, keepdims=True)
    normed = (moved * lax.rsqrt(spread + 1e-05) * gain_ref[...]).astype(BF)
    hidden = jax.nn.gelu(jnp.dot(normed, up_ref[...], preferred_element_type=F32), approximate=True)
    output = jnp.dot(hidden.astype(BF), down_ref[...], preferred_element_type=F32) + rows
    low = output[:, :width]
    high = output[:, width:]
    mine_ref[0] = jnp.where(first, low, high).astype(BF)
    theirs_ref[0] = jnp.where(first, high, low).astype(BF)


def tail_part(backs, tables, own, got, start, low, count, ln_gain, up_weight, down_weight, place, result, cycles):
    channels = backs[0].shape[4]
    _, nlon, width = own.shape
    fixed = lambda t, at: (0, 0)
    row = (1, nlon, width)
    specs = [
        pl.BlockSpec(row, lambda t, at: (start + low + t, 0, 0)),
        pl.BlockSpec(row, lambda t, at: (low + t, 0, 0)),
        pl.BlockSpec(ln_gain.shape, fixed),
        pl.BlockSpec(up_weight.shape, fixed),
        pl.BlockSpec(down_weight.shape, fixed),
    ]
    for back in backs:
        block = back.shape[:2] + (1,) + back.shape[3:]
        specs.append(pl.BlockSpec(block, lambda t, at: (0, 0, low + t, 0, 0)))
    specs += [pl.BlockSpec(table.shape, fixed) for table in tables]
    arguments = [own, got, ln_gain, up_weight, down_weight, *backs, *tables]
    aliases = {}
    if result is not None:
        aliases[1 + len(arguments)] = 0
        specs.append(pl.BlockSpec(memory_space=pl.ANY))
        arguments.append(result)
    return pl.pallas_call(
        functools.partial(tail_kernel, len(backs)),
        out_shape=[
            jax.ShapeDtypeStruct((cycles, nlon, width), BF),
            jax.ShapeDtypeStruct((count, nlon, width), BF),
        ],
        grid_spec=pltpu.PrefetchScalarGridSpec(
            num_scalar_prefetch=1,
            grid=(count,),
            in_specs=specs,
            out_specs=[
                pl.BlockSpec(row, lambda t, at: (at[0] + start + low + t, 0, 0)),
                pl.BlockSpec(row, lambda t, at: (t, 0, 0)),
            ],
        ),
        input_output_aliases=aliases,
        compiler_params=params(60),
        cost_estimate=cost(
            2 * count * nlon * channels * (sum(table.shape[1] for table in tables) + 2 * channels),
            count * nlon * channels * 8,
        ),
    )(place, *arguments)


def fast(grid, basis, mix_weight, spectral_gain, conv_weight, lat_offsets, lon_offsets, ln_gain, up_weight, down_weight):
    cycles, nlon, width = grid.shape
    groups = lax.axis_size("lat")
    sides = lax.axis_size("chan")
    rank = lax.axis_index("lat")
    side = lax.axis_index("chan")
    nlat = cycles * groups
    modes = basis.shape[0]
    few = modes // sides
    parts = few // STEP
    span = cycles // sides
    third = span // 3
    counts = [third, third - 1, third - 1, span - 3 * third + 2]

    cosine, sine = angle_table(nlon)
    both = np.stack([cosine, -sine], axis=-1)
    fwd_table = both.reshape(nlon, groups * sides, few, 2).transpose(1, 2, 3, 0)
    weight_m = np.where(np.arange(MMAX) == 0, 1.0, 2.0)[None, :, None]
    inv_table = (both * weight_m).reshape(nlon, groups * sides, parts, STEP * 2)

    def inverse(low, high):
        return jnp.asarray(inv_table[:, :, low:high].reshape(nlon, -1), BF)


    up = [(i, i + 1) for i in range(groups - 1)]
    down = [(j, i) for i, j in up]
    before = lax.ppermute(grid[-1:], "lat", up)
    after = lax.ppermute(grid[:1], "lat", down)
    own_cycles = rank * cycles + jnp.arange(cycles, dtype=jnp.int32)
    moved = own_cycles[:, None] + jnp.arange(-NEAR, NEAR + 1, dtype=jnp.int32)[None, :]
    ratio = jnp.sin(cycle_angle(moved, nlat)) / jnp.sin(cycle_angle(own_cycles, nlat))[:, None]
    by_lat = lat_offsets[None, :] == jnp.arange(-NEAR, NEAR + 1, dtype=jnp.int32)[:, None]
    by_lon = lon_offsets[None, :] == jnp.arange(-REACH, REACH + 1, dtype=jnp.int32)[:, None]
    hit = (by_lat[:, None, :] & by_lon[None, :, :])[..., None]
    weight = jnp.sum(jnp.where(hit, conv_weight[None, None], 0.0), axis=2)

    other = lax.ppermute(mix_weight, "chan", SWAP)
    gathered = []
    bounds = [(0, few - STEP), (few - STEP, few)]
    for part, (low, high) in enumerate(bounds):
        table = jnp.asarray(fwd_table[:, low:high].reshape(-1, nlon), BF)
        spec = forward_part(grid, table, groups * sides)
        if part == 0:
            spec, before, after = lax.optimization_barrier((spec, before, after))
            asked = local_part(grid, before, after, ratio, weight, (1 - side) * span, span)
            got = exchanged(asked, counts)
        else:
            own = local_part(grid, before, after, ratio, weight, side * span, span)
            spec, own, other, got[0], got[1] = lax.optimization_barrier(
                (spec, own, other, got[0], got[1])
            )
        spec = lax.all_to_all(spec, ("lat", "chan"), 0, 0, tiled=True)
        gathered.append(spec.reshape((groups, sides) + spec.shape[1:]))

    theta = cycle_angle(jnp.arange(nlat, dtype=jnp.int32), nlat)
    quad = (math.pi / nlat * jnp.sin(theta))[None, :]
    gain = spectral_gain[:, None]

    filled = [None] * (len(counts) - 1)
    heads = []
    for part in range(parts):
        offset = jnp.stack([side * few + part * STEP, side]).astype(jnp.int32)
        late = part == parts - 1
        plan = [(1, 0, counts[0]) if late else (parts - 1, part, counts[0])]
        plan += [(parts, part, count) for count in counts[1:]]
        head = heads[-1] if heads and not late else None
        ready = middle_part(
            gathered[int(late)], 0 if late else part, basis, quad, mix_weight, other, gain,
            offset, plan, [head] + filled,
        )
        heads.append(ready[0])
        filled = list(ready[1:])

    def shuffled(value):
        return lax.all_to_all(value, ("lat", "chan"), 0, 0, tiled=True)

    place = jnp.stack([side * span, side]).astype(jnp.int32)

    sent = []

    def finished(at, backs, tables, result):
        pieces = [counts[at]]
        low = 0
        needed = []
        for count in pieces:
            result, theirs = tail_part(
                backs, tables, own, got[at], sum(counts[:at]), low, count, ln_gain[None, :],
                up_weight, down_weight, place, result, cycles,
            )
            sent.append(lax.ppermute(theirs, "chan", SWAP))
            needed.append(theirs if low else sent[-1])
            low += count
        return (result, needed)

    begin, end = heads[-2:]
    begin, _, got[2] = lax.optimization_barrier((begin, gathered[1], got[2]))
    begin = shuffled(begin)
    end, begin, got[3] = lax.optimization_barrier((end, begin, got[3]))
    end = shuffled(end)
    backs = [[begin, end]]
    tables = [[inverse(0, parts - 1), inverse(parts - 1, parts)]] + [[inverse(0, parts)]] * 3
    last = end
    result = None
    for at, value in enumerate(filled):
        if at == 0:
            value, last = lax.optimization_barrier((value, last))
            backs[0][1] = last
        else:
            value, last = lax.optimization_barrier((value, last))
            backs[-1] = [last]
        if at > 0:
            value, *_ = lax.optimization_barrier((value, *tied))
        last = shuffled(value)
        result, tied = finished(at, backs[-1], tables[at], result)
        backs.append([last])
    result, _ = finished(len(filled), [last], tables[-1], result)
    start = 0
    for value in sent:
        count = value.shape[0]
        result = lax.dynamic_update_slice_in_dim(result, value, (1 - side) * span + start, 0)
        start += count
    return result


def padded_2(value, sides, width):
    for axis, dim in sides:
        size, length = (lax.axis_size(axis), value.shape[dim])
        up = [(i, (i + 1) % size) for i in range(size - 1)]
        down = [(j, i) for i, j in up]
        last = lax.slice_in_dim(value, length - width, length, axis=dim)
        first = lax.slice_in_dim(value, 0, width, axis=dim)
        before = lax.ppermute(last, axis, up)
        after = lax.ppermute(first, axis, down)
        value = jnp.concatenate([before, value, after], axis=dim)
    return value


def complex_mix(real_in, imag_in, real_w, imag_w):
    real_out = jnp.dot(real_in, real_w, preferred_element_type=jnp.float32) - jnp.dot(
        imag_in, imag_w, preferred_element_type=jnp.float32
    )
    imag_out = jnp.dot(real_in, imag_w, preferred_element_type=jnp.float32) + jnp.dot(
        imag_in, real_w, preferred_element_type=jnp.float32
    )
    return (real_out, imag_out)


def plain(
    grid,
    basis,
    mix_weight,
    spectral_gain,
    conv_weight,
    lat_offsets,
    lon_offsets,
    ln_gain,
    up_weight,
    down_weight,
):
    cycles, nlon, width = grid.shape
    groups = lax.axis_size("lat")
    rank = lax.axis_index("lat")
    nlat = cycles * groups
    modes = basis.shape[0]
    points = jnp.arange(nlon, dtype=jnp.int32)
    all_orders = jnp.arange(MMAX, dtype=jnp.int32)
    phase = points[:, None] * all_orders[None, :] % nlon
    angle = 2.0 * math.pi * phase.astype(jnp.float32) / nlon
    fwd_table = (
        jnp.stack([jnp.cos(angle), -jnp.sin(angle)], axis=-1)
        .reshape(nlon, 2 * MMAX)
        .astype(jnp.bfloat16)
    )
    weight_m = jnp.where(all_orders == 0, 1.0, 2.0).astype(jnp.float32)[None, :]
    inv_table = (
        jnp.stack([weight_m * jnp.cos(angle), -weight_m * jnp.sin(angle)], axis=-1)
        .reshape(nlon, 2 * MMAX)
        .T.astype(jnp.bfloat16)
    )
    spec = jnp.einsum("tpc,pk->tkc", grid, fwd_table, preferred_element_type=jnp.float32) * (
        1.0 / nlon
    )
    spec = spec.astype(jnp.bfloat16).reshape(cycles, groups, modes, 2, width)
    gathered = lax.all_to_all(spec, "lat", split_axis=1, concat_axis=0, tiled=True).reshape(
        nlat, modes, 2 * width
    )
    theta = cycle_angle(jnp.arange(nlat, dtype=jnp.int32), nlat)
    quad = math.pi / nlat * jnp.sin(theta)
    fwd_leg = (basis * quad[None, None, :]).astype(jnp.bfloat16)
    inv_leg = basis.astype(jnp.bfloat16)
    coeff = jnp.einsum(
        "jlt,tjk->jlk", fwd_leg, gathered, preferred_element_type=jnp.float32
    ).astype(jnp.bfloat16)
    coeff = coeff.reshape(modes, L, 2, width)
    piece = lax.all_gather(coeff, "chan", axis=3, tiled=True)
    count = piece.shape[3]
    real_w = mix_weight[0]
    imag_w = mix_weight[1]
    real_out, imag_out = complex_mix(
        piece[:, :, 0, :].reshape(-1, count), piece[:, :, 1, :].reshape(-1, count), real_w, imag_w
    )
    summed_modes = jnp.concatenate([real_out, imag_out], axis=1)
    mixed = (summed_modes.reshape(modes, L, 2 * width) * spectral_gain[None, :, None]).astype(
        jnp.bfloat16
    )
    back = jnp.einsum("jlt,jlk->tjk", inv_leg, mixed, preferred_element_type=jnp.float32).astype(
        jnp.bfloat16
    )
    back = lax.all_to_all(
        back.reshape(nlat, 1, modes, 2, width), "lat", split_axis=0, concat_axis=1, tiled=True
    )
    back = back.reshape(cycles, 2 * MMAX, width)
    spectral = jnp.einsum("tkc,kp->tpc", back, inv_table, preferred_element_type=jnp.float32)
    padded = padded_2(grid, (("lat", 0),), 1)
    own_cycles = rank * cycles + jnp.arange(cycles, dtype=jnp.int32)
    here = jnp.sin(cycle_angle(own_cycles, nlat))
    local = jnp.zeros((cycles, nlon, width), jnp.float32)
    for tap in range(conv_weight.shape[0]):
        shift = lat_offsets[tap]
        source = lax.dynamic_slice_in_dim(padded, 1 + shift, cycles, 0)
        source = jnp.roll(source, -lon_offsets[tap], axis=1)
        ratio = (jnp.sin(cycle_angle(own_cycles + shift, nlat)) / here)[:, None, None]
        local = local + conv_weight[tap][None, None, :] * ratio * source.astype(jnp.float32)
    summed = (spectral + local + grid.astype(jnp.float32)).astype(jnp.bfloat16)
    block = lax.all_to_all(summed, "chan", split_axis=1, concat_axis=2, tiled=True)
    count, span, channels = block.shape
    rows = block.reshape(-1, channels).astype(jnp.float32)
    center = jnp.mean(rows, axis=-1, keepdims=True)
    spread = jnp.mean((rows - center) ** 2, axis=-1, keepdims=True)
    normed = ((rows - center) / jnp.sqrt(spread + 1e-05) * ln_gain).astype(jnp.bfloat16)
    hidden = jax.nn.gelu(
        jnp.dot(normed, up_weight, preferred_element_type=jnp.float32), approximate=True
    ).astype(jnp.bfloat16)
    output = (jnp.dot(hidden, down_weight, preferred_element_type=jnp.float32) + rows).astype(
        jnp.bfloat16
    )
    return lax.all_to_all(
        output.reshape(count, span, channels), "chan", split_axis=2, concat_axis=1, tiled=True
    )


def on_device(*arguments):
    grid, basis = arguments[:2]
    cycles, nlon, width = grid.shape
    sides = lax.axis_size("chan")
    fits = (
        sides == 2
        and cycles % 8 == 0
        and cycles % sides == 0
        and cycles // sides >= 6
        and basis.shape[0] // (sides * STEP) >= 2
        and basis.shape[0] % (sides * STEP) == 0
        and nlon % 8 == 0
        and width % 128 == 0
    )
    return (fast if fits else plain)(*arguments)


def solution(mesh):
    return jax.shard_map(
        on_device,
        mesh=mesh,
        in_specs=(
            P("lat", None, "chan"),
            P("lat", None, None),
            P(None, None, "chan"),
            P(),
            P(None, "chan"),
            P(),
            P(),
            P(),
            P(),
            P(),
        ),
        out_specs=P("lat", None, "chan"),
        check_vma=False,
    )
```

```python
import functools
import math

import jax
import jax.numpy as jnp
import numpy as np
from jax import lax
from jax.experimental import pallas as pl
from jax.experimental.pallas import tpu as pltpu
from jax.sharding import PartitionSpec as P

MMAX = 384
L = 384
STEP = 4
LANES = 128
NEAR = 1
REACH = 3
BF = jnp.bfloat16
F32 = jnp.float32
SWAP = [(0, 1), (1, 0)]


def cycle_angle(rows, nlat):
    return math.pi * (rows.astype(F32) + 0.5) / nlat


def params(mib):
    return pltpu.CompilerParams(vmem_limit_bytes=mib * 1024 * 1024)


def cost(flops, nbytes):
    return pl.CostEstimate(flops=int(flops), bytes_accessed=int(nbytes), transcendentals=0)


def angle_table(nlon):
    phase = np.arange(nlon)[:, None] * np.arange(MMAX)[None, :] % nlon
    angle = (2.0 * math.pi * phase / nlon).astype(np.float32).astype(np.float64)
    return np.cos(angle), np.sin(angle)


def forward_kernel(scale, table_ref, grid_ref, out_ref):
    places, blocks, few, slots, width = out_ref.shape
    for t in range(few):
        value = jnp.dot(table_ref[...], grid_ref[t], preferred_element_type=F32) * scale
        out_ref[:, :, t] = value.reshape(places, blocks, slots, width).astype(BF)


def forward_part(grid, table, places):
    cycles, nlon, width = grid.shape
    rows = table.shape[0]
    slots = 2 * STEP
    blocks = rows // places // slots
    few = 8
    return pl.pallas_call(
        functools.partial(forward_kernel, 1.0 / nlon),
        out_shape=jax.ShapeDtypeStruct((places, blocks, cycles, slots, width), BF),
        grid=(cycles // few,),
        in_specs=[
            pl.BlockSpec(table.shape, lambda t: (0, 0)),
            pl.BlockSpec((few, nlon, width), lambda t: (t, 0, 0)),
        ],
        out_specs=pl.BlockSpec((places, blocks, few, slots, width), lambda t: (0, 0, t, 0, 0)),
        compiler_params=params(60),
        cost_estimate=cost(2 * rows * nlon * cycles * width, grid.size * 2),
    )(table, grid)


def middle_kernel(plan, at_ref, spec_ref, basis_ref, quad_ref, own_ref, other_ref, gain_ref, *rest):
    outs, mix_ref, held, loose = (rest[-len(plan) - 3 : -3], *rest[-3:])
    mode = pl.program_id(0)
    groups, sides, _, cycles, slots, width = spec_ref.shape
    lanes = width // LANES

    @pl.when(mode == 0)
    def _():
        for at in range(sides * lanes):
            low = at % lanes * LANES
            piece = spec_ref[:, at // lanes, 0, :, :, low : low + LANES].astype(F32)
            loose[at] = piece.reshape(groups * cycles * slots, LANES)
        first = at_ref[1] == 0
        channels = sides * width
        own = own_ref[...].astype(F32)
        other = other_ref[...].astype(F32)
        low = jnp.where(first, own, other)
        high = jnp.where(first, other, own)
        whole = jnp.concatenate([low, high], axis=2).astype(BF)
        for at in range(sides):
            block = whole[:, at * width : (at + 1) * width]
            real = pl.ds(2 * at * width, width)
            imag = pl.ds((2 * at + 1) * width, width)
            mix_ref[real, 0:channels] = block[0]
            mix_ref[real, channels : 2 * channels] = block[1]
            mix_ref[imag, 0:channels] = -block[1]
            mix_ref[imag, channels : 2 * channels] = block[0]

    nlat = groups * cycles
    table = basis_ref[0]
    forward = (table * quad_ref[...]).astype(BF)
    pieces = []
    for side in range(sides):
        for part in range(2):
            for at in range(side * lanes, (side + 1) * lanes):
                rows = pl.ds(2 * mode + part, nlat, stride=slots)
                pieces.append(loose[at, rows, :].astype(BF))
    spec = jnp.concatenate(pieces, axis=1)
    coeff = jnp.dot(forward, spec, preferred_element_type=F32).astype(BF)
    mixed = jnp.dot(coeff, mix_ref[...], preferred_element_type=F32) * gain_ref[...]
    inverse = table.T.astype(BF)
    back = jnp.dot(inverse, mixed.astype(BF), preferred_element_type=F32)
    half = back.shape[1] // 2
    for part in range(2):
        for where in range(STEP):

            @pl.when(mode == where)
            def _():
                row = 2 * where + part
                for at in range(half // LANES):
                    low = part * half + at * LANES
                    held[at, pl.ds(row, nlat, stride=slots), :] = back[:, low : low + LANES]

    @pl.when(mode == STEP - 1)
    def _():
        for at in range(half // LANES):
            whole = held[at].reshape(groups * sides, nlat // (groups * sides), slots, LANES)
            start = 0
            for out, (_, _, count) in zip(outs, plan):
                part = whole[:, start : start + count].astype(BF)
                out[:, 0, :, :, at * LANES : (at + 1) * LANES] = part
                start += count


def middle_part(spec, skip, basis, quad, mix, other, gain, offset, plan, filled):
    groups, sides, _, cycles, slots, width = spec.shape
    nlat = groups * cycles
    channels = sides * width
    fixed = lambda m, at: (0, 0)
    specs = [
        pl.BlockSpec((groups, sides, 1, cycles, slots, width), lambda m, at: (0, 0, skip, 0, 0, 0)),
        pl.BlockSpec((1, L, nlat), lambda m, at: (at[0] + m, 0, 0)),
        pl.BlockSpec((1, nlat), fixed),
        pl.BlockSpec(mix.shape, lambda m, at: (0, 0, 0)),
        pl.BlockSpec(mix.shape, lambda m, at: (0, 0, 0)),
        pl.BlockSpec((L, 1), fixed),
    ]
    arguments = [spec, basis, quad, mix, other, gain]
    aliases = {}
    for at, value in enumerate(filled):
        if value is not None:
            aliases[1 + len(arguments)] = at
            specs.append(pl.BlockSpec(memory_space=pl.ANY))
            arguments.append(value)
    return pl.pallas_call(
        functools.partial(middle_kernel, plan),
        out_shape=[
            jax.ShapeDtypeStruct((groups * sides, total, count, slots, channels), BF)
            for total, _, count in plan
        ],
        grid_spec=pltpu.PrefetchScalarGridSpec(
            num_scalar_prefetch=1,
            grid=(STEP,),
            in_specs=specs,
            out_specs=[
                pl.BlockSpec(
                    (groups * sides, 1, count, slots, channels),
                    functools.partial(lambda slot, m, at: (0, slot, 0, 0, 0), slot),
                )
                for _, slot, count in plan
            ],
            scratch_shapes=[
                pltpu.VMEM((2 * channels, 2 * channels), BF),
                pltpu.VMEM((channels // LANES, nlat * slots, LANES), F32),
                pltpu.VMEM((channels // LANES, nlat * slots, LANES), F32),
            ],
        ),
        input_output_aliases=aliases,
        compiler_params=params(60),
        cost_estimate=cost(
            2 * STEP * (2 * L * nlat * 2 * channels + L * 4 * channels * channels),
            STEP * (L * nlat * 4 + nlat * channels * 8) + mix.size * 2,
        ),
    )(offset, *arguments)


def local_rows(base_ref, ratio_ref, weight_ref, prev_ref, here_ref, after_ref, edge_ref, tail_ref, out_ref, held):
    t = pl.program_id(0)
    cycle = base_ref[0] + t
    cycles = base_ref[1]
    _, nlon, width = out_ref.shape
    near = weight_ref.shape[0] // 2
    reach = weight_ref.shape[1] // 2
    pad = 8
    block = max(size for size in range(8, 73, 8) if nlon % size == 0)
    wide = block + 2 * pad

    def fill(slot, row):
        held[slot, pl.ds(pad, nlon), :] = row
        held[slot, pl.ds(0, pad), :] = row[nlon - pad :]
        held[slot, pl.ds(pad + nlon, pad), :] = row[:pad]

    @pl.when(t == 0)
    def _():
        fill(0, here_ref[0].astype(F32))

        @pl.when(cycle == 0)
        def _():
            fill(2, edge_ref[0].astype(F32))

        @pl.when(cycle > 0)
        def _():
            fill(2, prev_ref[0].astype(F32))

    after = lax.rem(t + 1, 3)

    @pl.when(cycle < cycles - 1)
    def _():
        fill(after, after_ref[0].astype(F32))

    @pl.when(cycle == cycles - 1)
    def _():
        fill(after, tail_ref[0].astype(F32))

    slots = [lax.rem(t + 2 + a, 3) for a in range(2 * near + 1)]
    for low in range(0, width, LANES):
        lanes = slice(low, low + LANES)
        weights = [
            [weight_ref[a, b : b + 1, lanes] * ratio_ref[cycle, a] for b in range(2 * reach + 1)]
            for a in range(2 * near + 1)
        ]

        def body(at, carry):
            start = pl.multiple_of(at * block, 8)
            rows = [held[slot, pl.ds(start, wide), lanes] for slot in slots]
            total = rows[near][pad : pad + block]
            for b in range(2 * reach + 1):
                value = rows[0] * weights[0][b]
                for a in range(1, 2 * near + 1):
                    value = value + rows[a] * weights[a][b]
                if b != reach:
                    value = pltpu.roll(value, (wide + reach - b) % wide, 0)
                total = total + value[pad : pad + block]
            out_ref[0, pl.ds(start, block), lanes] = total.astype(BF)
            return carry

        lax.fori_loop(0, nlon // block, body, 0)


def local_part(grid, before, after, ratio, weight, base, span):
    cycles, nlon, width = grid.shape
    row = (1, nlon, width)
    edge = lambda t, *_: (0, 0, 0)
    return pl.pallas_call(
        local_rows,
        out_shape=jax.ShapeDtypeStruct((span, nlon, width), BF),
        grid_spec=pltpu.PrefetchScalarGridSpec(
            num_scalar_prefetch=2,
            grid=(span,),
            in_specs=[
                pl.BlockSpec(weight.shape, edge),
                pl.BlockSpec(row, lambda t, at, _: (jnp.maximum(at[0] - 1, 0), 0, 0)),
                pl.BlockSpec(row, lambda t, at, _: (at[0] + t, 0, 0)),
                pl.BlockSpec(row, lambda t, at, _: (jnp.minimum(at[0] + t + 1, cycles - 1), 0, 0)),
                pl.BlockSpec(row, edge),
                pl.BlockSpec(row, edge),
            ],
            out_specs=pl.BlockSpec(row, lambda t, *_: (t, 0, 0)),
            scratch_shapes=[pltpu.VMEM((3, nlon + 16, width), F32)],
        ),
        compiler_params=params(60),
        cost_estimate=cost(span * nlon * width * 400, span * nlon * width * 6),
    )(jnp.stack([base, cycles]).astype(jnp.int32), ratio, weight, grid, grid, grid, before, after)


def exchanged(value, counts):
    got = []
    start = 0
    for count in counts:
        piece = lax.slice_in_dim(value, start, start + count, axis=0)
        got.append(lax.ppermute(piece, "chan", SWAP))
        start += count
    return got


def tail_kernel(pieces, place_ref, own_ref, got_ref, gain_ref, up_ref, down_ref, *rest):
    mine_ref, theirs_ref = rest[-2:]
    first = place_ref[1] == 0
    channels = up_ref.shape[0]
    width = own_ref.shape[2]
    spectral = 0.0
    for back_ref, table_ref in zip(rest[:pieces], rest[pieces : 2 * pieces]):
        back = back_ref[:, :, 0].astype(F32).reshape(table_ref.shape[1], channels).astype(BF)
        spectral += jnp.dot(table_ref[...], back, preferred_element_type=F32)
    own = own_ref[0].astype(F32)
    got = got_ref[0].astype(F32)
    low = jnp.where(first, own, got)
    high = jnp.where(first, got, own)
    local = jnp.concatenate([low, high], axis=1)
    rows = (spectral + local).astype(BF).astype(F32)
    center = jnp.mean(rows, axis=-1, keepdims=True)
    moved = rows - center
    spread = jnp.mean(moved * moved, axis=-1, keepdims=True)
    normed = (moved * lax.rsqrt(spread + 1e-05) * gain_ref[...]).astype(BF)
    hidden = jax.nn.gelu(jnp.dot(normed, up_ref[...], preferred_element_type=F32), approximate=True)
    output = jnp.dot(hidden.astype(BF), down_ref[...], preferred_element_type=F32) + rows
    low = output[:, :width]
    high = output[:, width:]
    mine_ref[0] = jnp.where(first, low, high).astype(BF)
    theirs_ref[0] = jnp.where(first, high, low).astype(BF)


def tail_part(backs, tables, own, got, start, low, count, ln_gain, up_weight, down_weight, place, result, cycles):
    channels = backs[0].shape[4]
    _, nlon, width = own.shape
    fixed = lambda t, at: (0, 0)
    row = (1, nlon, width)
    specs = [
        pl.BlockSpec(row, lambda t, at: (start + low + t, 0, 0)),
        pl.BlockSpec(row, lambda t, at: (low + t, 0, 0)),
        pl.BlockSpec(ln_gain.shape, fixed),
        pl.BlockSpec(up_weight.shape, fixed),
        pl.BlockSpec(down_weight.shape, fixed),
    ]
    for back in backs:
        block = back.shape[:2] + (1,) + back.shape[3:]
        specs.append(pl.BlockSpec(block, lambda t, at: (0, 0, low + t, 0, 0)))
    specs += [pl.BlockSpec(table.shape, fixed) for table in tables]
    arguments = [own, got, ln_gain, up_weight, down_weight, *backs, *tables]
    aliases = {}
    if result is not None:
        aliases[1 + len(arguments)] = 0
        specs.append(pl.BlockSpec(memory_space=pl.ANY))
        arguments.append(result)
    return pl.pallas_call(
        functools.partial(tail_kernel, len(backs)),
        out_shape=[
            jax.ShapeDtypeStruct((cycles, nlon, width), BF),
            jax.ShapeDtypeStruct((count, nlon, width), BF),
        ],
        grid_spec=pltpu.PrefetchScalarGridSpec(
            num_scalar_prefetch=1,
            grid=(count,),
            in_specs=specs,
            out_specs=[
                pl.BlockSpec(row, lambda t, at: (at[0] + start + low + t, 0, 0)),
                pl.BlockSpec(row, lambda t, at: (t, 0, 0)),
            ],
        ),
        input_output_aliases=aliases,
        compiler_params=params(60),
        cost_estimate=cost(
            2 * count * nlon * channels * (sum(table.shape[1] for table in tables) + 2 * channels),
            count * nlon * channels * 8,
        ),
    )(place, *arguments)


def fast(grid, basis, mix_weight, spectral_gain, conv_weight, lat_offsets, lon_offsets, ln_gain, up_weight, down_weight):
    cycles, nlon, width = grid.shape
    groups = lax.axis_size("lat")
    sides = lax.axis_size("chan")
    rank = lax.axis_index("lat")
    side = lax.axis_index("chan")
    nlat = cycles * groups
    modes = basis.shape[0]
    few = modes // sides
    parts = few // STEP
    span = cycles // sides
    third = span // 3
    counts = [third, third - 1, third - 1, span - 3 * third + 2]

    cosine, sine = angle_table(nlon)
    both = np.stack([cosine, -sine], axis=-1)
    fwd_table = both.reshape(nlon, groups * sides, few, 2).transpose(1, 2, 3, 0)
    weight_m = np.where(np.arange(MMAX) == 0, 1.0, 2.0)[None, :, None]
    inv_table = (both * weight_m).reshape(nlon, groups * sides, parts, STEP * 2)

    def inverse(low, high):
        return jnp.asarray(inv_table[:, :, low:high].reshape(nlon, -1), BF)


    up = [(i, i + 1) for i in range(groups - 1)]
    down = [(j, i) for i, j in up]
    before = lax.ppermute(grid[-1:], "lat", up)
    after = lax.ppermute(grid[:1], "lat", down)
    own_cycles = rank * cycles + jnp.arange(cycles, dtype=jnp.int32)
    moved = own_cycles[:, None] + jnp.arange(-NEAR, NEAR + 1, dtype=jnp.int32)[None, :]
    ratio = jnp.sin(cycle_angle(moved, nlat)) / jnp.sin(cycle_angle(own_cycles, nlat))[:, None]
    by_lat = lat_offsets[None, :] == jnp.arange(-NEAR, NEAR + 1, dtype=jnp.int32)[:, None]
    by_lon = lon_offsets[None, :] == jnp.arange(-REACH, REACH + 1, dtype=jnp.int32)[:, None]
    hit = (by_lat[:, None, :] & by_lon[None, :, :])[..., None]
    weight = jnp.sum(jnp.where(hit, conv_weight[None, None], 0.0), axis=2)

    other = lax.ppermute(mix_weight, "chan", SWAP)
    gathered = []
    bounds = [(0, few - STEP), (few - STEP, few)]
    for part, (low, high) in enumerate(bounds):
        table = jnp.asarray(fwd_table[:, low:high].reshape(-1, nlon), BF)
        spec = forward_part(grid, table, groups * sides)
        if part == 0:
            spec, before, after = lax.optimization_barrier((spec, before, after))
            asked = local_part(grid, before, after, ratio, weight, (1 - side) * span, span)
            got = exchanged(asked, counts)
        else:
            own = local_part(grid, before, after, ratio, weight, side * span, span)
            spec, own, other, got[0], got[1] = lax.optimization_barrier(
                (spec, own, other, got[0], got[1])
            )
        spec = lax.all_to_all(spec, ("lat", "chan"), 0, 0, tiled=True)
        gathered.append(spec.reshape((groups, sides) + spec.shape[1:]))

    theta = cycle_angle(jnp.arange(nlat, dtype=jnp.int32), nlat)
    quad = (math.pi / nlat * jnp.sin(theta))[None, :]
    gain = spectral_gain[:, None]

    filled = [None] * (len(counts) - 1)
    heads = []
    for part in range(parts):
        offset = jnp.stack([side * few + part * STEP, side]).astype(jnp.int32)
        late = part == parts - 1
        plan = [(1, 0, counts[0]) if late else (parts - 1, part, counts[0])]
        plan += [(parts, part, count) for count in counts[1:]]
        head = heads[-1] if heads and not late else None
        ready = middle_part(
            gathered[int(late)], 0 if late else part, basis, quad, mix_weight, other, gain,
            offset, plan, [head] + filled,
        )
        heads.append(ready[0])
        filled = list(ready[1:])

    def shuffled(value):
        return lax.all_to_all(value, ("lat", "chan"), 0, 0, tiled=True)

    place = jnp.stack([side * span, side]).astype(jnp.int32)

    sent = []

    def finished(at, backs, tables, result):
        pieces = [counts[at] - 1, 1] if at == 0 and counts[at] > 1 else [counts[at]]
        low = 0
        needed = sent[1:2] if at == 1 else []
        for count in pieces:
            result, theirs = tail_part(
                backs, tables, own, got[at], sum(counts[:at]), low, count, ln_gain[None, :],
                up_weight, down_weight, place, result, cycles,
            )
            sent.append(lax.ppermute(theirs, "chan", SWAP))
            needed.append(theirs if low else sent[-1])
            low += count
        return (result, needed)

    begin, end = heads[-2:]
    begin, _, got[2] = lax.optimization_barrier((begin, gathered[1], got[2]))
    begin = shuffled(begin)
    end, begin, got[3] = lax.optimization_barrier((end, begin, got[3]))
    end = shuffled(end)
    backs = [[begin, end]]
    tables = [[inverse(0, parts - 1), inverse(parts - 1, parts)]] + [[inverse(0, parts)]] * 3
    last = end
    result = None
    for at, value in enumerate(filled):
        if at == 0:
            value, last = lax.optimization_barrier((value, last))
            backs[0][1] = last
        else:
            value, last = lax.optimization_barrier((value, last))
            backs[-1] = [last]
        if at > 0:
            value, *_ = lax.optimization_barrier((value, *tied))
        last = shuffled(value)
        result, tied = finished(at, backs[-1], tables[at], result)
        backs.append([last])
    result, _ = finished(len(filled), [last], tables[-1], result)
    start = 0
    for value in sent:
        count = value.shape[0]
        result = lax.dynamic_update_slice_in_dim(result, value, (1 - side) * span + start, 0)
        start += count
    return result


def padded_2(value, sides, width):
    for axis, dim in sides:
        size, length = (lax.axis_size(axis), value.shape[dim])
        up = [(i, (i + 1) % size) for i in range(size - 1)]
        down = [(j, i) for i, j in up]
        last = lax.slice_in_dim(value, length - width, length, axis=dim)
        first = lax.slice_in_dim(value, 0, width, axis=dim)
        before = lax.ppermute(last, axis, up)
        after = lax.ppermute(first, axis, down)
        value = jnp.concatenate([before, value, after], axis=dim)
    return value


def complex_mix(real_in, imag_in, real_w, imag_w):
    real_out = jnp.dot(real_in, real_w, preferred_element_type=jnp.float32) - jnp.dot(
        imag_in, imag_w, preferred_element_type=jnp.float32
    )
    imag_out = jnp.dot(real_in, imag_w, preferred_element_type=jnp.float32) + jnp.dot(
        imag_in, real_w, preferred_element_type=jnp.float32
    )
    return (real_out, imag_out)


def plain(
    grid,
    basis,
    mix_weight,
    spectral_gain,
    conv_weight,
    lat_offsets,
    lon_offsets,
    ln_gain,
    up_weight,
    down_weight,
):
    cycles, nlon, width = grid.shape
    groups = lax.axis_size("lat")
    rank = lax.axis_index("lat")
    nlat = cycles * groups
    modes = basis.shape[0]
    points = jnp.arange(nlon, dtype=jnp.int32)
    all_orders = jnp.arange(MMAX, dtype=jnp.int32)
    phase = points[:, None] * all_orders[None, :] % nlon
    angle = 2.0 * math.pi * phase.astype(jnp.float32) / nlon
    fwd_table = (
        jnp.stack([jnp.cos(angle), -jnp.sin(angle)], axis=-1)
        .reshape(nlon, 2 * MMAX)
        .astype(jnp.bfloat16)
    )
    weight_m = jnp.where(all_orders == 0, 1.0, 2.0).astype(jnp.float32)[None, :]
    inv_table = (
        jnp.stack([weight_m * jnp.cos(angle), -weight_m * jnp.sin(angle)], axis=-1)
        .reshape(nlon, 2 * MMAX)
        .T.astype(jnp.bfloat16)
    )
    spec = jnp.einsum("tpc,pk->tkc", grid, fwd_table, preferred_element_type=jnp.float32) * (
        1.0 / nlon
    )
    spec = spec.astype(jnp.bfloat16).reshape(cycles, groups, modes, 2, width)
    gathered = lax.all_to_all(spec, "lat", split_axis=1, concat_axis=0, tiled=True).reshape(
        nlat, modes, 2 * width
    )
    theta = cycle_angle(jnp.arange(nlat, dtype=jnp.int32), nlat)
    quad = math.pi / nlat * jnp.sin(theta)
    fwd_leg = (basis * quad[None, None, :]).astype(jnp.bfloat16)
    inv_leg = basis.astype(jnp.bfloat16)
    coeff = jnp.einsum(
        "jlt,tjk->jlk", fwd_leg, gathered, preferred_element_type=jnp.float32
    ).astype(jnp.bfloat16)
    coeff = coeff.reshape(modes, L, 2, width)
    piece = lax.all_gather(coeff, "chan", axis=3, tiled=True)
    count = piece.shape[3]
    real_w = mix_weight[0]
    imag_w = mix_weight[1]
    real_out, imag_out = complex_mix(
        piece[:, :, 0, :].reshape(-1, count), piece[:, :, 1, :].reshape(-1, count), real_w, imag_w
    )
    summed_modes = jnp.concatenate([real_out, imag_out], axis=1)
    mixed = (summed_modes.reshape(modes, L, 2 * width) * spectral_gain[None, :, None]).astype(
        jnp.bfloat16
    )
    back = jnp.einsum("jlt,jlk->tjk", inv_leg, mixed, preferred_element_type=jnp.float32).astype(
        jnp.bfloat16
    )
    back = lax.all_to_all(
        back.reshape(nlat, 1, modes, 2, width), "lat", split_axis=0, concat_axis=1, tiled=True
    )
    back = back.reshape(cycles, 2 * MMAX, width)
    spectral = jnp.einsum("tkc,kp->tpc", back, inv_table, preferred_element_type=jnp.float32)
    padded = padded_2(grid, (("lat", 0),), 1)
    own_cycles = rank * cycles + jnp.arange(cycles, dtype=jnp.int32)
    here = jnp.sin(cycle_angle(own_cycles, nlat))
    local = jnp.zeros((cycles, nlon, width), jnp.float32)
    for tap in range(conv_weight.shape[0]):
        shift = lat_offsets[tap]
        source = lax.dynamic_slice_in_dim(padded, 1 + shift, cycles, 0)
        source = jnp.roll(source, -lon_offsets[tap], axis=1)
        ratio = (jnp.sin(cycle_angle(own_cycles + shift, nlat)) / here)[:, None, None]
        local = local + conv_weight[tap][None, None, :] * ratio * source.astype(jnp.float32)
    summed = (spectral + local + grid.astype(jnp.float32)).astype(jnp.bfloat16)
    block = lax.all_to_all(summed, "chan", split_axis=1, concat_axis=2, tiled=True)
    count, span, channels = block.shape
    rows = block.reshape(-1, channels).astype(jnp.float32)
    center = jnp.mean(rows, axis=-1, keepdims=True)
    spread = jnp.mean((rows - center) ** 2, axis=-1, keepdims=True)
    normed = ((rows - center) / jnp.sqrt(spread + 1e-05) * ln_gain).astype(jnp.bfloat16)
    hidden = jax.nn.gelu(
        jnp.dot(normed, up_weight, preferred_element_type=jnp.float32), approximate=True
    ).astype(jnp.bfloat16)
    output = (jnp.dot(hidden, down_weight, preferred_element_type=jnp.float32) + rows).astype(
        jnp.bfloat16
    )
    return lax.all_to_all(
        output.reshape(count, span, channels), "chan", split_axis=2, concat_axis=1, tiled=True
    )


def on_device(*arguments):
    grid, basis = arguments[:2]
    cycles, nlon, width = grid.shape
    sides = lax.axis_size("chan")
    fits = (
        sides == 2
        and cycles % 8 == 0
        and cycles % sides == 0
        and cycles // sides >= 6
        and basis.shape[0] // (sides * STEP) >= 2
        and basis.shape[0] % (sides * STEP) == 0
        and nlon % 8 == 0
        and width % 128 == 0
    )
    return (fast if fits else plain)(*arguments)


def solution(mesh):
    return jax.shard_map(
        on_device,
        mesh=mesh,
        in_specs=(
            P("lat", None, "chan"),
            P("lat", None, None),
            P(None, None, "chan"),
            P(),
            P(None, "chan"),
            P(),
            P(),
            P(),
            P(),
            P(),
        ),
        out_specs=P("lat", None, "chan"),
        check_vma=False,
    )
```
